256 devices in a mesh: band: 16 (over x_hi, z), slab: 16 (over x_lo, y, core).
Axes of the slice: x: 4 (x_hi: 2, x_lo: 2; x = x_hi * 2 + x_lo), y: 4, z: 8, core: 2. Of those that a mesh axis runs over, the one named last changes fastest.
Arguments:
- orbitals: float32 [256, 128, 4096], P('band', 'slab'), may hold values from -0.6 to 0.6
- occupations: float32 [256], P('band'), may hold values from 0.1 to 2
- projectors: float32 [128, 13, 512], P('slab'), may hold values from -0.25 to 0.25
- shapes: float32 [128, 9, 512], P('slab'), may hold values from -6 to 6
- coupling: float32 [9, 13, 13], replicated, may hold values from -0.3 to 0.3
- sphere_offsets: int32 [128, 512], P('slab'), may hold values from 0 to 73727, as said below
- sphere_sizes: int32 [128], P('slab'), may hold values from 64 to 512
Outputs:
- density: float32 [128, 4096], P('slab', 'band')
- density_matrices: float32 [128, 13, 13], P('slab')
The draws below stay inside these ranges and needn't reach their ends.
Inputs may be any that keep to these rules, and one draw needn't show every extreme that they name: `sphere_offsets`: the plane part o // 4096 of an offset lies within 5 planes of the atom's centre plane, which lies in the slab's own planes 5 to 12; in-plane parts are arbitrary.
All inputs are finite; a program needn't handle non-finite values.
Results may differ from the reference program's by a relative error of at most 0.000062.
Values sent between devices are 32-bit elements; how exact they have to be, the bound alone decides.
No kernel may reach another device: no remote copies, remote signals or barrier semaphores. Data moves between devices by JAX's collectives and lax.ppermute only.
A program may use at most 128 MiB of HBM per device.

```python
import math
import jax
import jax.numpy as jnp
from jax import lax

PLANE = 4096
CZ = 8
ATOM_DEV = 8
SPHERE = 512
HALO = 5
NI = 13
NL = 9
NBANDS = 256
NZ = 128
ATOMS = 128


def draw_sphere_offsets(key, part):
    key_centre = jax.random.fold_in(key, 11)
    key_plane = jax.random.fold_in(key, 12)
    key_point = jax.random.fold_in(key, 13)
    which = jnp.arange(ATOMS, dtype=jnp.int32) % ATOM_DEV
    centre = jax.random.randint(key_centre, (ATOMS,), HALO, HALO + CZ, dtype=jnp.int32)
    centre = jnp.where(which == 0, HALO, centre)
    centre = jnp.where(which == 1, HALO + CZ - 1, centre)
    shift = jax.random.randint(key_plane, (ATOMS, SPHERE), -HALO, HALO + 1, dtype=jnp.int32)
    shift = shift.at[:, 0].set(-HALO).at[:, 1].set(HALO)
    point = jax.random.randint(key_point, (ATOMS, SPHERE), 0, PLANE, dtype=jnp.int32)
    point = point.at[:, 0].set(0).at[:, 1].set(PLANE - 1)
    plane = centre[:, None] + shift
    return (plane * PLANE + point).astype(jnp.int32)


def draw_sphere_sizes(key, part):
    key_size = jax.random.fold_in(key, 21)
    sizes = jax.random.randint(key_size, (ATOMS,), SPHERE // 8, SPHERE + 1, dtype=jnp.int32)
    atom_index = jnp.arange(ATOMS, dtype=jnp.int32)
    sizes = jnp.where(atom_index == 0, SPHERE, sizes)
    sizes = jnp.where(atom_index == 1, SPHERE // 8, sizes)
    return sizes.astype(jnp.int32)


def block_levels(stream_key, dims, cuts, low, high):
    level, own = 1.0, jax.random.fold_in(stream_key, 6)
    for dim, parts in cuts:
        steps = jnp.exp(jax.random.uniform(jax.random.fold_in(own, dim), (parts,), jnp.float32, low / len(cuts), high / len(cuts)))
        level = level * jnp.repeat(steps, dims[dim] // parts).reshape([-1 if axis == dim else 1 for axis in range(len(dims))])
    return level


def gaussian(stream_key, dims, width, limit, cuts=(), kind=jnp.bfloat16):
    result = width * jax.random.normal(stream_key, dims, jnp.float32)
    if cuts:
        result = result * block_levels(stream_key, dims, cuts, -0.22, 0.18)
    return jnp.clip(result, -limit, limit).astype(kind)


def setup_inputs(seed: int = 0) -> dict:
    seeds = jax.random.split(jax.random.key(seed), 8)
    orbitals = gaussian(seeds[0], (NBANDS, NZ, PLANE), 0.09, 0.6, ((0, 16), (1, 16)), jnp.float32)
    occupations = jnp.clip(jnp.exp(math.log(2.0) - 2.9957323 * jax.random.uniform(seeds[1], (NBANDS,), jnp.float32) ** block_levels(seeds[1], (NBANDS,), ((0, 16),), -0.2, 0.2)), 0.1, 2.0)
    projectors = gaussian(seeds[2], (ATOMS, NI, SPHERE), SPHERE ** -0.5, 0.25, ((0, 16),), jnp.float32)
    shapes = gaussian(seeds[3], (ATOMS, NL, SPHERE), 1.0, 6.0, ((0, 16),), jnp.float32)
    coupling = gaussian(seeds[4], (NL, NI, NI), 0.05, 0.3, (), jnp.float32)
    sphere_offsets = draw_sphere_offsets(jax.random.fold_in(seeds[7], 71), 0)
    sphere_sizes = draw_sphere_sizes(jax.random.fold_in(seeds[7], 71), 0)
    return {"orbitals": orbitals, "occupations": occupations, "projectors": projectors, "shapes": shapes, "coupling": coupling, "sphere_offsets": sphere_offsets, "sphere_sizes": sphere_sizes}


def reference(orbitals, occupations, projectors, shapes, coupling, sphere_offsets, sphere_sizes):
    hi = lax.Precision.HIGHEST
    owner = (jnp.arange(ATOMS, dtype=jnp.int32) // ATOM_DEV).astype(jnp.int32)
    plane_ext = sphere_offsets // PLANE
    inplane = sphere_offsets % PLANE
    plane_glob = (owner[:, None] * CZ + plane_ext - HALO) % NZ
    site = (plane_glob * PLANE + inplane).astype(jnp.int32)
    live = (jnp.arange(SPHERE, dtype=jnp.int32)[None, :] < sphere_sizes[:, None]).astype(jnp.float32)
    flat = orbitals.reshape(NBANDS, NZ * PLANE)
    on_sphere = flat[:, site]
    masked = projectors * live[:, None, :]
    proj = jnp.einsum("bag,aig->bai", on_sphere, masked, precision=hi)
    weighted = proj * occupations[:, None, None]
    density_matrices = jnp.einsum("bai,baj->aij", weighted, proj, precision=hi)
    charges = jnp.einsum("lij,aij->al", coupling, density_matrices, precision=hi)
    comp = jnp.einsum("al,alg->ag", charges, shapes, precision=hi) * live

    def add_band(total, pair):
        psi, occ = pair
        return total + occ * psi * psi, None

    pseudo, _ = lax.scan(add_band, jnp.zeros((NZ, PLANE), jnp.float32), (orbitals, occupations))
    density = pseudo.reshape(-1).at[site.reshape(-1)].add(comp.reshape(-1)).reshape(NZ, PLANE)
    return density, density_matrices
```

```python
import functools

import jax
import jax.numpy as jnp
from jax import lax
from jax.experimental import pallas as pl
from jax.experimental.pallas import tpu as pltpu
from jax.sharding import PartitionSpec as P

HALO = 5
PLANE = 4096
CZ = 8
ATOM_DEV = 8
SPHERE = 512
NI = 13
NL = 9
BANDS = 16
LANES = 128
STEP = 16
HIGHEST = lax.Precision.HIGHEST
F32 = jnp.float32
BF16 = jnp.bfloat16

VM = pl.BlockSpec(memory_space=pltpu.VMEM)
SM = pl.BlockSpec(memory_space=pltpu.SMEM)


def params():
    return pltpu.CompilerParams(vmem_limit_bytes=48 * 2**20)


def gather_rows(offsets, sizes, table, rows):
    for a in range(ATOM_DEV):
        steps = (sizes[a] + (STEP - 1)) // STEP

        def body(step, carry, a=a):
            first = pl.multiple_of(a * SPHERE + step * STEP, STEP)
            for u in range(STEP):
                point = offsets[first + u] & (PLANE - 1)
                rows[pl.ds(first + u, 1), :] = table[pl.ds(point, 1), :]
            return carry

        lax.fori_loop(0, steps, body, 0)


def project(pay, rows, shift):
    lane_plane = lax.broadcasted_iota(jnp.int32, (16, LANES), 1) % CZ
    sub = lax.broadcasted_iota(jnp.int32, (16, SPHERE), 0)
    parts = []
    for a in range(ATOM_DEV):
        block = pay[a]
        plane = (block[13:14, :].astype(jnp.int32) >> 12) + shift
        proj = jnp.where(sub < NI, block, 0.0)
        high = proj.astype(BF16).astype(F32)
        low = proj - high
        pieces = []
        for piece in (high, low):
            for z in range(CZ):
                pieces.append(jnp.where(plane == z, piece, 0.0))
        left = jnp.concatenate(pieces, axis=0).astype(BF16)
        gathered = rows[a * SPHERE : (a + 1) * SPHERE, :]
        g_high = gathered.astype(BF16)
        g_low = (gathered - g_high.astype(F32)).astype(BF16)
        first = jnp.dot(left, g_high, preferred_element_type=F32)
        second = jnp.dot(left[:LANES], g_low, preferred_element_type=F32)
        total = first[:LANES] + first[LANES:] + second
        acc = jnp.zeros((16, LANES), F32)
        for z in range(CZ):
            acc = acc + jnp.where(lane_plane == z, total[z * 16 : (z + 1) * 16, :], 0.0)
        parts.append(acc)
    summed = jnp.concatenate(parts, axis=0)
    band = lax.broadcasted_iota(jnp.int32, (BANDS, LANES), 0)
    lane_band = lax.broadcasted_iota(jnp.int32, (BANDS, LANES), 1) // CZ
    pick = (band == lane_band).astype(F32)
    return lax.dot_general(
        pick, summed, (((1,), (1,)), ((), ())), precision=HIGHEST, preferred_element_type=F32
    )


def own_kernel(offsets, sizes, occ, x, pay, pseudo, table, q, rows):
    for c in range(PLANE // LANES):
        cols = slice(c * LANES, (c + 1) * LANES)
        acc = jnp.zeros((CZ, LANES), F32)
        for n in range(BANDS):
            v = x[n * CZ : (n + 1) * CZ, cols]
            acc = acc + occ[n] * (v * v)
        pseudo[c // 2, (c % 2) * CZ : (c % 2 + 1) * CZ, :] = acc
        table[cols, :] = x[:, cols].T
    rows[...] = jnp.zeros_like(rows)
    gather_rows(offsets, sizes, table, rows)
    q[...] = project(pay, rows, -HALO)


def side_kernel(off_lo, size_lo, off_hi, size_hi, table, pay_lo, pay_hi, q_lo, q_hi, rows):
    rows[...] = jnp.zeros_like(rows)
    gather_rows(off_lo, size_lo, table, rows)
    q_lo[...] = project(pay_lo, rows, -HALO - CZ)
    gather_rows(off_hi, size_hi, table, rows)
    q_hi[...] = project(pay_hi, rows, CZ - HALO)


def matrix_kernel(q0, q1, q2, occ, pseudo, out):
    proj = q0[...] + q1[...] + q2[...]
    weighted = proj * occ[...]
    full = lax.dot_general(
        weighted, proj, (((0,), (0,)), ((), ())), precision=HIGHEST, preferred_element_type=F32
    )
    lane_atom = lax.broadcasted_iota(jnp.int32, (16, LANES), 1) // 16
    acc = jnp.zeros((16, LANES), F32)
    for a in range(ATOM_DEV):
        acc = acc + jnp.where(lane_atom == a, full[a * 16 : (a + 1) * 16, :], 0.0)
    for b in range(16):
        out[b, 0:16, :] = pseudo[b]
        out[b, 16:32, :] = acc


def charge_kernel(start, recv, coupling, shapes, offsets, core, down, up, matrices):
    total = recv[0]
    for b in range(1, 16):
        total = total + recv[b]
    matrix = total[16:32]
    matrices[...] = matrix
    per_lane = jnp.concatenate(
        [jnp.sum(coupling[l] * matrix, axis=0, keepdims=True) for l in range(NL)], axis=0
    )
    atom = lax.broadcasted_iota(jnp.int32, (ATOM_DEV, LANES), 0)
    lane_atom = lax.broadcasted_iota(jnp.int32, (ATOM_DEV, LANES), 1) // 16
    pick = (atom == lane_atom).astype(F32)
    charges = lax.dot_general(
        pick, per_lane, (((1,), (1,)), ((), ())), precision=HIGHEST, preferred_element_type=F32
    )
    comp = jnp.zeros((ATOM_DEV, SPHERE), F32)
    for l in range(NL):
        comp = comp + charges[:, l : l + 1] * shapes[l]
    c1 = comp.astype(BF16).astype(F32)
    c2 = (comp - c1).astype(BF16).astype(F32)
    c3 = comp - c1 - c2
    plane = offsets[...] >> 12
    column = (offsets[...] & (PLANE - 1)) - start[0]
    row = lax.broadcasted_iota(jnp.int32, (24, SPHERE), 0)
    target = jnp.where(row < 8, row + HALO, jnp.where(row < 16, row - 11, row - 3))
    col = lax.broadcasted_iota(jnp.int32, (256, SPHERE), 0)
    acc = jnp.zeros((80, 256), F32)
    for a in range(ATOM_DEV):
        here = target == plane[a : a + 1, :]
        left = jnp.concatenate(
            [jnp.where(here, c[a : a + 1, :], 0.0) for c in (c1, c2, c3)]
            + [jnp.zeros((8, SPHERE), F32)],
            axis=0,
        ).astype(BF16)
        right = jnp.where(col == column[a : a + 1, :], 1.0, 0.0).astype(BF16)
        acc = acc + lax.dot_general(
            left, right, (((1,), (1,)), ((), ())), preferred_element_type=F32
        )
    placed = acc[0:24] + acc[24:48] + acc[48:72]
    core[...] = placed[0:8] + jnp.concatenate([total[0:8], total[8:16]], axis=1)
    down[...] = placed[8:16]
    up[...] = placed[16:24]


def shape(*dims):
    return jax.ShapeDtypeStruct(dims, F32)


def local(orbitals, occupations, projectors, shapes, coupling, sphere_offsets, sphere_sizes):
    slabs = lax.axis_size("slab")
    to_next = [(i, (i + 1) % slabs) for i in range(slabs)]
    to_prev = [((i + 1) % slabs, i) for i in range(slabs)]
    live = jnp.arange(SPHERE, dtype=jnp.int32)[None, :] < sphere_sizes[:, None]
    masked = jnp.where(live[:, None, :], projectors, 0.0)
    pay = jnp.concatenate(
        [
            masked,
            sphere_offsets.astype(F32)[:, None, :],
            jnp.broadcast_to(sphere_sizes.astype(F32)[:, None, None], (ATOM_DEV, 1, SPHERE)),
            jnp.zeros((ATOM_DEV, 1, SPHERE), F32),
        ],
        axis=1,
    )
    pay_lo = lax.ppermute(pay, "slab", to_next)
    pay_hi = lax.ppermute(pay, "slab", to_prev)

    pseudo, table, q_own = pl.pallas_call(
        own_kernel,
        out_shape=(shape(16, 16, LANES), shape(PLANE, LANES), shape(BANDS, LANES)),
        in_specs=[SM, SM, SM, VM, VM],
        out_specs=(VM, VM, VM),
        scratch_shapes=[pltpu.VMEM((ATOM_DEV * SPHERE, LANES), F32)],
        compiler_params=params(),
        cost_estimate=pl.CostEstimate(flops=2 * 10**9, bytes_accessed=8 * 2**20, transcendentals=0),
        name="own_points",
    )(
        sphere_offsets.reshape(-1),
        sphere_sizes,
        occupations,
        orbitals.reshape(BANDS * CZ, PLANE),
        pay,
    )

    def lists(block):
        return block[:, 13, :].astype(jnp.int32).reshape(-1), block[:, 14, 0].astype(jnp.int32)

    off_lo, size_lo = lists(pay_lo)
    off_hi, size_hi = lists(pay_hi)
    q_lo, q_hi = pl.pallas_call(
        side_kernel,
        out_shape=(shape(BANDS, LANES), shape(BANDS, LANES)),
        in_specs=[SM, SM, SM, SM, VM, VM, VM],
        out_specs=(VM, VM),
        scratch_shapes=[pltpu.VMEM((ATOM_DEV * SPHERE, LANES), F32)],
        compiler_params=params(),
        name="side_points",
    )(off_lo, size_lo, off_hi, size_hi, table, pay_lo, pay_hi)
    back_hi = lax.ppermute(q_lo, "slab", to_prev)
    back_lo = lax.ppermute(q_hi, "slab", to_next)

    packed = pl.pallas_call(
        matrix_kernel,
        out_shape=shape(16, 32, LANES),
        in_specs=[VM] * 5,
        out_specs=VM,
        compiler_params=params(),
        name="partial_matrices",
    )(q_own, back_hi, back_lo, jnp.broadcast_to(occupations[:, None], (BANDS, LANES)), pseudo)
    recv = lax.all_to_all(packed, "band", 0, 0)

    coupling_lanes = jnp.tile(jnp.pad(coupling, ((0, 0), (0, 3), (0, 3))), (1, 1, ATOM_DEV))
    shapes_live = jnp.where(live[:, None, :], shapes, 0.0).transpose(1, 0, 2)
    width = PLANE // lax.axis_size("band")
    start = (lax.axis_index("band") * width).astype(jnp.int32).reshape(1)
    core, down, up, matrices = pl.pallas_call(
        charge_kernel,
        out_shape=(shape(CZ, 256), shape(CZ, 256), shape(CZ, 256), shape(16, LANES)),
        in_specs=[SM, VM, VM, VM, VM],
        out_specs=(VM, VM, VM, VM),
        compiler_params=params(),
        name="charges",
    )(start, recv, coupling_lanes, shapes_live, sphere_offsets)
    from_above = lax.ppermute(down, "slab", to_prev)
    from_below = lax.ppermute(up, "slab", to_next)
    density = core + from_above + from_below
    density_matrices = matrices.reshape(16, ATOM_DEV, 16)[:NI, :, :NI].transpose(1, 0, 2)
    return (density, density_matrices)


def solution(mesh):
    placed = (
        P("band", "slab", None),
        P("band"),
        P("slab", None, None),
        P("slab", None, None),
        P(),
        P("slab", None),
        P("slab"),
    )
    return jax.shard_map(
        local,
        mesh=mesh,
        in_specs=placed,
        out_specs=(P("slab", "band"), P("slab", None, None)),
        check_vma=False,
    )
```

```python
import jax
import jax.numpy as jnp
import numpy as np
from jax import lax
from jax.experimental import pallas as pl
from jax.experimental.pallas import tpu as pltpu
from jax.sharding import PartitionSpec as P

HALO = 5
PLANE = 4096
CZ = 8
ATOM_DEV = 8
SPHERE = 512
NI = 13
NL = 9
BANDS = 16
LANES = 128
STEP = 32
HIGHEST = lax.Precision.HIGHEST
F32 = jnp.float32
BF16 = jnp.bfloat16

VM = pl.BlockSpec(memory_space=pltpu.VMEM)
SM = pl.BlockSpec(memory_space=pltpu.SMEM)


def params():
    return pltpu.CompilerParams(vmem_limit_bytes=48 * 2**20)


def gather_rows(points, row, first, last, table, rows, base):
    def body(step, carry):
        k = pl.multiple_of(step * STEP, STEP)
        for u in range(STEP):
            rows[pl.ds(base + k + u, 1), :] = table[pl.ds(points[row, k + u], 1), :]
        return carry

    lax.fori_loop(first, last, body, 0)


def project(pay, rows, shift, planes, begin, end):
    width = end - begin
    span = len(planes) * 16
    lane_plane = lax.broadcasted_iota(jnp.int32, (16, LANES), 1) % CZ
    sub = lax.broadcasted_iota(jnp.int32, (16, width), 0)
    parts = []
    for a in range(ATOM_DEV):
        block = pay[a * 16 : (a + 1) * 16, begin:end]
        plane = block[15:16, :].astype(jnp.int32) + shift
        proj = jnp.where(sub < NI, block, 0.0)
        high = proj.astype(BF16).astype(F32)
        low = proj - high
        pieces = []
        for piece in (high, low):
            for z in planes:
                pieces.append(jnp.where(plane == z, piece, 0.0))
        left = jnp.concatenate(pieces, axis=0).astype(BF16)
        gathered = rows[a * SPHERE + begin : a * SPHERE + end, :]
        g_high = gathered.astype(BF16)
        g_low = (gathered - g_high.astype(F32)).astype(BF16)
        first = jnp.dot(left, g_high, preferred_element_type=F32)
        second = jnp.dot(left[:span], g_low, preferred_element_type=F32)
        total = first[:span] + first[span:] + second
        acc = jnp.zeros((16, LANES), F32)
        for k, z in enumerate(planes):
            acc = acc + jnp.where(lane_plane == z, total[k * 16 : (k + 1) * 16, :], 0.0)
        parts.append(acc)
    summed = jnp.concatenate(parts, axis=0)
    band = lax.broadcasted_iota(jnp.int32, (BANDS, LANES), 0)
    lane_band = lax.broadcasted_iota(jnp.int32, (BANDS, LANES), 1) // CZ
    pick = (band == lane_band).astype(F32)
    return lax.dot_general(
        pick, summed, (((1,), (1,)), ((), ())), precision=HIGHEST, preferred_element_type=F32
    )


def sort_kernel(sizes, offsets, projectors, pay, lists):
    sub = lax.broadcasted_iota(jnp.int32, (ATOM_DEV, SPHERE), 0)
    lane = lax.broadcasted_iota(jnp.int32, (ATOM_DEV, SPHERE), 1)
    size = jnp.zeros((ATOM_DEV, SPHERE), jnp.int32)
    for a in range(ATOM_DEV):
        size = jnp.where(sub == a, sizes[a], size)
    live = lane < size
    off = offsets[...]
    plane = off >> 12
    point = off & (PLANE - 1)
    below = live & (plane < HALO)
    above = live & (plane >= HALO + CZ)
    own = live & (plane >= HALO) & (plane < HALO + CZ)
    flags = jnp.concatenate(
        [jnp.where(m, 1.0, 0.0) for m in (below, own, above)] + [jnp.zeros((8, SPHERE), F32)],
        axis=0,
    ).astype(BF16)
    before = lax.broadcasted_iota(jnp.int32, (SPHERE, SPHERE), 0)
    after = lax.broadcasted_iota(jnp.int32, (SPHERE, SPHERE), 1)
    until = jnp.where(before <= after, 1.0, 0.0).astype(BF16)
    rank = jnp.dot(flags, until, preferred_element_type=F32).astype(jnp.int32)
    n_below = jnp.max(rank[0:8], axis=1, keepdims=True)
    n_own = jnp.max(rank[8:16], axis=1, keepdims=True)
    n_above = jnp.max(rank[16:24], axis=1, keepdims=True)
    place = jnp.where(
        below,
        rank[0:8] - 1,
        jnp.where(own, n_below + rank[8:16] - 1, jnp.where(above, SPHERE - rank[16:24], -1)),
    )
    table = jnp.concatenate(
        [
            projectors[...],
            (point >> 6).astype(F32)[None],
            (point & 63).astype(F32)[None],
            plane.astype(F32)[None],
        ],
        axis=0,
    )
    table = jnp.transpose(table, (1, 0, 2))
    points = []
    for a in range(ATOM_DEV):
        high = table[a].astype(BF16)
        low = (table[a] - high.astype(F32)).astype(BF16)
        move = jnp.where(before == place[a : a + 1, :], 1.0, 0.0).astype(BF16)
        moved = lax.dot_general(
            jnp.concatenate([high, low], axis=0),
            move,
            (((1,), (1,)), ((), ())),
            preferred_element_type=F32,
        )
        moved = moved[0:16] + moved[16:32]
        pay[a * 16 : (a + 1) * 16, :] = moved
        points.append(moved[13:14] * 64.0 + moved[14:15])
    points = jnp.concatenate(points, axis=0)
    pay[128:136, :] = points
    pay[136:144, :] = jnp.where(lane < SPHERE // 2, n_below, n_above).astype(F32)
    lists[0:8, :] = points.astype(jnp.int32)
    lists[8:16, :] = jnp.where(lane < SPHERE // 2, n_below, n_below + n_own)


def own_kernel(lists, occ, x, pay, pseudo, table, q, rows):
    rows[...] = jnp.zeros_like(rows)
    for c in range(PLANE // LANES):
        cols = slice(c * LANES, (c + 1) * LANES)
        acc = jnp.zeros((CZ, LANES), F32)
        for n in range(BANDS):
            v = x[n * CZ : (n + 1) * CZ, cols]
            acc = acc + occ[n] * (v * v)
        pseudo[c // 2, (c % 2) * CZ : (c % 2 + 1) * CZ, :] = acc
        table[cols, :] = x[:, cols].T
    for a in range(ATOM_DEV):
        first = lists[8 + a, 0] // STEP
        last = (lists[8 + a, SPHERE - 1] + (STEP - 1)) // STEP
        gather_rows(lists, a, first, last, table, rows, a * SPHERE)
    q[...] = project(pay, rows, -HALO, range(CZ), 0, SPHERE)


def side_kernel(table, pay_lo, pay_hi, q_lo, q_hi, rows, ints, lists, sem):
    ints[0:16, :] = pay_lo[128:144, :].astype(jnp.int32)
    ints[16:32, :] = pay_hi[128:144, :].astype(jnp.int32)
    copy = pltpu.make_async_copy(ints, lists, sem)
    copy.start()
    rows[...] = jnp.zeros_like(rows)
    copy.wait()
    half = SPHERE // 2
    most = lists[8, SPHERE - 1]
    for a in range(ATOM_DEV):
        most = jnp.maximum(most, jnp.maximum(lists[8 + a, SPHERE - 1], lists[24 + a, 0]))

    def from_below():
        for a in range(ATOM_DEV):
            first = (SPHERE - lists[8 + a, SPHERE - 1]) // STEP
            gather_rows(lists, a, first, SPHERE // STEP, table, rows, a * SPHERE)

    def from_above():
        for a in range(ATOM_DEV):
            last = (lists[24 + a, 0] + (STEP - 1)) // STEP
            gather_rows(lists, 16 + a, 0, last, table, rows, a * SPHERE)

    @pl.when(most <= half)
    def _():
        from_below()
        from_above()
        q_lo[...] = project(pay_lo, rows, -HALO - CZ, range(HALO), half, SPHERE)
        q_hi[...] = project(pay_hi, rows, CZ - HALO, range(CZ - HALO, CZ), 0, half)

    @pl.when(most > half)
    def _():
        from_below()
        q_lo[...] = project(pay_lo, rows, -HALO - CZ, range(HALO), 0, SPHERE)
        from_above()
        q_hi[...] = project(pay_hi, rows, CZ - HALO, range(CZ - HALO, CZ), 0, SPHERE)


def matrix_kernel(q0, q1, q2, occ, pseudo, out):
    proj = q0[...] + q1[...] + q2[...]
    weighted = proj * occ[...]
    full = lax.dot_general(
        weighted, proj, (((0,), (0,)), ((), ())), precision=HIGHEST, preferred_element_type=F32
    )
    lane_atom = lax.broadcasted_iota(jnp.int32, (16, LANES), 1) // 16
    acc = jnp.zeros((16, LANES), F32)
    for a in range(ATOM_DEV):
        acc = acc + jnp.where(lane_atom == a, full[a * 16 : (a + 1) * 16, :], 0.0)
    i = lax.broadcasted_iota(jnp.int32, (8, LANES), 0)
    j = lax.broadcasted_iota(jnp.int32, (8, LANES), 1) % 16
    corner = pltpu.roll(pltpu.roll(acc[8:16], 1, 0), LANES - 8, 1)
    packed = jnp.where(j < i, corner, acc[0:8])
    for b in range(16):
        out[b, 0:16, :] = pseudo[b]
        out[b, 16:24, :] = packed


def charge_kernel(start, recv, coupling, shapes, offsets, core, down, up, matrices):
    total = recv[0]
    for b in range(1, 16):
        total = total + recv[b]
    matrix = total[16:24]
    matrices[...] = matrix
    per_lane = jnp.concatenate(
        [jnp.sum(coupling[l] * matrix, axis=0, keepdims=True) for l in range(NL)], axis=0
    )
    atom = lax.broadcasted_iota(jnp.int32, (ATOM_DEV, LANES), 0)
    lane_atom = lax.broadcasted_iota(jnp.int32, (ATOM_DEV, LANES), 1) // 16
    pick = (atom == lane_atom).astype(F32)
    charges = lax.dot_general(
        pick, per_lane, (((1,), (1,)), ((), ())), precision=HIGHEST, preferred_element_type=F32
    )
    comp = jnp.zeros((ATOM_DEV, SPHERE), F32)
    for l in range(NL):
        comp = comp + charges[:, l : l + 1] * shapes[l]
    c1 = comp.astype(BF16).astype(F32)
    c2 = (comp - c1).astype(BF16).astype(F32)
    c3 = comp - c1 - c2
    plane = offsets[...] >> 12
    column = (offsets[...] & (PLANE - 1)) - start[0]
    row = lax.broadcasted_iota(jnp.int32, (24, SPHERE), 0)
    target = jnp.where(row < 8, row + HALO, jnp.where(row < 16, row - 11, row - 3))
    col = lax.broadcasted_iota(jnp.int32, (256, SPHERE), 0)
    acc = jnp.zeros((80, 256), F32)
    for a in range(ATOM_DEV):
        here = target == plane[a : a + 1, :]
        left = jnp.concatenate(
            [jnp.where(here, c[a : a + 1, :], 0.0) for c in (c1, c2, c3)]
            + [jnp.zeros((8, SPHERE), F32)],
            axis=0,
        ).astype(BF16)
        right = jnp.where(col == column[a : a + 1, :], 1.0, 0.0).astype(BF16)
        acc = acc + lax.dot_general(
            left, right, (((1,), (1,)), ((), ())), preferred_element_type=F32
        )
    placed = acc[0:24] + acc[24:48] + acc[48:72]
    core[...] = placed[0:8] + jnp.concatenate([total[0:8], total[8:16]], axis=1)
    down[...] = placed[8:16]
    up[...] = placed[16:24]


def shape(*dims):
    return jax.ShapeDtypeStruct(dims, F32)


def packed_places():
    places = {}
    for i in range(NI):
        for j in range(NI):
            r, c = min(i, j), max(i, j)
            places[i, j] = (r, c) if r < 8 else (c - 7, r - 8)
    return places


def local(orbitals, occupations, projectors, shapes, coupling, sphere_offsets, sphere_sizes):
    slabs = lax.axis_size("slab")
    to_next = [(i, (i + 1) % slabs) for i in range(slabs)]
    to_prev = [((i + 1) % slabs, i) for i in range(slabs)]
    pay, lists = pl.pallas_call(
        sort_kernel,
        out_shape=(shape(144, SPHERE), jax.ShapeDtypeStruct((16, SPHERE), jnp.int32)),
        in_specs=[SM, VM, VM],
        out_specs=(VM, VM),
        compiler_params=params(),
        name="sort_points",
    )(sphere_sizes, sphere_offsets, projectors.transpose(1, 0, 2))
    pay_lo = lax.ppermute(pay, "slab", to_next)
    pay_hi = lax.ppermute(pay, "slab", to_prev)

    pseudo, table, q_own = pl.pallas_call(
        own_kernel,
        out_shape=(shape(16, 16, LANES), shape(PLANE, LANES), shape(BANDS, LANES)),
        in_specs=[SM, SM, VM, VM],
        out_specs=(VM, VM, VM),
        scratch_shapes=[pltpu.VMEM((ATOM_DEV * SPHERE, LANES), F32)],
        compiler_params=params(),
        cost_estimate=pl.CostEstimate(flops=2 * 10**9, bytes_accessed=8 * 2**20, transcendentals=0),
        name="own_points",
    )(lists, occupations, orbitals.reshape(BANDS * CZ, PLANE), pay)

    q_lo, q_hi = pl.pallas_call(
        side_kernel,
        out_shape=(shape(BANDS, LANES), shape(BANDS, LANES)),
        in_specs=[VM, VM, VM],
        out_specs=(VM, VM),
        scratch_shapes=[
            pltpu.VMEM((ATOM_DEV * SPHERE, LANES), F32),
            pltpu.VMEM((32, SPHERE), jnp.int32),
            pltpu.SMEM((32, SPHERE), jnp.int32),
            pltpu.SemaphoreType.DMA,
        ],
        compiler_params=params(),
        name="side_points",
    )(table, pay_lo, pay_hi)
    back_hi = lax.ppermute(q_lo, "slab", to_prev)
    back_lo = lax.ppermute(q_hi, "slab", to_next)

    packed = pl.pallas_call(
        matrix_kernel,
        out_shape=shape(16, 24, LANES),
        in_specs=[VM] * 5,
        out_specs=VM,
        compiler_params=params(),
        name="partial_matrices",
    )(q_own, back_hi, back_lo, jnp.broadcast_to(occupations[:, None], (BANDS, LANES)), pseudo)
    recv = lax.all_to_all(packed, "band", 0, 0)

    places = packed_places()
    unpack = np.zeros((8, 16, NI, NI), np.float32)
    for (i, j), (p, q) in places.items():
        unpack[p, q, i, j] = 1.0
    coupling_packed = jnp.einsum("lij,pqij->lpq", coupling, unpack, precision=HIGHEST)
    coupling_lanes = jnp.tile(coupling_packed, (1, 1, ATOM_DEV))
    live = jnp.arange(SPHERE, dtype=jnp.int32)[None, :] < sphere_sizes[:, None]
    shapes_live = jnp.where(live[:, None, :], shapes, 0.0).transpose(1, 0, 2)
    width = PLANE // lax.axis_size("band")
    start = (lax.axis_index("band") * width).astype(jnp.int32).reshape(1)
    core, down, up, matrices = pl.pallas_call(
        charge_kernel,
        out_shape=(shape(CZ, 256), shape(CZ, 256), shape(CZ, 256), shape(8, LANES)),
        in_specs=[SM, VM, VM, VM, VM],
        out_specs=(VM, VM, VM, VM),
        compiler_params=params(),
        name="charges",
    )(start, recv, coupling_lanes, shapes_live, sphere_offsets)
    from_above = lax.ppermute(down, "slab", to_prev)
    from_below = lax.ppermute(up, "slab", to_next)
    density = core + from_above + from_below
    density_matrices = jnp.einsum(
        "paq,pqij->aij", matrices.reshape(8, ATOM_DEV, 16), unpack, precision=HIGHEST
    )
    return (density, density_matrices)


def solution(mesh):
    placed = (
        P("band", "slab", None),
        P("band"),
        P("slab", None, None),
        P("slab", None, None),
        P(),
        P("slab", None),
        P("slab"),
    )
    return jax.shard_map(
        local,
        mesh=mesh,
        in_specs=placed,
        out_specs=(P("slab", "band"), P("slab", None, None)),
        check_vma=False,
    )
```

```python
import jax
import jax.numpy as jnp
import numpy as np
from jax import lax
from jax.experimental import pallas as pl
from jax.experimental.pallas import tpu as pltpu
from jax.sharding import PartitionSpec as P

HALO = 5
PLANE = 4096
CZ = 8
ATOM_DEV = 8
SPHERE = 512
NI = 13
NL = 9
BANDS = 16
LANES = 128
STEP = 32
LIST = 16
TILES = SPHERE // LANES
SORTED = TILES * ATOM_DEV * 16
HIGHEST = lax.Precision.HIGHEST
F32 = jnp.float32
BF16 = jnp.bfloat16

VM = pl.BlockSpec(memory_space=pltpu.VMEM)
SM = pl.BlockSpec(memory_space=pltpu.SMEM)


def params(limit=48 * 2**20):
    return pltpu.CompilerParams(vmem_limit_bytes=limit)


def gather_rows(points, row, first, last, table, rows, base):
    def body(step, carry):
        k = pl.multiple_of(step * STEP, STEP)
        at = (step >> 2) * (LIST * LANES) + row * LANES + (step & 3) * STEP
        for u in range(STEP):
            rows[pl.ds(base + k + u, 1), :] = table[pl.ds(points[at + u], 1), :]
        return carry

    lax.fori_loop(first, last, body, 0)


def project(pay, rows, shift, planes, begin, end):
    width = end - begin
    span = len(planes) * 16
    lane_plane = lax.broadcasted_iota(jnp.int32, (16, LANES), 1) % CZ
    sub = lax.broadcasted_iota(jnp.int32, (16, width), 0)
    parts = []
    for a in range(ATOM_DEV):
        block = jnp.concatenate(
            [
                pay[(t * ATOM_DEV + a) * 16 : (t * ATOM_DEV + a + 1) * 16, :]
                for t in range(begin // LANES, end // LANES)
            ],
            axis=1,
        )
        plane = block[15:16, :].astype(jnp.int32) + shift
        proj = jnp.where(sub < NI, block, 0.0)
        high = proj.astype(BF16).astype(F32)
        low = proj - high
        pieces = []
        for piece in (high, low):
            for z in planes:
                pieces.append(jnp.where(plane == z, piece, 0.0))
        left = jnp.concatenate(pieces, axis=0).astype(BF16)
        gathered = rows[a * SPHERE + begin : a * SPHERE + end, :]
        g_high = gathered.astype(BF16)
        g_low = (gathered - g_high.astype(F32)).astype(BF16)
        first = jnp.dot(left, g_high, preferred_element_type=F32)
        second = jnp.dot(left[:span], g_low, preferred_element_type=F32)
        total = first[:span] + first[span:] + second
        acc = jnp.zeros((16, LANES), F32)
        for k, z in enumerate(planes):
            acc = acc + jnp.where(lane_plane == z, total[k * 16 : (k + 1) * 16, :], 0.0)
        parts.append(acc)
    summed = jnp.concatenate(parts, axis=0)
    band = lax.broadcasted_iota(jnp.int32, (BANDS, LANES), 0)
    lane_band = lax.broadcasted_iota(jnp.int32, (BANDS, LANES), 1) // CZ
    pick = (band == lane_band).astype(F32)
    return lax.dot_general(
        pick, summed, (((1,), (1,)), ((), ())), precision=HIGHEST, preferred_element_type=F32
    )


def table_kernel(x, table):
    for c in range(PLANE // LANES):
        cols = slice(c * LANES, (c + 1) * LANES)
        table[cols, :] = x[:, cols].T


def sort_kernel(sizes, offsets, projectors, pay, lists):
    sub = lax.broadcasted_iota(jnp.int32, (ATOM_DEV, SPHERE), 0)
    lane = lax.broadcasted_iota(jnp.int32, (ATOM_DEV, SPHERE), 1)
    size = jnp.zeros((ATOM_DEV, SPHERE), jnp.int32)
    for a in range(ATOM_DEV):
        size = jnp.where(sub == a, sizes[a], size)
    live = lane < size
    off = offsets[...]
    plane = off >> 12
    point = off & (PLANE - 1)
    below = live & (plane < HALO)
    above = live & (plane >= HALO + CZ)
    own = live & (plane >= HALO) & (plane < HALO + CZ)
    flags = jnp.concatenate(
        [jnp.where(m, 1.0, 0.0) for m in (below, own, above)] + [jnp.zeros((8, SPHERE), F32)],
        axis=0,
    ).astype(BF16)
    before = lax.broadcasted_iota(jnp.int32, (SPHERE, SPHERE), 0)
    after = lax.broadcasted_iota(jnp.int32, (SPHERE, SPHERE), 1)
    until = jnp.where(before <= after, 1.0, 0.0).astype(BF16)
    rank = jnp.dot(flags, until, preferred_element_type=F32).astype(jnp.int32)
    n_below = jnp.max(rank[0:8], axis=1, keepdims=True)
    n_own = jnp.max(rank[8:16], axis=1, keepdims=True)
    n_above = jnp.max(rank[16:24], axis=1, keepdims=True)
    place = jnp.where(
        below,
        rank[0:8] - 1,
        jnp.where(own, n_below + rank[8:16] - 1, jnp.where(above, SPHERE - rank[16:24], -1)),
    )
    table = jnp.concatenate(
        [
            projectors[...],
            (point >> 6).astype(F32)[None],
            (point & 63).astype(F32)[None],
            plane.astype(F32)[None],
        ],
        axis=0,
    )
    table = jnp.transpose(table, (1, 0, 2))
    points = []
    for a in range(ATOM_DEV):
        high = table[a].astype(BF16)
        low = (table[a] - high.astype(F32)).astype(BF16)
        move = jnp.where(before == place[a : a + 1, :], 1.0, 0.0).astype(BF16)
        moved = lax.dot_general(
            jnp.concatenate([high, low], axis=0),
            move,
            (((1,), (1,)), ((), ())),
            preferred_element_type=F32,
        )
        moved = moved[0:16] + moved[16:32]
        for t in range(TILES):
            first = (t * ATOM_DEV + a) * 16
            pay[first : first + 16, :] = moved[:, t * LANES : (t + 1) * LANES]
        points.append(moved[13:14] * 64.0 + moved[14:15])
    points = jnp.concatenate(points, axis=0)
    counts = jnp.where(lane < SPHERE // 2, n_below, n_above).astype(F32)
    ends = jnp.where(lane < SPHERE // 2, n_below, n_below + n_own)
    for t in range(TILES):
        cols = slice(t * LANES, (t + 1) * LANES)
        for k, (sent, kept) in enumerate(((points, points.astype(jnp.int32)), (counts, ends))):
            first = t * LIST + k * ATOM_DEV
            pay[SORTED + first : SORTED + first + ATOM_DEV, :] = sent[:, cols]
            lists[first : first + ATOM_DEV, :] = kept[:, cols]


def listed(points, row, k):
    return points[(k // LANES * LIST + row) * LANES + k % LANES]


def own_kernel(lists, occ, x, table, pay, pseudo, q, rows):
    rows[...] = jnp.zeros_like(rows)
    for c in range(PLANE // LANES):
        cols = slice(c * LANES, (c + 1) * LANES)
        acc = jnp.zeros((CZ, LANES), F32)
        for n in range(BANDS):
            v = x[n * CZ : (n + 1) * CZ, cols]
            acc = acc + occ[n] * (v * v)
        pseudo[c // 2, (c % 2) * CZ : (c % 2 + 1) * CZ, :] = acc
    for a in range(ATOM_DEV):
        first = listed(lists, 8 + a, 0) // STEP
        last = (listed(lists, 8 + a, SPHERE - 1) + (STEP - 1)) // STEP
        gather_rows(lists, a, first, last, table, rows, a * SPHERE)
    q[...] = project(pay, rows, -HALO, range(CZ), 0, SPHERE)


def side_kernel(list_lo, list_hi, table, pay_lo, pay_hi, q_lo, q_hi, rows):
    rows[...] = jnp.zeros_like(rows)
    half = SPHERE // 2
    most = jnp.int32(0)
    for a in range(ATOM_DEV):
        most = jnp.maximum(most, listed(list_lo, 8 + a, SPHERE - 1))
        most = jnp.maximum(most, listed(list_hi, 8 + a, 0))

    def from_below():
        for a in range(ATOM_DEV):
            first = (SPHERE - listed(list_lo, 8 + a, SPHERE - 1)) // STEP
            gather_rows(list_lo, a, first, SPHERE // STEP, table, rows, a * SPHERE)

    def from_above():
        for a in range(ATOM_DEV):
            last = (listed(list_hi, 8 + a, 0) + (STEP - 1)) // STEP
            gather_rows(list_hi, a, 0, last, table, rows, a * SPHERE)

    @pl.when(most <= half)
    def _():
        from_below()
        from_above()
        q_lo[...] = project(pay_lo, rows, -HALO - CZ, range(HALO), half, SPHERE)
        q_hi[...] = project(pay_hi, rows, CZ - HALO, range(CZ - HALO, CZ), 0, half)

    @pl.when(most > half)
    def _():
        from_below()
        q_lo[...] = project(pay_lo, rows, -HALO - CZ, range(HALO), 0, SPHERE)
        from_above()
        q_hi[...] = project(pay_hi, rows, CZ - HALO, range(CZ - HALO, CZ), 0, SPHERE)


def matrix_kernel(q0, q1, q2, occ, pseudo, out):
    proj = q0[...] + q1[...] + q2[...]
    weighted = proj * occ[...]
    full = lax.dot_general(
        weighted, proj, (((0,), (0,)), ((), ())), precision=HIGHEST, preferred_element_type=F32
    )
    lane_atom = lax.broadcasted_iota(jnp.int32, (16, LANES), 1) // 16
    acc = jnp.zeros((16, LANES), F32)
    for a in range(ATOM_DEV):
        acc = acc + jnp.where(lane_atom == a, full[a * 16 : (a + 1) * 16, :], 0.0)
    i = lax.broadcasted_iota(jnp.int32, (8, LANES), 0)
    j = lax.broadcasted_iota(jnp.int32, (8, LANES), 1) % 16
    corner = pltpu.roll(pltpu.roll(acc[8:16], 1, 0), LANES - 8, 1)
    packed = jnp.where(j < i, corner, acc[0:8])
    for b in range(16):
        out[b, 0:16, :] = pseudo[b]
        out[b, 16:24, :] = packed


def charge_kernel(start, recv, coupling, shapes, offsets, core, down, up, matrices):
    total = recv[0]
    for b in range(1, 16):
        total = total + recv[b]
    matrix = total[16:24]
    matrices[...] = matrix
    per_lane = jnp.concatenate(
        [jnp.sum(coupling[l] * matrix, axis=0, keepdims=True) for l in range(NL)], axis=0
    )
    atom = lax.broadcasted_iota(jnp.int32, (ATOM_DEV, LANES), 0)
    lane_atom = lax.broadcasted_iota(jnp.int32, (ATOM_DEV, LANES), 1) // 16
    pick = (atom == lane_atom).astype(F32)
    charges = lax.dot_general(
        pick, per_lane, (((1,), (1,)), ((), ())), precision=HIGHEST, preferred_element_type=F32
    )
    comp = jnp.zeros((ATOM_DEV, SPHERE), F32)
    for l in range(NL):
        comp = comp + charges[:, l : l + 1] * shapes[l]
    c1 = comp.astype(BF16).astype(F32)
    c2 = (comp - c1).astype(BF16).astype(F32)
    c3 = comp - c1 - c2
    plane = offsets[...] >> 12
    column = (offsets[...] & (PLANE - 1)) - start[0]
    row = lax.broadcasted_iota(jnp.int32, (24, SPHERE), 0)
    target = jnp.where(row < 8, row + HALO, jnp.where(row < 16, row - 11, row - 3))
    col = lax.broadcasted_iota(jnp.int32, (256, SPHERE), 0)
    acc = jnp.zeros((80, 256), F32)
    for a in range(ATOM_DEV):
        here = target == plane[a : a + 1, :]
        left = jnp.concatenate(
            [jnp.where(here, c[a : a + 1, :], 0.0) for c in (c1, c2, c3)]
            + [jnp.zeros((8, SPHERE), F32)],
            axis=0,
        ).astype(BF16)
        right = jnp.where(col == column[a : a + 1, :], 1.0, 0.0).astype(BF16)
        acc = acc + lax.dot_general(
            left, right, (((1,), (1,)), ((), ())), preferred_element_type=F32
        )
    placed = acc[0:24] + acc[24:48] + acc[48:72]
    core[...] = placed[0:8] + jnp.concatenate([total[0:8], total[8:16]], axis=1)
    down[...] = placed[8:16]
    up[...] = placed[16:24]


def shape(*dims):
    return jax.ShapeDtypeStruct(dims, F32)


def packed_places():
    places = {}
    for i in range(NI):
        for j in range(NI):
            r, c = min(i, j), max(i, j)
            places[i, j] = (r, c) if r < 8 else (c - 7, r - 8)
    return places


def local(orbitals, occupations, projectors, shapes, coupling, sphere_offsets, sphere_sizes):
    slabs = lax.axis_size("slab")
    to_next = [(i, (i + 1) % slabs) for i in range(slabs)]
    to_prev = [((i + 1) % slabs, i) for i in range(slabs)]
    grid_values = orbitals.reshape(BANDS * CZ, PLANE)
    table = pl.pallas_call(
        table_kernel,
        out_shape=shape(PLANE, LANES),
        in_specs=[VM],
        out_specs=VM,
        compiler_params=params(),
        cost_estimate=pl.CostEstimate(flops=0, bytes_accessed=8 * 2**20, transcendentals=0),
        name="grid_table",
    )(grid_values)
    pay, lists = pl.pallas_call(
        sort_kernel,
        out_shape=(
            shape(SORTED + TILES * LIST, LANES),
            jax.ShapeDtypeStruct((TILES * LIST, LANES), jnp.int32),
        ),
        in_specs=[SM, VM, VM],
        out_specs=(VM, VM),
        compiler_params=params(),
        cost_estimate=pl.CostEstimate(flops=10**9, bytes_accessed=8 * 2**20, transcendentals=0),
        name="sort_points",
    )(sphere_sizes, sphere_offsets, projectors.transpose(1, 0, 2))
    pay_lo = lax.ppermute(pay, "slab", to_next)
    pay_hi = lax.ppermute(pay, "slab", to_prev)

    pseudo, q_own = pl.pallas_call(
        own_kernel,
        out_shape=(shape(16, 16, LANES), shape(BANDS, LANES)),
        in_specs=[SM, SM, VM, VM, VM],
        out_specs=(VM, VM),
        scratch_shapes=[pltpu.VMEM((ATOM_DEV * SPHERE, LANES), F32)],
        compiler_params=params(),
        cost_estimate=pl.CostEstimate(flops=2 * 10**9, bytes_accessed=12 * 2**20, transcendentals=0),
        name="own_points",
    )(lists.reshape(-1), occupations, grid_values, table, pay)

    q_lo, q_hi = pl.pallas_call(
        side_kernel,
        out_shape=(shape(BANDS, LANES), shape(BANDS, LANES)),
        in_specs=[SM, SM, VM, VM, VM],
        out_specs=(VM, VM),
        scratch_shapes=[pltpu.VMEM((ATOM_DEV * SPHERE, LANES), F32)],
        compiler_params=params(),
        name="side_points",
    )(
        pay_lo[SORTED:].astype(jnp.int32).reshape(-1),
        pay_hi[SORTED:].astype(jnp.int32).reshape(-1),
        table,
        pay_lo,
        pay_hi,
    )
    back_hi = lax.ppermute(q_lo, "slab", to_prev)
    back_lo = lax.ppermute(q_hi, "slab", to_next)

    packed = pl.pallas_call(
        matrix_kernel,
        out_shape=shape(16, 24, LANES),
        in_specs=[VM] * 5,
        out_specs=VM,
        compiler_params=params(),
        name="partial_matrices",
    )(q_own, back_hi, back_lo, jnp.broadcast_to(occupations[:, None], (BANDS, LANES)), pseudo)
    recv = lax.all_to_all(packed, "band", 0, 0)

    places = packed_places()
    unpack = np.zeros((8, 16, NI, NI), np.float32)
    for (i, j), (p, q) in places.items():
        unpack[p, q, i, j] = 1.0
    coupling_packed = jnp.einsum("lij,pqij->lpq", coupling, unpack, precision=HIGHEST)
    coupling_lanes = jnp.tile(coupling_packed, (1, 1, ATOM_DEV))
    live = jnp.arange(SPHERE, dtype=jnp.int32)[None, :] < sphere_sizes[:, None]
    shapes_live = jnp.where(live[:, None, :], shapes, 0.0).transpose(1, 0, 2)
    width = PLANE // lax.axis_size("band")
    start = (lax.axis_index("band") * width).astype(jnp.int32).reshape(1)
    core, down, up, matrices = pl.pallas_call(
        charge_kernel,
        out_shape=(shape(CZ, 256), shape(CZ, 256), shape(CZ, 256), shape(8, LANES)),
        in_specs=[SM, VM, VM, VM, VM],
        out_specs=(VM, VM, VM, VM),
        compiler_params=params(),
        name="charges",
    )(start, recv, coupling_lanes, shapes_live, sphere_offsets)
    from_above = lax.ppermute(down, "slab", to_prev)
    from_below = lax.ppermute(up, "slab", to_next)
    density = core + from_above + from_below
    density_matrices = jnp.einsum(
        "paq,pqij->aij", matrices.reshape(8, ATOM_DEV, 16), unpack, precision=HIGHEST
    )
    return (density, density_matrices)


def solution(mesh):
    placed = (
        P("band", "slab", None),
        P("band"),
        P("slab", None, None),
        P("slab", None, None),
        P(),
        P("slab", None),
        P("slab"),
    )
    return jax.shard_map(
        local,
        mesh=mesh,
        in_specs=placed,
        out_specs=(P("slab", "band"), P("slab", None, None)),
        check_vma=False,
    )
```

```python
import jax
import jax.numpy as jnp
from jax import lax
from jax.experimental import pallas as pl
from jax.experimental.pallas import tpu as pltpu
from jax.sharding import PartitionSpec as P

HALO = 5
PLANE = 4096
CZ = 8
ATOM_DEV = 8
SPHERE = 512
NI = 13
NL = 9
BANDS = 16
LANES = 128
STEP = 32
EARLY = 4
LIST = 16
TILES = SPHERE // LANES
SORTED = TILES * ATOM_DEV * 16
HIGHEST = lax.Precision.HIGHEST
F32 = jnp.float32
BF16 = jnp.bfloat16

VM = pl.BlockSpec(memory_space=pltpu.VMEM)
SM = pl.BlockSpec(memory_space=pltpu.SMEM)
ANY = pl.BlockSpec(memory_space=pl.ANY)


def params(limit=48 * 2**20):
    return pltpu.CompilerParams(vmem_limit_bytes=limit)


def gather_rows(points, row, first, last, table, rows, base):
    def body(step, carry):
        k = pl.multiple_of(step * STEP, STEP)
        at = (step >> 2) * (LIST * LANES) + row * LANES + (step & 3) * STEP
        for u in range(STEP):
            rows[pl.ds(base + k + u, 1), :] = table[pl.ds(points[at + u], 1), :]
        return carry

    lax.fori_loop(first, last, body, 0)


def project(pay, rows, shift, planes, begin, end, atoms=range(ATOM_DEV)):
    width = end - begin
    span = len(planes) * 16
    lane_plane = lax.broadcasted_iota(jnp.int32, (16, LANES), 1) % CZ
    sub = lax.broadcasted_iota(jnp.int32, (16, width), 0)
    parts = []
    for a in range(ATOM_DEV):
        if a not in atoms:
            parts.append(jnp.zeros((16, LANES), F32))
            continue
        block = jnp.concatenate(
            [
                pay[(t * ATOM_DEV + a) * 16 : (t * ATOM_DEV + a + 1) * 16, :]
                for t in range(begin // LANES, end // LANES)
            ],
            axis=1,
        )
        plane = block[15:16, :].astype(jnp.int32) + shift
        proj = jnp.where(sub < NI, block, 0.0)
        high = proj.astype(BF16).astype(F32)
        low = proj - high
        pieces = []
        for piece in (high, low):
            for z in planes:
                pieces.append(jnp.where(plane == z, piece, 0.0))
        left = jnp.concatenate(pieces, axis=0).astype(BF16)
        gathered = rows[a * SPHERE + begin : a * SPHERE + end, :]
        g_high = gathered.astype(BF16)
        g_low = (gathered - g_high.astype(F32)).astype(BF16)
        first = jnp.dot(left, g_high, preferred_element_type=F32)
        second = jnp.dot(left[:span], g_low, preferred_element_type=F32)
        total = first[:span] + first[span:] + second
        acc = jnp.zeros((16, LANES), F32)
        for k, z in enumerate(planes):
            acc = acc + jnp.where(lane_plane == z, total[k * 16 : (k + 1) * 16, :], 0.0)
        parts.append(acc)
    summed = jnp.concatenate(parts, axis=0)
    band = lax.broadcasted_iota(jnp.int32, (BANDS, LANES), 0)
    lane_band = lax.broadcasted_iota(jnp.int32, (BANDS, LANES), 1) // CZ
    pick = (band == lane_band).astype(F32)
    return lax.dot_general(
        pick, summed, (((1,), (1,)), ((), ())), precision=HIGHEST, preferred_element_type=F32
    )


def table_kernel(x, table):
    for c in range(PLANE // LANES):
        cols = slice(c * LANES, (c + 1) * LANES)
        table[cols, :] = x[:, cols].T


def sort_kernel(sizes_in, offsets_in, projectors_in, pay, lists, sizes, offsets, projectors, sems):
    pairs = ((sizes_in, sizes), (offsets_in, offsets), (projectors_in, projectors))
    copies = [pltpu.make_async_copy(a, b, sems.at[k]) for k, (a, b) in enumerate(pairs)]
    for copy in copies:
        copy.start()
    for copy in copies:
        copy.wait()
    sub = lax.broadcasted_iota(jnp.int32, (ATOM_DEV, SPHERE), 0)
    lane = lax.broadcasted_iota(jnp.int32, (ATOM_DEV, SPHERE), 1)
    size = jnp.zeros((ATOM_DEV, SPHERE), jnp.int32)
    for a in range(ATOM_DEV):
        size = jnp.where(sub == a, sizes[a], size)
    live = lane < size
    off = offsets[...]
    plane = off >> 12
    point = off & (PLANE - 1)
    below = live & (plane < HALO)
    above = live & (plane >= HALO + CZ)
    own = live & (plane >= HALO) & (plane < HALO + CZ)
    flags = jnp.concatenate(
        [jnp.where(m, 1.0, 0.0) for m in (below, own, above)] + [jnp.zeros((8, SPHERE), F32)],
        axis=0,
    ).astype(BF16)
    before = lax.broadcasted_iota(jnp.int32, (SPHERE, SPHERE), 0)
    after = lax.broadcasted_iota(jnp.int32, (SPHERE, SPHERE), 1)
    until = jnp.where(before <= after, 1.0, 0.0).astype(BF16)
    rank = jnp.dot(flags, until, preferred_element_type=F32).astype(jnp.int32)
    n_below = jnp.max(rank[0:8], axis=1, keepdims=True)
    n_own = jnp.max(rank[8:16], axis=1, keepdims=True)
    n_above = jnp.max(rank[16:24], axis=1, keepdims=True)
    place = jnp.where(
        below,
        rank[0:8] - 1,
        jnp.where(own, n_below + rank[8:16] - 1, jnp.where(above, SPHERE - rank[16:24], -1)),
    )
    table = jnp.concatenate(
        [
            projectors[...],
            (point >> 6).astype(F32)[None],
            (point & 63).astype(F32)[None],
            plane.astype(F32)[None],
        ],
        axis=0,
    )
    table = jnp.transpose(table, (1, 0, 2))
    points = []
    for a in range(ATOM_DEV):
        high = table[a].astype(BF16)
        low = (table[a] - high.astype(F32)).astype(BF16)
        move = jnp.where(before == place[a : a + 1, :], 1.0, 0.0).astype(BF16)
        moved = lax.dot_general(
            jnp.concatenate([high, low], axis=0),
            move,
            (((1,), (1,)), ((), ())),
            preferred_element_type=F32,
        )
        moved = moved[0:16] + moved[16:32]
        for t in range(TILES):
            first = (t * ATOM_DEV + a) * 16
            pay[first : first + 16, :] = moved[:, t * LANES : (t + 1) * LANES]
        points.append(moved[13:14] * 64.0 + moved[14:15])
    points = jnp.concatenate(points, axis=0)
    counts = jnp.where(lane < SPHERE // 2, n_below, n_above).astype(F32)
    ends = jnp.where(lane < SPHERE // 2, n_below, n_below + n_own)
    for t in range(TILES):
        cols = slice(t * LANES, (t + 1) * LANES)
        for k, (sent, kept) in enumerate(((points, points.astype(jnp.int32)), (counts, ends))):
            first = t * LIST + k * ATOM_DEV
            pay[SORTED + first : SORTED + first + ATOM_DEV, :] = sent[:, cols]
            lists[first : first + ATOM_DEV, :] = kept[:, cols]


def listed(points, row, k):
    return points[(k // LANES * LIST + row) * LANES + k % LANES]


def own_points(atoms, lists, table, pay, rows):
    rows[...] = jnp.zeros_like(rows)
    for a in atoms:
        first = listed(lists, 8 + a, 0) // STEP
        last = (listed(lists, 8 + a, SPHERE - 1) + (STEP - 1)) // STEP
        gather_rows(lists, a, first, last, table, rows, a * SPHERE)
    return project(pay, rows, -HALO, range(CZ), 0, SPHERE, atoms)


def early_kernel(lists, table, pay, q, rows):
    q[...] = own_points(range(EARLY), lists, table, pay, rows)


def late_kernel(lists, occ, x, table, pay, after, packed, q, rows):
    del after
    for c in range(PLANE // LANES):
        cols = slice(c * LANES, (c + 1) * LANES)
        acc = jnp.zeros((CZ, LANES), F32)
        for n in range(BANDS):
            v = x[n * CZ : (n + 1) * CZ, cols]
            acc = acc + occ[n] * (v * v)
        packed[c // 2, (c % 2) * CZ : (c % 2 + 1) * CZ, :] = acc
    q[...] = own_points(range(EARLY, ATOM_DEV), lists, table, pay, rows)


def side_kernel(list_lo, list_hi, table, pay_lo, pay_hi, q_lo, q_hi, rows):
    rows[...] = jnp.zeros_like(rows)
    half = SPHERE // 2
    most = jnp.int32(0)
    for a in range(ATOM_DEV):
        most = jnp.maximum(most, listed(list_lo, 8 + a, SPHERE - 1))
        most = jnp.maximum(most, listed(list_hi, 8 + a, 0))

    def from_below():
        for a in range(ATOM_DEV):
            first = (SPHERE - listed(list_lo, 8 + a, SPHERE - 1)) // STEP
            gather_rows(list_lo, a, first, SPHERE // STEP, table, rows, a * SPHERE)

    def from_above():
        for a in range(ATOM_DEV):
            last = (listed(list_hi, 8 + a, 0) + (STEP - 1)) // STEP
            gather_rows(list_hi, a, 0, last, table, rows, a * SPHERE)

    @pl.when(most <= half)
    def _():
        from_below()
        from_above()
        q_lo[...] = project(pay_lo, rows, -HALO - CZ, range(HALO), half, SPHERE)
        q_hi[...] = project(pay_hi, rows, CZ - HALO, range(CZ - HALO, CZ), 0, half)

    @pl.when(most > half)
    def _():
        from_below()
        q_lo[...] = project(pay_lo, rows, -HALO - CZ, range(HALO), 0, SPHERE)
        from_above()
        q_hi[...] = project(pay_hi, rows, CZ - HALO, range(CZ - HALO, CZ), 0, SPHERE)


def matrix_kernel(q0, q1, q2, q3, occ, packed, out, block, sem):
    del packed
    proj = q0[...] + q1[...] + q2[...] + q3[...]
    weighted = proj * occ[...]
    full = lax.dot_general(
        weighted, proj, (((0,), (0,)), ((), ())), precision=HIGHEST, preferred_element_type=F32
    )
    lane_atom = lax.broadcasted_iota(jnp.int32, (16, LANES), 1) // 16
    acc = jnp.zeros((16, LANES), F32)
    for a in range(ATOM_DEV):
        acc = acc + jnp.where(lane_atom == a, full[a * 16 : (a + 1) * 16, :], 0.0)
    for b in range(16):
        block[b] = acc
    copy = pltpu.make_async_copy(block, out.at[:, pl.ds(16, 16), :], sem)
    copy.start()
    copy.wait()


def charge_kernel(start, recv, coupling, shapes, offsets, core, down, up, matrices):
    total = recv[0]
    for b in range(1, 16):
        total = total + recv[b]
    matrix = total[16:32]
    matrices[...] = matrix
    per_lane = jnp.concatenate(
        [jnp.sum(coupling[l] * matrix, axis=0, keepdims=True) for l in range(NL)], axis=0
    )
    atom = lax.broadcasted_iota(jnp.int32, (ATOM_DEV, LANES), 0)
    lane_atom = lax.broadcasted_iota(jnp.int32, (ATOM_DEV, LANES), 1) // 16
    pick = (atom == lane_atom).astype(F32)
    charges = lax.dot_general(
        pick, per_lane, (((1,), (1,)), ((), ())), precision=HIGHEST, preferred_element_type=F32
    )
    comp = jnp.zeros((ATOM_DEV, SPHERE), F32)
    for l in range(NL):
        comp = comp + charges[:, l : l + 1] * shapes[l]
    c1 = comp.astype(BF16).astype(F32)
    c2 = (comp - c1).astype(BF16).astype(F32)
    c3 = comp - c1 - c2
    plane = offsets[...] >> 12
    column = (offsets[...] & (PLANE - 1)) - start[0]
    row = lax.broadcasted_iota(jnp.int32, (24, SPHERE), 0)
    target = jnp.where(row < 8, row + HALO, jnp.where(row < 16, row - 11, row - 3))
    col = lax.broadcasted_iota(jnp.int32, (256, SPHERE), 0)
    acc = jnp.zeros((80, 256), F32)
    for a in range(ATOM_DEV):
        here = target == plane[a : a + 1, :]
        left = jnp.concatenate(
            [jnp.where(here, c[a : a + 1, :], 0.0) for c in (c1, c2, c3)]
            + [jnp.zeros((8, SPHERE), F32)],
            axis=0,
        ).astype(BF16)
        right = jnp.where(col == column[a : a + 1, :], 1.0, 0.0).astype(BF16)
        acc = acc + lax.dot_general(
            left, right, (((1,), (1,)), ((), ())), preferred_element_type=F32
        )
    placed = acc[0:24] + acc[24:48] + acc[48:72]
    core[...] = placed[0:8] + jnp.concatenate([total[0:8], total[8:16]], axis=1)
    down[...] = placed[8:16]
    up[...] = placed[16:24]


def shape(*dims):
    return jax.ShapeDtypeStruct(dims, F32)


def local(orbitals, occupations, projectors, shapes, coupling, sphere_offsets, sphere_sizes):
    slabs = lax.axis_size("slab")
    to_next = [(i, (i + 1) % slabs) for i in range(slabs)]
    to_prev = [((i + 1) % slabs, i) for i in range(slabs)]
    grid_values = orbitals.reshape(BANDS * CZ, PLANE)
    table = pl.pallas_call(
        table_kernel,
        out_shape=shape(PLANE, LANES),
        in_specs=[VM],
        out_specs=VM,
        compiler_params=params(),
        cost_estimate=pl.CostEstimate(flops=0, bytes_accessed=8 * 2**20, transcendentals=0),
        name="grid_table",
    )(grid_values)
    pay, lists = pl.pallas_call(
        sort_kernel,
        out_shape=(
            shape(SORTED + TILES * LIST, LANES),
            jax.ShapeDtypeStruct((TILES * LIST, LANES), jnp.int32),
        ),
        in_specs=[ANY] * 3,
        out_specs=(VM, VM),
        scratch_shapes=[
            pltpu.SMEM((ATOM_DEV,), jnp.int32),
            pltpu.VMEM((ATOM_DEV, SPHERE), jnp.int32),
            pltpu.VMEM((NI, ATOM_DEV, SPHERE), F32),
            pltpu.SemaphoreType.DMA((3,)),
        ],
        compiler_params=params(58 * 2**20),
        cost_estimate=pl.CostEstimate(flops=10**9, bytes_accessed=8 * 2**20, transcendentals=0),
        name="sort_points",
    )(sphere_sizes, sphere_offsets, projectors.transpose(1, 0, 2))
    pay_lo = lax.ppermute(pay, "slab", to_next)
    pay_hi = lax.ppermute(pay, "slab", to_prev)

    own_list = lists.reshape(-1)
    scratch = [pltpu.VMEM((ATOM_DEV * SPHERE, LANES), F32)]
    q_early = pl.pallas_call(
        early_kernel,
        out_shape=shape(BANDS, LANES),
        in_specs=[SM, VM, VM],
        out_specs=VM,
        scratch_shapes=scratch,
        compiler_params=params(),
        cost_estimate=pl.CostEstimate(flops=10**9, bytes_accessed=8 * 2**20, transcendentals=0),
        name="own_points_early",
    )(own_list, table, pay)

    q_lo, q_hi = pl.pallas_call(
        side_kernel,
        out_shape=(shape(BANDS, LANES), shape(BANDS, LANES)),
        in_specs=[SM, SM, VM, VM, VM],
        out_specs=(VM, VM),
        scratch_shapes=[pltpu.VMEM((ATOM_DEV * SPHERE, LANES), F32)],
        compiler_params=params(),
        name="side_points",
    )(
        pay_lo[SORTED:].astype(jnp.int32).reshape(-1),
        pay_hi[SORTED:].astype(jnp.int32).reshape(-1),
        table,
        pay_lo,
        pay_hi,
    )
    back_hi = lax.ppermute(q_lo, "slab", to_prev)
    back_lo = lax.ppermute(q_hi, "slab", to_next)

    packed, q_late = pl.pallas_call(
        late_kernel,
        out_shape=(shape(16, 32, LANES), shape(BANDS, LANES)),
        in_specs=[SM, SM, VM, VM, VM, ANY],
        out_specs=(VM, VM),
        scratch_shapes=scratch,
        compiler_params=params(),
        cost_estimate=pl.CostEstimate(flops=10**9, bytes_accessed=8 * 2**20, transcendentals=0),
        name="own_points_late",
    )(own_list, occupations, grid_values, table, pay, q_lo)

    packed = pl.pallas_call(
        matrix_kernel,
        out_shape=shape(16, 32, LANES),
        in_specs=[VM] * 5 + [ANY],
        out_specs=ANY,
        scratch_shapes=[pltpu.VMEM((16, 16, LANES), F32), pltpu.SemaphoreType.DMA],
        input_output_aliases={5: 0},
        compiler_params=params(),
        name="partial_matrices",
    )(
        q_early,
        q_late,
        back_hi,
        back_lo,
        jnp.broadcast_to(occupations[:, None], (BANDS, LANES)),
        packed,
    )
    recv = lax.all_to_all(packed, "band", 0, 0)

    coupling_lanes = jnp.tile(jnp.pad(coupling, ((0, 0), (0, 3), (0, 3))), (1, 1, ATOM_DEV))
    live = jnp.arange(SPHERE, dtype=jnp.int32)[None, :] < sphere_sizes[:, None]
    shapes_live = jnp.where(live[:, None, :], shapes, 0.0).transpose(1, 0, 2)
    width = PLANE // lax.axis_size("band")
    start = (lax.axis_index("band") * width).astype(jnp.int32).reshape(1)
    core, down, up, matrices = pl.pallas_call(
        charge_kernel,
        out_shape=(shape(CZ, 256), shape(CZ, 256), shape(CZ, 256), shape(16, LANES)),
        in_specs=[SM, VM, VM, VM, VM],
        out_specs=(VM, VM, VM, VM),
        compiler_params=params(),
        name="charges",
    )(start, recv, coupling_lanes, shapes_live, sphere_offsets)
    from_above = lax.ppermute(down, "slab", to_prev)
    from_below = lax.ppermute(up, "slab", to_next)
    density = core + from_above + from_below
    density_matrices = matrices.reshape(16, ATOM_DEV, 16)[:NI, :, :NI].transpose(1, 0, 2)
    return (density, density_matrices)


def solution(mesh):
    placed = (
        P("band", "slab", None),
        P("band"),
        P("slab", None, None),
        P("slab", None, None),
        P(),
        P("slab", None),
        P("slab"),
    )
    return jax.shard_map(
        local,
        mesh=mesh,
        in_specs=placed,
        out_specs=(P("slab", "band"), P("slab", None, None)),
        check_vma=False,
    )
```

```python
import jax
import jax.numpy as jnp
from jax import lax
from jax.experimental import pallas as pl
from jax.experimental.pallas import tpu as pltpu
from jax.sharding import PartitionSpec as P

HALO = 5
PLANE = 4096
CZ = 8
ATOM_DEV = 8
SPHERE = 512
NI = 13
NL = 9
BANDS = 16
LANES = 128
EARLY = 4
TILES = SPHERE // LANES
WORDS = SPHERE // 2
SORTED = TILES * ATOM_DEV * 16
LIST = WORDS // LANES * ATOM_DEV + ATOM_DEV
HIGHEST = lax.Precision.HIGHEST
F32 = jnp.float32
BF16 = jnp.bfloat16

VM = pl.BlockSpec(memory_space=pltpu.VMEM)
SM = pl.BlockSpec(memory_space=pltpu.SMEM)
ANY = pl.BlockSpec(memory_space=pl.ANY)


def params(limit=48 * 2**20):
    return pltpu.CompilerParams(vmem_limit_bytes=limit)


def gather_rows(points, atom, first, last, step, table, rows):
    base = atom * SPHERE

    def body(s, carry):
        i = pl.multiple_of(s * step, step)
        at = (i >> 7) * (ATOM_DEV * LANES) + atom * LANES + (i & (LANES - 1))
        for u in range(step):
            word = points[at + u]
            rows[pl.ds(base + i + u, 1), :] = table[pl.ds(word & (PLANE - 1), 1), :]
            rows[pl.ds(base + WORDS + i + u, 1), :] = table[pl.ds(word >> 12, 1), :]
        return carry

    lax.fori_loop(first, last, body, 0)


def counts(points, atom):
    at = WORDS * ATOM_DEV + atom * LANES
    return points[at], points[at + LANES - 1]


def project(pay, rows, shift, planes, tiles, atoms=range(ATOM_DEV)):
    width = len(tiles) * LANES
    span = len(planes) * 16
    lane_plane = lax.broadcasted_iota(jnp.int32, (16, LANES), 1) % CZ
    sub = lax.broadcasted_iota(jnp.int32, (16, width), 0)
    parts = []
    for a in range(ATOM_DEV):
        if a not in atoms:
            parts.append(jnp.zeros((16, LANES), F32))
            continue
        block = jnp.concatenate(
            [pay[(a * TILES + t) * 16 : (a * TILES + t + 1) * 16, :] for t in tiles], axis=1
        )
        plane = block[15:16, :].astype(jnp.int32) + shift
        proj = jnp.where(sub < NI, block, 0.0)
        high = proj.astype(BF16).astype(F32)
        low = proj - high
        pieces = []
        for piece in (high, low):
            for z in planes:
                pieces.append(jnp.where(plane == z, piece, 0.0))
        left = jnp.concatenate(pieces, axis=0).astype(BF16)
        gathered = jnp.concatenate(
            [rows[a * SPHERE + t * LANES : a * SPHERE + (t + 1) * LANES, :] for t in tiles], axis=0
        )
        g_high = gathered.astype(BF16)
        g_low = (gathered - g_high.astype(F32)).astype(BF16)
        first = jnp.dot(left, g_high, preferred_element_type=F32)
        second = jnp.dot(left[:span], g_low, preferred_element_type=F32)
        total = first[:span] + first[span:] + second
        acc = jnp.zeros((16, LANES), F32)
        for k, z in enumerate(planes):
            acc = acc + jnp.where(lane_plane == z, total[k * 16 : (k + 1) * 16, :], 0.0)
        parts.append(acc)
    summed = jnp.concatenate(parts, axis=0)
    band = lax.broadcasted_iota(jnp.int32, (BANDS, LANES), 0)
    lane_band = lax.broadcasted_iota(jnp.int32, (BANDS, LANES), 1) // CZ
    pick = (band == lane_band).astype(F32)
    return lax.dot_general(
        pick, summed, (((1,), (1,)), ((), ())), precision=HIGHEST, preferred_element_type=F32
    )


def table_kernel(x, table):
    for c in range(PLANE // LANES):
        cols = slice(c * LANES, (c + 1) * LANES)
        table[cols, :] = x[:, cols].T


def sort_kernel(
    sizes_in, offsets_in, projectors_in, pay_out, lists, pay, sizes, offsets, projectors, sems
):
    pairs = ((sizes_in, sizes), (offsets_in, offsets), (projectors_in, projectors))
    copies = [pltpu.make_async_copy(a, b, sems.at[k]) for k, (a, b) in enumerate(pairs)]
    for copy in copies:
        copy.start()
    before = lax.broadcasted_iota(jnp.int32, (SPHERE, SPHERE), 0)
    after = lax.broadcasted_iota(jnp.int32, (SPHERE, SPHERE), 1)
    until = jnp.where(before <= after, 1.0, 0.0).astype(BF16)
    sub = lax.broadcasted_iota(jnp.int32, (ATOM_DEV, SPHERE), 0)
    lane = lax.broadcasted_iota(jnp.int32, (ATOM_DEV, SPHERE), 1)
    copies[0].wait()
    copies[1].wait()
    size = jnp.zeros((ATOM_DEV, SPHERE), jnp.int32)
    for a in range(ATOM_DEV):
        size = jnp.where(sub == a, sizes[a], size)
    live = lane < size
    off = offsets[...]
    plane = off >> 12
    point = off & (PLANE - 1)
    below = live & (plane < HALO)
    above = live & (plane >= HALO + CZ)
    own = live & (plane >= HALO) & (plane < HALO + CZ)
    flags = jnp.concatenate(
        [jnp.where(m, 1.0, 0.0) for m in (below, own, above)] + [jnp.zeros((8, SPHERE), F32)],
        axis=0,
    ).astype(BF16)
    rank = jnp.dot(flags, until, preferred_element_type=F32).astype(jnp.int32)
    n_below = jnp.max(rank[0:8], axis=1, keepdims=True)
    n_own = jnp.max(rank[8:16], axis=1, keepdims=True)
    n_above = jnp.max(rank[16:24], axis=1, keepdims=True)
    place = jnp.where(
        below,
        rank[0:8] - 1,
        jnp.where(own, n_below + rank[8:16] - 1, SPHERE - rank[16:24]),
    )
    place = jnp.where(live, (place >> 1) + (place & 1) * WORDS, -1)
    copies[2].wait()
    table = jnp.concatenate(
        [
            projectors[...],
            (point >> 6).astype(F32)[None],
            (point & 63).astype(F32)[None],
            plane.astype(F32)[None],
        ],
        axis=0,
    )
    table = jnp.transpose(table, (1, 0, 2))
    points = []
    sent = []
    for a in range(ATOM_DEV):
        high = table[a].astype(BF16)
        low = (table[a] - high.astype(F32)).astype(BF16)
        move = jnp.where(before == place[a : a + 1, :], 1.0, 0.0).astype(BF16)
        moved = lax.dot_general(
            jnp.concatenate([high, low], axis=0),
            move,
            (((1,), (1,)), ((), ())),
            preferred_element_type=F32,
        )
        moved = moved[0:16] + moved[16:32]
        first = a * TILES * 16
        for t in range(TILES):
            pay[first + t * 16 : first + (t + 1) * 16, :] = moved[:, t * LANES : (t + 1) * LANES]
        block = pl.ds(first, TILES * 16)
        sent.append(pltpu.make_async_copy(pay.at[block], pay_out.at[block], sems.at[3 + a]))
        sent[-1].start()
        points.append(moved[13:14] * 64.0 + moved[14:15])
    points = jnp.concatenate(points, axis=0)
    words = points[:, :WORDS] + points[:, WORDS:] * float(PLANE)
    for t in range(WORDS // LANES):
        part = words[:, t * LANES : (t + 1) * LANES]
        at = t * ATOM_DEV
        pay[SORTED + at : SORTED + at + ATOM_DEV, :] = part
        lists[at : at + ATOM_DEV, :] = part.astype(jnp.int32)
    at = LIST - ATOM_DEV
    lead = lane[:, :LANES] < LANES // 2
    pay[SORTED + at : SORTED + LIST, :] = jnp.where(lead, n_below, n_above).astype(F32)
    lists[at:LIST, :] = jnp.where(lead, n_below, n_below + n_own)
    block = pl.ds(SORTED, LIST)
    sent.append(pltpu.make_async_copy(pay.at[block], pay_out.at[block], sems.at[3 + ATOM_DEV]))
    sent[-1].start()
    for copy in sent:
        copy.wait()


def own_points(atoms, lists, table, pay, rows):
    rows[...] = jnp.zeros_like(rows)
    step = 16
    for a in atoms:
        begin, end = counts(lists, a)
        first = begin // (2 * step)
        last = (end + (2 * step - 1)) // (2 * step)
        gather_rows(lists, a, first, last, step, table, rows)
    return project(pay, rows, -HALO, range(CZ), range(TILES), atoms)


def early_kernel(lists, table, pay, q, rows):
    q[...] = own_points(range(EARLY), lists, table, pay, rows)


def late_kernel(lists, occ, x, table, pay, after, packed, q, rows):
    del after
    for c in range(PLANE // LANES):
        cols = slice(c * LANES, (c + 1) * LANES)
        acc = jnp.zeros((CZ, LANES), F32)
        for n in range(BANDS):
            v = x[n * CZ : (n + 1) * CZ, cols]
            acc = acc + occ[n] * (v * v)
        packed[c // 2, (c % 2) * CZ : (c % 2 + 1) * CZ, :] = acc
    q[...] = own_points(range(EARLY, ATOM_DEV), lists, table, pay, rows)


def side_kernel(list_lo, list_hi, table, pay_lo, pay_hi, q_lo, q_hi, rows):
    rows[...] = jnp.zeros_like(rows)
    step = 8
    most = jnp.int32(0)
    for a in range(ATOM_DEV):
        most = jnp.maximum(most, jnp.maximum(counts(list_lo, a)[1], counts(list_hi, a)[0]))

    def from_below():
        for a in range(ATOM_DEV):
            first = (SPHERE - counts(list_lo, a)[1]) // (2 * step)
            gather_rows(list_lo, a, first, WORDS // step, step, table, rows)

    def from_above():
        for a in range(ATOM_DEV):
            last = (counts(list_hi, a)[0] + (2 * step - 1)) // (2 * step)
            gather_rows(list_hi, a, 0, last, step, table, rows)

    low, high = range(HALO), range(CZ - HALO, CZ)

    @pl.when(most <= WORDS)
    def _():
        from_below()
        from_above()
        q_lo[...] = project(pay_lo, rows, -HALO - CZ, low, (1, 3))
        q_hi[...] = project(pay_hi, rows, CZ - HALO, high, (0, 2))

    @pl.when(most > WORDS)
    def _():
        from_below()
        q_lo[...] = project(pay_lo, rows, -HALO - CZ, low, range(TILES))
        from_above()
        q_hi[...] = project(pay_hi, rows, CZ - HALO, high, range(TILES))


def matrix_kernel(q0, q1, q2, q3, occ, packed, out, block, sem):
    del packed
    proj = q0[...] + q1[...] + q2[...] + q3[...]
    weighted = proj * occ[...]
    full = lax.dot_general(
        weighted, proj, (((0,), (0,)), ((), ())), precision=HIGHEST, preferred_element_type=F32
    )
    lane_atom = lax.broadcasted_iota(jnp.int32, (16, LANES), 1) // 16
    acc = jnp.zeros((16, LANES), F32)
    for a in range(ATOM_DEV):
        acc = acc + jnp.where(lane_atom == a, full[a * 16 : (a + 1) * 16, :], 0.0)
    for b in range(16):
        block[b] = acc
    copy = pltpu.make_async_copy(block, out.at[:, pl.ds(16, 16), :], sem)
    copy.start()
    copy.wait()


def charge_kernel(start, recv, coupling, shapes, offsets, core, down, up, matrices):
    total = recv[0]
    for b in range(1, 16):
        total = total + recv[b]
    matrix = total[16:32]
    matrices[...] = matrix
    per_lane = jnp.concatenate(
        [jnp.sum(coupling[l] * matrix, axis=0, keepdims=True) for l in range(NL)], axis=0
    )
    atom = lax.broadcasted_iota(jnp.int32, (ATOM_DEV, LANES), 0)
    lane_atom = lax.broadcasted_iota(jnp.int32, (ATOM_DEV, LANES), 1) // 16
    pick = (atom == lane_atom).astype(F32)
    charges = lax.dot_general(
        pick, per_lane, (((1,), (1,)), ((), ())), precision=HIGHEST, preferred_element_type=F32
    )
    comp = jnp.zeros((ATOM_DEV, SPHERE), F32)
    for l in range(NL):
        comp = comp + charges[:, l : l + 1] * shapes[l]
    c1 = comp.astype(BF16).astype(F32)
    c2 = (comp - c1).astype(BF16).astype(F32)
    c3 = comp - c1 - c2
    plane = offsets[...] >> 12
    column = (offsets[...] & (PLANE - 1)) - start[0]
    row = lax.broadcasted_iota(jnp.int32, (24, SPHERE), 0)
    target = jnp.where(row < 8, row + HALO, jnp.where(row < 16, row - 11, row - 3))
    col = lax.broadcasted_iota(jnp.int32, (256, SPHERE), 0)
    acc = jnp.zeros((80, 256), F32)
    for a in range(ATOM_DEV):
        here = target == plane[a : a + 1, :]
        left = jnp.concatenate(
            [jnp.where(here, c[a : a + 1, :], 0.0) for c in (c1, c2, c3)]
            + [jnp.zeros((8, SPHERE), F32)],
            axis=0,
        ).astype(BF16)
        right = jnp.where(col == column[a : a + 1, :], 1.0, 0.0).astype(BF16)
        acc = acc + lax.dot_general(
            left, right, (((1,), (1,)), ((), ())), preferred_element_type=F32
        )
    placed = acc[0:24] + acc[24:48] + acc[48:72]
    core[...] = placed[0:8] + jnp.concatenate([total[0:8], total[8:16]], axis=1)
    down[...] = placed[8:16]
    up[...] = placed[16:24]


def shape(*dims):
    return jax.ShapeDtypeStruct(dims, F32)


def local(orbitals, occupations, projectors, shapes, coupling, sphere_offsets, sphere_sizes):
    slabs = lax.axis_size("slab")
    to_next = [(i, (i + 1) % slabs) for i in range(slabs)]
    to_prev = [((i + 1) % slabs, i) for i in range(slabs)]
    grid_values = orbitals.reshape(BANDS * CZ, PLANE)
    table = pl.pallas_call(
        table_kernel,
        out_shape=shape(PLANE, LANES),
        in_specs=[VM],
        out_specs=VM,
        compiler_params=params(),
        cost_estimate=pl.CostEstimate(flops=0, bytes_accessed=8 * 2**20, transcendentals=0),
        name="grid_table",
    )(grid_values)
    pay, lists = pl.pallas_call(
        sort_kernel,
        out_shape=(
            shape(SORTED + LIST, LANES),
            jax.ShapeDtypeStruct((LIST, LANES), jnp.int32),
        ),
        in_specs=[ANY] * 3,
        out_specs=(ANY, VM),
        scratch_shapes=[
            pltpu.VMEM((SORTED + LIST, LANES), F32),
            pltpu.SMEM((ATOM_DEV,), jnp.int32),
            pltpu.VMEM((ATOM_DEV, SPHERE), jnp.int32),
            pltpu.VMEM((NI, ATOM_DEV, SPHERE), F32),
            pltpu.SemaphoreType.DMA((4 + ATOM_DEV,)),
        ],
        compiler_params=params(58 * 2**20),
        cost_estimate=pl.CostEstimate(flops=10**9, bytes_accessed=8 * 2**20, transcendentals=0),
        name="sort_points",
    )(sphere_sizes, sphere_offsets, projectors.transpose(1, 0, 2))
    pay_lo = lax.ppermute(pay, "slab", to_next)
    pay_hi = lax.ppermute(pay, "slab", to_prev)

    own_list = lists.reshape(-1)
    scratch = [pltpu.VMEM((ATOM_DEV * SPHERE, LANES), F32)]
    q_early = pl.pallas_call(
        early_kernel,
        out_shape=shape(BANDS, LANES),
        in_specs=[SM, VM, VM],
        out_specs=VM,
        scratch_shapes=scratch,
        compiler_params=params(),
        cost_estimate=pl.CostEstimate(flops=10**9, bytes_accessed=8 * 2**20, transcendentals=0),
        name="own_points_early",
    )(own_list, table, pay)

    q_lo, q_hi = pl.pallas_call(
        side_kernel,
        out_shape=(shape(BANDS, LANES), shape(BANDS, LANES)),
        in_specs=[SM, SM, VM, VM, VM],
        out_specs=(VM, VM),
        scratch_shapes=[pltpu.VMEM((ATOM_DEV * SPHERE, LANES), F32)],
        compiler_params=params(),
        name="side_points",
    )(
        pay_lo[SORTED:].astype(jnp.int32).reshape(-1),
        pay_hi[SORTED:].astype(jnp.int32).reshape(-1),
        table,
        pay_lo,
        pay_hi,
    )
    back_hi = lax.ppermute(q_lo, "slab", to_prev)
    back_lo = lax.ppermute(q_hi, "slab", to_next)

    packed, q_late = pl.pallas_call(
        late_kernel,
        out_shape=(shape(16, 32, LANES), shape(BANDS, LANES)),
        in_specs=[SM, SM, VM, VM, VM, ANY],
        out_specs=(VM, VM),
        scratch_shapes=scratch,
        compiler_params=params(),
        cost_estimate=pl.CostEstimate(flops=10**9, bytes_accessed=8 * 2**20, transcendentals=0),
        name="own_points_late",
    )(own_list, occupations, grid_values, table, pay, q_lo)

    packed = pl.pallas_call(
        matrix_kernel,
        out_shape=shape(16, 32, LANES),
        in_specs=[VM] * 5 + [ANY],
        out_specs=ANY,
        scratch_shapes=[pltpu.VMEM((16, 16, LANES), F32), pltpu.SemaphoreType.DMA],
        input_output_aliases={5: 0},
        compiler_params=params(),
        name="partial_matrices",
    )(
        q_early,
        q_late,
        back_hi,
        back_lo,
        jnp.broadcast_to(occupations[:, None], (BANDS, LANES)),
        packed,
    )
    recv = lax.all_to_all(packed, "band", 0, 0)

    coupling_lanes = jnp.tile(jnp.pad(coupling, ((0, 0), (0, 3), (0, 3))), (1, 1, ATOM_DEV))
    live = jnp.arange(SPHERE, dtype=jnp.int32)[None, :] < sphere_sizes[:, None]
    shapes_live = jnp.where(live[:, None, :], shapes, 0.0).transpose(1, 0, 2)
    width = PLANE // lax.axis_size("band")
    start = (lax.axis_index("band") * width).astype(jnp.int32).reshape(1)
    core, down, up, matrices = pl.pallas_call(
        charge_kernel,
        out_shape=(shape(CZ, 256), shape(CZ, 256), shape(CZ, 256), shape(16, LANES)),
        in_specs=[SM, VM, VM, VM, VM],
        out_specs=(VM, VM, VM, VM),
        compiler_params=params(),
        name="charges",
    )(start, recv, coupling_lanes, shapes_live, sphere_offsets)
    from_above = lax.ppermute(down, "slab", to_prev)
    from_below = lax.ppermute(up, "slab", to_next)
    density = core + from_above + from_below
    density_matrices = matrices.reshape(16, ATOM_DEV, 16)[:NI, :, :NI].transpose(1, 0, 2)
    return (density, density_matrices)


def solution(mesh):
    placed = (
        P("band", "slab", None),
        P("band"),
        P("slab", None, None),
        P("slab", None, None),
        P(),
        P("slab", None),
        P("slab"),
    )
    return jax.shard_map(
        local,
        mesh=mesh,
        in_specs=placed,
        out_specs=(P("slab", "band"), P("slab", None, None)),
        check_vma=False,
    )
```

```python
import jax
import jax.numpy as jnp
from jax import lax
from jax.experimental import pallas as pl
from jax.experimental.pallas import tpu as pltpu
from jax.sharding import PartitionSpec as P

HALO = 5
PLANE = 4096
CZ = 8
ATOM_DEV = 8
SPHERE = 512
NI = 13
NL = 9
BANDS = 16
LANES = 128
EARLY = 6
TILES = SPHERE // LANES
WORDS = SPHERE // 2
SORTED = TILES * ATOM_DEV * 16
LIST = WORDS // LANES * ATOM_DEV + ATOM_DEV
HIGHEST = lax.Precision.HIGHEST
F32 = jnp.float32
BF16 = jnp.bfloat16

VM = pl.BlockSpec(memory_space=pltpu.VMEM)
SM = pl.BlockSpec(memory_space=pltpu.SMEM)
ANY = pl.BlockSpec(memory_space=pl.ANY)


def params(limit=48 * 2**20):
    return pltpu.CompilerParams(vmem_limit_bytes=limit)


def gather_rows(points, atom, first, last, step, table, rows):
    base = atom * SPHERE

    def body(s, carry):
        i = pl.multiple_of(s * step, step)
        at = (i >> 7) * (ATOM_DEV * LANES) + atom * LANES + (i & (LANES - 1))
        for u in range(step):
            word = points[at + u]
            rows[pl.ds(base + i + u, 1), :] = table[pl.ds(word & (PLANE - 1), 1), :]
            rows[pl.ds(base + WORDS + i + u, 1), :] = table[pl.ds(word >> 12, 1), :]
        return carry

    lax.fori_loop(first, last, body, 0)


def counts(points, atom):
    at = WORDS * ATOM_DEV + atom * LANES
    return points[at], points[at + LANES - 1]


def project(pay, rows, shift, planes, tiles, atoms=range(ATOM_DEV)):
    width = len(tiles) * LANES
    span = len(planes) * 16
    lane_plane = lax.broadcasted_iota(jnp.int32, (16, LANES), 1) % CZ
    sub = lax.broadcasted_iota(jnp.int32, (16, width), 0)
    parts = []
    for a in range(ATOM_DEV):
        if a not in atoms:
            parts.append(jnp.zeros((16, LANES), F32))
            continue
        block = jnp.concatenate(
            [pay[(a * TILES + t) * 16 : (a * TILES + t + 1) * 16, :] for t in tiles], axis=1
        )
        plane = block[15:16, :].astype(jnp.int32) + shift
        proj = jnp.where(sub < NI, block, 0.0)
        high = proj.astype(BF16).astype(F32)
        low = proj - high
        pieces = []
        for piece in (high, low):
            for z in planes:
                pieces.append(jnp.where(plane == z, piece, 0.0))
        left = jnp.concatenate(pieces, axis=0).astype(BF16)
        gathered = jnp.concatenate(
            [rows[a * SPHERE + t * LANES : a * SPHERE + (t + 1) * LANES, :] for t in tiles], axis=0
        )
        g_high = gathered.astype(BF16)
        g_low = (gathered - g_high.astype(F32)).astype(BF16)
        first = jnp.dot(left, g_high, preferred_element_type=F32)
        second = jnp.dot(left[:span], g_low, preferred_element_type=F32)
        total = first[:span] + first[span:] + second
        acc = jnp.zeros((16, LANES), F32)
        for k, z in enumerate(planes):
            acc = acc + jnp.where(lane_plane == z, total[k * 16 : (k + 1) * 16, :], 0.0)
        parts.append(acc)
    summed = jnp.concatenate(parts, axis=0)
    band = lax.broadcasted_iota(jnp.int32, (BANDS, LANES), 0)
    lane_band = lax.broadcasted_iota(jnp.int32, (BANDS, LANES), 1) // CZ
    pick = (band == lane_band).astype(F32)
    return lax.dot_general(
        pick, summed, (((1,), (1,)), ((), ())), precision=HIGHEST, preferred_element_type=F32
    )


def table_kernel(x, table):
    for c in range(PLANE // LANES):
        cols = slice(c * LANES, (c + 1) * LANES)
        table[cols, :] = x[:, cols].T


def sort_kernel(
    sizes_in, offsets_in, projectors_in, pay, lists, sizes, offsets, projectors, sems
):
    pairs = ((sizes_in, sizes), (offsets_in, offsets), (projectors_in, projectors))
    copies = [pltpu.make_async_copy(a, b, sems.at[k]) for k, (a, b) in enumerate(pairs)]
    for copy in copies:
        copy.start()
    before = lax.broadcasted_iota(jnp.int32, (SPHERE, SPHERE), 0)
    after = lax.broadcasted_iota(jnp.int32, (SPHERE, SPHERE), 1)
    until = jnp.where(before <= after, 1.0, 0.0).astype(BF16)
    sub = lax.broadcasted_iota(jnp.int32, (ATOM_DEV, SPHERE), 0)
    lane = lax.broadcasted_iota(jnp.int32, (ATOM_DEV, SPHERE), 1)
    copies[0].wait()
    copies[1].wait()
    size = jnp.zeros((ATOM_DEV, SPHERE), jnp.int32)
    for a in range(ATOM_DEV):
        size = jnp.where(sub == a, sizes[a], size)
    live = lane < size
    off = offsets[...]
    plane = off >> 12
    point = off & (PLANE - 1)
    below = live & (plane < HALO)
    above = live & (plane >= HALO + CZ)
    own = live & (plane >= HALO) & (plane < HALO + CZ)
    flags = jnp.concatenate(
        [jnp.where(m, 1.0, 0.0) for m in (below, own, above)] + [jnp.zeros((8, SPHERE), F32)],
        axis=0,
    ).astype(BF16)
    rank = jnp.dot(flags, until, preferred_element_type=F32).astype(jnp.int32)
    n_below = jnp.max(rank[0:8], axis=1, keepdims=True)
    n_own = jnp.max(rank[8:16], axis=1, keepdims=True)
    n_above = jnp.max(rank[16:24], axis=1, keepdims=True)
    place = jnp.where(
        below,
        rank[0:8] - 1,
        jnp.where(own, n_below + rank[8:16] - 1, SPHERE - rank[16:24]),
    )
    place = jnp.where(live, (place >> 1) + (place & 1) * WORDS, -1)
    copies[2].wait()
    table = jnp.concatenate(
        [
            projectors[...],
            (point >> 6).astype(F32)[None],
            (point & 63).astype(F32)[None],
            plane.astype(F32)[None],
        ],
        axis=0,
    )
    table = jnp.transpose(table, (1, 0, 2))
    points = []
    for a in range(ATOM_DEV):
        high = table[a].astype(BF16)
        low = (table[a] - high.astype(F32)).astype(BF16)
        move = jnp.where(before == place[a : a + 1, :], 1.0, 0.0).astype(BF16)
        moved = lax.dot_general(
            jnp.concatenate([high, low], axis=0),
            move,
            (((1,), (1,)), ((), ())),
            preferred_element_type=F32,
        )
        moved = moved[0:16] + moved[16:32]
        first = a * TILES * 16
        for t in range(TILES):
            pay[first + t * 16 : first + (t + 1) * 16, :] = moved[:, t * LANES : (t + 1) * LANES]
        points.append(moved[13:14] * 64.0 + moved[14:15])
    points = jnp.concatenate(points, axis=0)
    words = points[:, :WORDS] + points[:, WORDS:] * float(PLANE)
    for t in range(WORDS // LANES):
        at = t * ATOM_DEV
        lists[at : at + ATOM_DEV, :] = words[:, t * LANES : (t + 1) * LANES].astype(jnp.int32)
        for start, shift in ((SORTED, 0), (SORTED + LIST, WORDS)):
            part = points[:, shift + t * LANES : shift + (t + 1) * LANES]
            pay[start + at : start + at + ATOM_DEV, :] = part
    at = LIST - ATOM_DEV
    lead = lane[:, :LANES] < LANES // 2
    pay[SORTED + at : SORTED + LIST, :] = jnp.where(lead, n_below, n_above).astype(F32)
    pay[SORTED + LIST + at : SORTED + 2 * LIST, :] = jnp.zeros((ATOM_DEV, LANES), F32)
    lists[at:LIST, :] = jnp.where(lead, n_below, n_below + n_own)


def words_of(pay):
    words = pay[SORTED : SORTED + LIST] + pay[SORTED + LIST :] * float(PLANE)
    return words.astype(jnp.int32).reshape(-1)


def own_points(atoms, lists, table, pay, rows):
    rows[...] = jnp.zeros_like(rows)
    step = 16
    for a in atoms:
        begin, end = counts(lists, a)
        first = begin // (2 * step)
        last = (end + (2 * step - 1)) // (2 * step)
        gather_rows(lists, a, first, last, step, table, rows)
    return project(pay, rows, -HALO, range(CZ), range(TILES), atoms)


def early_kernel(lists, table, pay, q, rows):
    q[...] = own_points(range(EARLY), lists, table, pay, rows)


def late_kernel(lists, occ, x, table, pay, after, packed, q, rows):
    del after
    for c in range(PLANE // LANES):
        cols = slice(c * LANES, (c + 1) * LANES)
        acc = jnp.zeros((CZ, LANES), F32)
        for n in range(BANDS):
            v = x[n * CZ : (n + 1) * CZ, cols]
            acc = acc + occ[n] * (v * v)
        packed[c // 2, (c % 2) * CZ : (c % 2 + 1) * CZ, :] = acc
    q[...] = own_points(range(EARLY, ATOM_DEV), lists, table, pay, rows)


def side_kernel(list_lo, list_hi, table, pay_lo, pay_hi, q_lo, q_hi, rows):
    rows[...] = jnp.zeros_like(rows)
    step = 8
    most = jnp.int32(0)
    for a in range(ATOM_DEV):
        most = jnp.maximum(most, jnp.maximum(counts(list_lo, a)[1], counts(list_hi, a)[0]))

    def from_below():
        for a in range(ATOM_DEV):
            first = (SPHERE - counts(list_lo, a)[1]) // (2 * step)
            gather_rows(list_lo, a, first, WORDS // step, step, table, rows)

    def from_above():
        for a in range(ATOM_DEV):
            last = (counts(list_hi, a)[0] + (2 * step - 1)) // (2 * step)
            gather_rows(list_hi, a, 0, last, step, table, rows)

    low, high = range(HALO), range(CZ - HALO, CZ)

    @pl.when(most <= WORDS)
    def _():
        from_below()
        from_above()
        q_lo[...] = project(pay_lo, rows, -HALO - CZ, low, (1, 3))
        q_hi[...] = project(pay_hi, rows, CZ - HALO, high, (0, 2))

    @pl.when(most > WORDS)
    def _():
        from_below()
        q_lo[...] = project(pay_lo, rows, -HALO - CZ, low, range(TILES))
        from_above()
        q_hi[...] = project(pay_hi, rows, CZ - HALO, high, range(TILES))


def matrix_kernel(q0, q1, q2, q3, occ, packed, out, block, sem):
    del packed
    proj = q0[...] + q1[...] + q2[...] + q3[...]
    weighted = proj * occ[...]
    full = lax.dot_general(
        weighted, proj, (((0,), (0,)), ((), ())), precision=HIGHEST, preferred_element_type=F32
    )
    lane_atom = lax.broadcasted_iota(jnp.int32, (16, LANES), 1) // 16
    acc = jnp.zeros((16, LANES), F32)
    for a in range(ATOM_DEV):
        acc = acc + jnp.where(lane_atom == a, full[a * 16 : (a + 1) * 16, :], 0.0)
    for b in range(16):
        block[b] = acc
    copy = pltpu.make_async_copy(block, out.at[:, pl.ds(16, 16), :], sem)
    copy.start()
    copy.wait()


def charge_kernel(start, recv, coupling, shapes, offsets, core, down, up, matrices):
    total = recv[0]
    for b in range(1, 16):
        total = total + recv[b]
    matrix = total[16:32]
    matrices[...] = matrix
    per_lane = jnp.concatenate(
        [jnp.sum(coupling[l] * matrix, axis=0, keepdims=True) for l in range(NL)], axis=0
    )
    atom = lax.broadcasted_iota(jnp.int32, (ATOM_DEV, LANES), 0)
    lane_atom = lax.broadcasted_iota(jnp.int32, (ATOM_DEV, LANES), 1) // 16
    pick = (atom == lane_atom).astype(F32)
    charges = lax.dot_general(
        pick, per_lane, (((1,), (1,)), ((), ())), precision=HIGHEST, preferred_element_type=F32
    )
    comp = jnp.zeros((ATOM_DEV, SPHERE), F32)
    for l in range(NL):
        comp = comp + charges[:, l : l + 1] * shapes[l]
    c1 = comp.astype(BF16).astype(F32)
    c2 = (comp - c1).astype(BF16).astype(F32)
    c3 = comp - c1 - c2
    plane = offsets[...] >> 12
    column = (offsets[...] & (PLANE - 1)) - start[0]
    row = lax.broadcasted_iota(jnp.int32, (24, SPHERE), 0)
    target = jnp.where(row < 8, row + HALO, jnp.where(row < 16, row - 11, row - 3))
    col = lax.broadcasted_iota(jnp.int32, (256, SPHERE), 0)
    acc = jnp.zeros((80, 256), F32)
    for a in range(ATOM_DEV):
        here = target == plane[a : a + 1, :]
        left = jnp.concatenate(
            [jnp.where(here, c[a : a + 1, :], 0.0) for c in (c1, c2, c3)]
            + [jnp.zeros((8, SPHERE), F32)],
            axis=0,
        ).astype(BF16)
        right = jnp.where(col == column[a : a + 1, :], 1.0, 0.0).astype(BF16)
        acc = acc + lax.dot_general(
            left, right, (((1,), (1,)), ((), ())), preferred_element_type=F32
        )
    placed = acc[0:24] + acc[24:48] + acc[48:72]
    core[...] = placed[0:8] + jnp.concatenate([total[0:8], total[8:16]], axis=1)
    down[...] = placed[8:16]
    up[...] = placed[16:24]


def shape(*dims):
    return jax.ShapeDtypeStruct(dims, F32)


def local(orbitals, occupations, projectors, shapes, coupling, sphere_offsets, sphere_sizes):
    slabs = lax.axis_size("slab")
    to_next = [(i, (i + 1) % slabs) for i in range(slabs)]
    to_prev = [((i + 1) % slabs, i) for i in range(slabs)]
    grid_values = orbitals.reshape(BANDS * CZ, PLANE)
    table = pl.pallas_call(
        table_kernel,
        out_shape=shape(PLANE, LANES),
        in_specs=[VM],
        out_specs=VM,
        compiler_params=params(),
        cost_estimate=pl.CostEstimate(flops=0, bytes_accessed=8 * 2**20, transcendentals=0),
        name="grid_table",
    )(grid_values)
    pay, lists = pl.pallas_call(
        sort_kernel,
        out_shape=(
            shape(SORTED + 2 * LIST, LANES),
            jax.ShapeDtypeStruct((LIST, LANES), jnp.int32),
        ),
        in_specs=[ANY] * 3,
        out_specs=(VM, VM),
        scratch_shapes=[
            pltpu.SMEM((ATOM_DEV,), jnp.int32),
            pltpu.VMEM((ATOM_DEV, SPHERE), jnp.int32),
            pltpu.VMEM((NI, ATOM_DEV, SPHERE), F32),
            pltpu.SemaphoreType.DMA((3,)),
        ],
        compiler_params=params(58 * 2**20),
        cost_estimate=pl.CostEstimate(flops=10**9, bytes_accessed=8 * 2**20, transcendentals=0),
        name="sort_points",
    )(sphere_sizes, sphere_offsets, projectors.transpose(1, 0, 2))
    pay_lo = lax.ppermute(pay, "slab", to_next)
    pay_hi = lax.ppermute(pay, "slab", to_prev)

    own_list = lists.reshape(-1)
    scratch = [pltpu.VMEM((ATOM_DEV * SPHERE, LANES), F32)]
    q_early = pl.pallas_call(
        early_kernel,
        out_shape=shape(BANDS, LANES),
        in_specs=[SM, VM, VM],
        out_specs=VM,
        scratch_shapes=scratch,
        compiler_params=params(),
        cost_estimate=pl.CostEstimate(flops=10**9, bytes_accessed=8 * 2**20, transcendentals=0),
        name="own_points_early",
    )(own_list, table, pay)

    q_lo, q_hi = pl.pallas_call(
        side_kernel,
        out_shape=(shape(BANDS, LANES), shape(BANDS, LANES)),
        in_specs=[SM, SM, VM, VM, VM],
        out_specs=(VM, VM),
        scratch_shapes=[pltpu.VMEM((ATOM_DEV * SPHERE, LANES), F32)],
        compiler_params=params(),
        name="side_points",
    )(
        words_of(pay_lo),
        words_of(pay_hi),
        table,
        pay_lo,
        pay_hi,
    )
    back_hi = lax.ppermute(q_lo, "slab", to_prev)
    back_lo = lax.ppermute(q_hi, "slab", to_next)

    packed, q_late = pl.pallas_call(
        late_kernel,
        out_shape=(shape(16, 32, LANES), shape(BANDS, LANES)),
        in_specs=[SM, SM, VM, VM, VM, ANY],
        out_specs=(VM, VM),
        scratch_shapes=scratch,
        compiler_params=params(),
        cost_estimate=pl.CostEstimate(flops=10**9, bytes_accessed=8 * 2**20, transcendentals=0),
        name="own_points_late",
    )(own_list, occupations, grid_values, table, pay, q_lo)

    packed = pl.pallas_call(
        matrix_kernel,
        out_shape=shape(16, 32, LANES),
        in_specs=[VM] * 5 + [ANY],
        out_specs=ANY,
        scratch_shapes=[pltpu.VMEM((16, 16, LANES), F32), pltpu.SemaphoreType.DMA],
        input_output_aliases={5: 0},
        compiler_params=params(),
        name="partial_matrices",
    )(
        q_early,
        q_late,
        back_hi,
        back_lo,
        jnp.broadcast_to(occupations[:, None], (BANDS, LANES)),
        packed,
    )
    recv = lax.all_to_all(packed, "band", 0, 0)

    coupling_lanes = jnp.tile(jnp.pad(coupling, ((0, 0), (0, 3), (0, 3))), (1, 1, ATOM_DEV))
    live = jnp.arange(SPHERE, dtype=jnp.int32)[None, :] < sphere_sizes[:, None]
    shapes_live = jnp.where(live[:, None, :], shapes, 0.0).transpose(1, 0, 2)
    width = PLANE // lax.axis_size("band")
    start = (lax.axis_index("band") * width).astype(jnp.int32).reshape(1)
    core, down, up, matrices = pl.pallas_call(
        charge_kernel,
        out_shape=(shape(CZ, 256), shape(CZ, 256), shape(CZ, 256), shape(16, LANES)),
        in_specs=[SM, VM, VM, VM, VM],
        out_specs=(VM, VM, VM, VM),
        compiler_params=params(),
        name="charges",
    )(start, recv, coupling_lanes, shapes_live, sphere_offsets)
    from_above = lax.ppermute(down, "slab", to_prev)
    from_below = lax.ppermute(up, "slab", to_next)
    density = core + from_above + from_below
    density_matrices = matrices.reshape(16, ATOM_DEV, 16)[:NI, :, :NI].transpose(1, 0, 2)
    return (density, density_matrices)


def solution(mesh):
    placed = (
        P("band", "slab", None),
        P("band"),
        P("slab", None, None),
        P("slab", None, None),
        P(),
        P("slab", None),
        P("slab"),
    )
    return jax.shard_map(
        local,
        mesh=mesh,
        in_specs=placed,
        out_specs=(P("slab", "band"), P("slab", None, None)),
        check_vma=False,
    )
```

```python
import jax
import jax.numpy as jnp
from jax import lax
from jax.experimental import pallas as pl
from jax.experimental.pallas import tpu as pltpu
from jax.sharding import PartitionSpec as P

HALO = 5
PLANE = 4096
CZ = 8
ATOM_DEV = 8
SPHERE = 512
NI = 13
NL = 9
BANDS = 16
LANES = 128
TILES = SPHERE // LANES
WORDS = SPHERE // 2
SORTED = TILES * ATOM_DEV * 16
LIST = WORDS // LANES * ATOM_DEV + ATOM_DEV
HIGHEST = lax.Precision.HIGHEST
F32 = jnp.float32
BF16 = jnp.bfloat16

VM = pl.BlockSpec(memory_space=pltpu.VMEM)
SM = pl.BlockSpec(memory_space=pltpu.SMEM)
ANY = pl.BlockSpec(memory_space=pl.ANY)


def params(limit=48 * 2**20):
    return pltpu.CompilerParams(vmem_limit_bytes=limit)


def gather_rows(points, atom, first, last, step, table, rows):
    base = atom * SPHERE

    def body(s, carry):
        i = pl.multiple_of(s * step, step)
        at = (i >> 7) * (ATOM_DEV * LANES) + atom * LANES + (i & (LANES - 1))
        for u in range(step):
            word = points[at + u]
            rows[pl.ds(base + i + u, 1), :] = table[pl.ds(word & (PLANE - 1), 1), :]
            rows[pl.ds(base + WORDS + i + u, 1), :] = table[pl.ds(word >> 12, 1), :]
        return carry

    lax.fori_loop(first, last, body, 0)


def counts(points, atom):
    at = WORDS * ATOM_DEV + atom * LANES
    return points[at], points[at + LANES - 1]


def project(pay, rows, shift, planes, tiles, atoms=range(ATOM_DEV)):
    width = len(tiles) * LANES
    span = len(planes) * 16
    lane_plane = lax.broadcasted_iota(jnp.int32, (16, LANES), 1) % CZ
    sub = lax.broadcasted_iota(jnp.int32, (16, width), 0)
    parts = []
    for a in range(ATOM_DEV):
        if a not in atoms:
            parts.append(jnp.zeros((16, LANES), F32))
            continue
        block = jnp.concatenate(
            [pay[(a * TILES + t) * 16 : (a * TILES + t + 1) * 16, :] for t in tiles], axis=1
        )
        plane = block[15:16, :].astype(jnp.int32) + shift
        proj = jnp.where(sub < NI, block, 0.0)
        high = proj.astype(BF16).astype(F32)
        low = proj - high
        pieces = []
        for piece in (high, low):
            for z in planes:
                pieces.append(jnp.where(plane == z, piece, 0.0))
        left = jnp.concatenate(pieces, axis=0).astype(BF16)
        gathered = jnp.concatenate(
            [rows[a * SPHERE + t * LANES : a * SPHERE + (t + 1) * LANES, :] for t in tiles], axis=0
        )
        g_high = gathered.astype(BF16)
        g_low = (gathered - g_high.astype(F32)).astype(BF16)
        first = jnp.dot(left, g_high, preferred_element_type=F32)
        second = jnp.dot(left[:span], g_low, preferred_element_type=F32)
        total = first[:span] + first[span:] + second
        acc = jnp.zeros((16, LANES), F32)
        for k, z in enumerate(planes):
            acc = acc + jnp.where(lane_plane == z, total[k * 16 : (k + 1) * 16, :], 0.0)
        parts.append(acc)
    summed = jnp.concatenate(parts, axis=0)
    band = lax.broadcasted_iota(jnp.int32, (BANDS, LANES), 0)
    lane_band = lax.broadcasted_iota(jnp.int32, (BANDS, LANES), 1) // CZ
    pick = (band == lane_band).astype(F32)
    return lax.dot_general(
        pick, summed, (((1,), (1,)), ((), ())), precision=HIGHEST, preferred_element_type=F32
    )


def table_kernel(x, table):
    for c in range(PLANE // LANES):
        cols = slice(c * LANES, (c + 1) * LANES)
        table[cols, :] = x[:, cols].T


def sort_kernel(
    sizes_in, offsets_in, projectors_in, pay, lists, sizes, offsets, projectors, sems
):
    pairs = ((sizes_in, sizes), (offsets_in, offsets), (projectors_in, projectors))
    copies = [pltpu.make_async_copy(a, b, sems.at[k]) for k, (a, b) in enumerate(pairs)]
    for copy in copies:
        copy.start()
    before = lax.broadcasted_iota(jnp.int32, (SPHERE, SPHERE), 0)
    after = lax.broadcasted_iota(jnp.int32, (SPHERE, SPHERE), 1)
    until = jnp.where(before <= after, 1.0, 0.0).astype(BF16)
    sub = lax.broadcasted_iota(jnp.int32, (ATOM_DEV, SPHERE), 0)
    lane = lax.broadcasted_iota(jnp.int32, (ATOM_DEV, SPHERE), 1)
    copies[0].wait()
    copies[1].wait()
    size = jnp.zeros((ATOM_DEV, SPHERE), jnp.int32)
    for a in range(ATOM_DEV):
        size = jnp.where(sub == a, sizes[a], size)
    live = lane < size
    off = offsets[...]
    plane = off >> 12
    point = off & (PLANE - 1)
    below = live & (plane < HALO)
    above = live & (plane >= HALO + CZ)
    own = live & (plane >= HALO) & (plane < HALO + CZ)
    flags = jnp.concatenate(
        [jnp.where(m, 1.0, 0.0) for m in (below, own, above)] + [jnp.zeros((8, SPHERE), F32)],
        axis=0,
    ).astype(BF16)
    rank = jnp.dot(flags, until, preferred_element_type=F32).astype(jnp.int32)
    n_below = jnp.max(rank[0:8], axis=1, keepdims=True)
    n_own = jnp.max(rank[8:16], axis=1, keepdims=True)
    n_above = jnp.max(rank[16:24], axis=1, keepdims=True)
    place = jnp.where(
        below,
        rank[0:8] - 1,
        jnp.where(own, n_below + rank[8:16] - 1, SPHERE - rank[16:24]),
    )
    place = jnp.where(live, (place >> 1) + (place & 1) * WORDS, -1)
    copies[2].wait()
    table = jnp.concatenate(
        [
            projectors[...],
            (point >> 6).astype(F32)[None],
            (point & 63).astype(F32)[None],
            plane.astype(F32)[None],
        ],
        axis=0,
    )
    table = jnp.transpose(table, (1, 0, 2))
    points = []
    for a in range(ATOM_DEV):
        high = table[a].astype(BF16)
        low = (table[a] - high.astype(F32)).astype(BF16)
        move = jnp.where(before == place[a : a + 1, :], 1.0, 0.0).astype(BF16)
        moved = lax.dot_general(
            jnp.concatenate([high, low], axis=0),
            move,
            (((1,), (1,)), ((), ())),
            preferred_element_type=F32,
        )
        moved = moved[0:16] + moved[16:32]
        first = a * TILES * 16
        for t in range(TILES):
            pay[first + t * 16 : first + (t + 1) * 16, :] = moved[:, t * LANES : (t + 1) * LANES]
        points.append(moved[13:14] * 64.0 + moved[14:15])
    points = jnp.concatenate(points, axis=0)
    words = points[:, :WORDS] + points[:, WORDS:] * float(PLANE)
    for t in range(WORDS // LANES):
        at = t * ATOM_DEV
        lists[at : at + ATOM_DEV, :] = words[:, t * LANES : (t + 1) * LANES].astype(jnp.int32)
        for start, shift in ((SORTED, 0), (SORTED + LIST, WORDS)):
            part = points[:, shift + t * LANES : shift + (t + 1) * LANES]
            pay[start + at : start + at + ATOM_DEV, :] = part
    at = LIST - ATOM_DEV
    lead = lane[:, :LANES] < LANES // 2
    pay[SORTED + at : SORTED + LIST, :] = jnp.where(lead, n_below, n_above).astype(F32)
    pay[SORTED + LIST + at : SORTED + 2 * LIST, :] = jnp.zeros((ATOM_DEV, LANES), F32)
    lists[at:LIST, :] = jnp.where(lead, n_below, n_below + n_own)


def words_of(pay):
    words = pay[SORTED : SORTED + LIST] + pay[SORTED + LIST :] * float(PLANE)
    return words.astype(jnp.int32).reshape(-1)


def own_points(atoms, lists, table, pay, rows):
    rows[...] = jnp.zeros_like(rows)
    step = 16
    for a in atoms:
        begin, end = counts(lists, a)
        first = begin // (2 * step)
        last = (end + (2 * step - 1)) // (2 * step)
        gather_rows(lists, a, first, last, step, table, rows)
    return project(pay, rows, -HALO, range(CZ), range(TILES), atoms)


def own_kernel(lists, table, pay, q, rows):
    q[...] = own_points(range(ATOM_DEV), lists, table, pay, rows)


def pseudo_kernel(sizes, occ, x, offsets, shapes, after, packed, place):
    del after
    for c in range(PLANE // LANES):
        cols = slice(c * LANES, (c + 1) * LANES)
        acc = jnp.zeros((CZ, LANES), F32)
        for n in range(BANDS):
            v = x[n * CZ : (n + 1) * CZ, cols]
            acc = acc + occ[n] * (v * v)
        packed[c // 2, (c % 2) * CZ : (c % 2 + 1) * CZ, :] = acc
    sub = lax.broadcasted_iota(jnp.int32, (ATOM_DEV, SPHERE), 0)
    lane = lax.broadcasted_iota(jnp.int32, (ATOM_DEV, SPHERE), 1)
    size = jnp.zeros((ATOM_DEV, SPHERE), jnp.int32)
    for a in range(ATOM_DEV):
        size = jnp.where(sub == a, sizes[a], size)
    for l in range(NL):
        place[l] = jnp.where(lane < size, shapes[l], 0.0)
    place[NL] = offsets[...].astype(F32)


def side_kernel(list_lo, list_hi, table, pay_lo, pay_hi, q, q_lo, q_hi, to_prev, to_next, rows):
    rows[...] = jnp.zeros_like(rows)
    step = 8
    most = jnp.int32(0)
    for a in range(ATOM_DEV):
        most = jnp.maximum(most, jnp.maximum(counts(list_lo, a)[1], counts(list_hi, a)[0]))

    def from_below():
        for a in range(ATOM_DEV):
            first = (SPHERE - counts(list_lo, a)[1]) // (2 * step)
            gather_rows(list_lo, a, first, WORDS // step, step, table, rows)

    def from_above():
        for a in range(ATOM_DEV):
            last = (counts(list_hi, a)[0] + (2 * step - 1)) // (2 * step)
            gather_rows(list_hi, a, 0, last, step, table, rows)

    low, high = range(HALO), range(CZ - HALO, CZ)

    @pl.when(most <= WORDS)
    def _():
        from_below()
        from_above()
        q_lo[...] = project(pay_lo, rows, -HALO - CZ, low, (1, 3))
        q_hi[...] = project(pay_hi, rows, CZ - HALO, high, (0, 2))

    @pl.when(most > WORDS)
    def _():
        from_below()
        q_lo[...] = project(pay_lo, rows, -HALO - CZ, low, range(TILES))
        from_above()
        q_hi[...] = project(pay_hi, rows, CZ - HALO, high, range(TILES))

    to_prev[0:16, :] = q[...]
    to_prev[16:32, :] = q_lo[...]
    to_next[0:16, :] = q[...]
    to_next[16:32, :] = q_hi[...]


def matrix_kernel(
    q, q_lo, q_hi, prev, following, prev2, following2, occ, coupling, packed, out, block, sem
):
    del packed
    lane_atom = lax.broadcasted_iota(jnp.int32, (16, LANES), 1) // 16
    matrices = []
    for proj in (
        q[...] + prev[16:32, :] + following[16:32, :],
        q_lo[...] + prev[0:16, :] + prev2[...],
        q_hi[...] + following[0:16, :] + following2[...],
    ):
        full = lax.dot_general(
            proj * occ[...],
            proj,
            (((0,), (0,)), ((), ())),
            precision=HIGHEST,
            preferred_element_type=F32,
        )
        acc = jnp.zeros((16, LANES), F32)
        for a in range(ATOM_DEV):
            acc = acc + jnp.where(lane_atom == a, full[a * 16 : (a + 1) * 16, :], 0.0)
        matrices.append(acc)
    lanes = jnp.concatenate([per_lane(coupling, m) for m in matrices[1:]], axis=1)
    row = lax.broadcasted_iota(jnp.int32, (2 * LANES, LANES), 0)
    col = lax.broadcasted_iota(jnp.int32, (2 * LANES, LANES), 1)
    column = (row % LANES) // 16 * 16 + NI + row // LANES
    spread = jnp.where(col == column, 1.0, 0.0)
    acc = matrices[0] + jnp.dot(lanes, spread, precision=HIGHEST, preferred_element_type=F32)
    for b in range(16):
        block[b] = acc
    copy = pltpu.make_async_copy(block, out.at[:, pl.ds(16, 16), :], sem)
    copy.start()
    copy.wait()


def per_lane(coupling, matrix):
    rows = [jnp.sum(coupling[l] * matrix, axis=0, keepdims=True) for l in range(NL)]
    return jnp.concatenate(rows + [jnp.zeros((16 - NL, LANES), F32)], axis=0)


def charge_kernel(start, recv, coupling, place, place_lo, place_hi, density, matrices):
    total = recv[0]
    for b in range(1, 16):
        total = total + recv[b]
    matrix = total[16:32]
    matrices[...] = matrix
    atom = lax.broadcasted_iota(jnp.int32, (ATOM_DEV, LANES), 0)
    lane = lax.broadcasted_iota(jnp.int32, (ATOM_DEV, LANES), 1)
    row = lax.broadcasted_iota(jnp.int32, (CZ, SPHERE), 0)
    col = lax.broadcasted_iota(jnp.int32, (256, SPHERE), 0)
    acc = jnp.zeros((32, 256), F32)
    for terms, pick, here, shift in (
        (per_lane(coupling, matrix), lane // 16 == atom, place, -HALO),
        (matrix, lane == atom * 16 + NI, place_lo, -HALO - CZ),
        (matrix, lane == atom * 16 + NI + 1, place_hi, CZ - HALO),
    ):
        charges = lax.dot_general(
            pick.astype(F32),
            terms,
            (((1,), (1,)), ((), ())),
            precision=HIGHEST,
            preferred_element_type=F32,
        )
        comp = jnp.zeros((ATOM_DEV, SPHERE), F32)
        for l in range(NL):
            comp = comp + charges[:, l : l + 1] * here[l]
        c1 = comp.astype(BF16).astype(F32)
        c2 = (comp - c1).astype(BF16).astype(F32)
        c3 = comp - c1 - c2
        offsets = here[NL].astype(jnp.int32)
        plane = (offsets >> 12) + shift
        column = (offsets & (PLANE - 1)) - start[0]
        for a in range(ATOM_DEV):
            on = row == plane[a : a + 1, :]
            left = jnp.concatenate(
                [jnp.where(on, c[a : a + 1, :], 0.0) for c in (c1, c2, c3)]
                + [jnp.zeros((8, SPHERE), F32)],
                axis=0,
            ).astype(BF16)
            right = jnp.where(col == column[a : a + 1, :], 1.0, 0.0).astype(BF16)
            acc = acc + lax.dot_general(
                left, right, (((1,), (1,)), ((), ())), preferred_element_type=F32
            )
    density[...] = (acc[0:8] + acc[8:16] + acc[16:24]) + jnp.concatenate(
        [total[0:8], total[8:16]], axis=1
    )


def shape(*dims):
    return jax.ShapeDtypeStruct(dims, F32)


def local(orbitals, occupations, projectors, shapes, coupling, sphere_offsets, sphere_sizes):
    slabs = lax.axis_size("slab")
    to_next = [(i, (i + 1) % slabs) for i in range(slabs)]
    to_prev = [((i + 1) % slabs, i) for i in range(slabs)]
    to_next2 = [(i, (i + 2) % slabs) for i in range(slabs)]
    to_prev2 = [((i + 2) % slabs, i) for i in range(slabs)]
    grid_values = orbitals.reshape(BANDS * CZ, PLANE)
    table = pl.pallas_call(
        table_kernel,
        out_shape=shape(PLANE, LANES),
        in_specs=[VM],
        out_specs=VM,
        compiler_params=params(),
        cost_estimate=pl.CostEstimate(flops=0, bytes_accessed=8 * 2**20, transcendentals=0),
        name="grid_table",
    )(grid_values)
    pay, lists = pl.pallas_call(
        sort_kernel,
        out_shape=(
            shape(SORTED + 2 * LIST, LANES),
            jax.ShapeDtypeStruct((LIST, LANES), jnp.int32),
        ),
        in_specs=[ANY] * 3,
        out_specs=(VM, VM),
        scratch_shapes=[
            pltpu.SMEM((ATOM_DEV,), jnp.int32),
            pltpu.VMEM((ATOM_DEV, SPHERE), jnp.int32),
            pltpu.VMEM((NI, ATOM_DEV, SPHERE), F32),
            pltpu.SemaphoreType.DMA((3,)),
        ],
        compiler_params=params(58 * 2**20),
        cost_estimate=pl.CostEstimate(flops=10**9, bytes_accessed=8 * 2**20, transcendentals=0),
        name="sort_points",
    )(sphere_sizes, sphere_offsets, projectors.transpose(1, 0, 2))
    pay_lo = lax.ppermute(pay, "slab", to_next)
    pay_hi = lax.ppermute(pay, "slab", to_prev)

    own_list = lists.reshape(-1)
    scratch = [pltpu.VMEM((ATOM_DEV * SPHERE, LANES), F32)]
    q = pl.pallas_call(
        own_kernel,
        out_shape=shape(BANDS, LANES),
        in_specs=[SM, VM, VM],
        out_specs=VM,
        scratch_shapes=scratch,
        compiler_params=params(),
        cost_estimate=pl.CostEstimate(flops=2 * 10**9, bytes_accessed=8 * 2**20, transcendentals=0),
        name="own_points",
    )(own_list, table, pay)

    q_lo, q_hi, for_prev, for_next = pl.pallas_call(
        side_kernel,
        out_shape=(
            shape(BANDS, LANES),
            shape(BANDS, LANES),
            shape(2 * BANDS, LANES),
            shape(2 * BANDS, LANES),
        ),
        in_specs=[SM, SM, VM, VM, VM, VM],
        out_specs=(VM, VM, VM, VM),
        scratch_shapes=scratch,
        compiler_params=params(),
        name="side_points",
    )(words_of(pay_lo), words_of(pay_hi), table, pay_lo, pay_hi, q)
    prev = lax.ppermute(for_next, "slab", to_next)
    following = lax.ppermute(for_prev, "slab", to_prev)
    prev2 = lax.ppermute(q_hi, "slab", to_next2)
    following2 = lax.ppermute(q_lo, "slab", to_prev2)

    packed, place = pl.pallas_call(
        pseudo_kernel,
        out_shape=(shape(16, 32, LANES), shape(NL + 1, ATOM_DEV, SPHERE)),
        in_specs=[SM, SM, VM, VM, VM, ANY],
        out_specs=(VM, VM),
        compiler_params=params(),
        cost_estimate=pl.CostEstimate(flops=10**8, bytes_accessed=3 * 2**20, transcendentals=0),
        name="pseudo_density",
    )(
        sphere_sizes,
        occupations,
        grid_values,
        sphere_offsets,
        shapes.transpose(1, 0, 2),
        q_lo,
    )
    place_lo = lax.ppermute(place, "slab", to_next)
    place_hi = lax.ppermute(place, "slab", to_prev)

    coupling_lanes = jnp.tile(jnp.pad(coupling, ((0, 0), (0, 3), (0, 3))), (1, 1, ATOM_DEV))
    packed = pl.pallas_call(
        matrix_kernel,
        out_shape=shape(16, 32, LANES),
        in_specs=[VM] * 9 + [ANY],
        out_specs=ANY,
        scratch_shapes=[pltpu.VMEM((16, 16, LANES), F32), pltpu.SemaphoreType.DMA],
        input_output_aliases={9: 0},
        compiler_params=params(),
        name="partial_matrices",
    )(
        q,
        q_lo,
        q_hi,
        prev,
        following,
        prev2,
        following2,
        jnp.broadcast_to(occupations[:, None], (BANDS, LANES)),
        coupling_lanes,
        packed,
    )
    recv = lax.all_to_all(packed, "band", 0, 0)

    width = PLANE // lax.axis_size("band")
    start = (lax.axis_index("band") * width).astype(jnp.int32).reshape(1)
    density, matrices = pl.pallas_call(
        charge_kernel,
        out_shape=(shape(CZ, 256), shape(16, LANES)),
        in_specs=[SM, VM, VM, VM, VM, VM],
        out_specs=(VM, VM),
        compiler_params=params(),
        name="charges",
    )(start, recv, coupling_lanes, place, place_lo, place_hi)
    density_matrices = matrices.reshape(16, ATOM_DEV, 16)[:NI, :, :NI].transpose(1, 0, 2)
    return (density, density_matrices)


def solution(mesh):
    placed = (
        P("band", "slab", None),
        P("band"),
        P("slab", None, None),
        P("slab", None, None),
        P(),
        P("slab", None),
        P("slab"),
    )
    return jax.shard_map(
        local,
        mesh=mesh,
        in_specs=placed,
        out_specs=(P("slab", "band"), P("slab", None, None)),
        check_vma=False,
    )
```

```python
import jax
import jax.numpy as jnp
import numpy as np
from jax import lax
from jax.experimental import pallas as pl
from jax.experimental.pallas import tpu as pltpu
from jax.sharding import PartitionSpec as P

HALO = 5
PLANE = 4096
CZ = 8
ATOM_DEV = 8
SPHERE = 512
NI = 13
NL = 9
BANDS = 16
LANES = 128
EARLY = 6
TILES = SPHERE // LANES
WORDS = SPHERE // 2
SORTED = TILES * ATOM_DEV * 16
LIST = WORDS // LANES * ATOM_DEV + ATOM_DEV
HIGHEST = lax.Precision.HIGHEST
F32 = jnp.float32
BF16 = jnp.bfloat16

VM = pl.BlockSpec(memory_space=pltpu.VMEM)
SM = pl.BlockSpec(memory_space=pltpu.SMEM)
ANY = pl.BlockSpec(memory_space=pl.ANY)


def params(limit=48 * 2**20):
    return pltpu.CompilerParams(vmem_limit_bytes=limit)


def gather_rows(points, atom, first, last, step, table, rows):
    base = atom * SPHERE

    def body(s, carry):
        i = pl.multiple_of(s * step, step)
        at = (i >> 7) * (ATOM_DEV * LANES) + atom * LANES + (i & (LANES - 1))
        for u in range(step):
            word = points[at + u]
            rows[pl.ds(base + i + u, 1), :] = table[pl.ds(word & (PLANE - 1), 1), :]
            rows[pl.ds(base + WORDS + i + u, 1), :] = table[pl.ds(word >> 12, 1), :]
        return carry

    lax.fori_loop(first, last, body, 0)


def counts(points, atom):
    at = WORDS * ATOM_DEV + atom * LANES
    return points[at], points[at + LANES - 1]


def project(pay, rows, shift, planes, tiles, atoms=range(ATOM_DEV)):
    width = len(tiles) * LANES
    span = len(planes) * 16
    lane_plane = lax.broadcasted_iota(jnp.int32, (16, LANES), 1) % CZ
    sub = lax.broadcasted_iota(jnp.int32, (16, width), 0)
    parts = []
    for a in range(ATOM_DEV):
        if a not in atoms:
            parts.append(jnp.zeros((16, LANES), F32))
            continue
        block = jnp.concatenate(
            [pay[(a * TILES + t) * 16 : (a * TILES + t + 1) * 16, :] for t in tiles], axis=1
        )
        plane = block[15:16, :].astype(jnp.int32) + shift
        proj = jnp.where(sub < NI, block, 0.0)
        high = proj.astype(BF16).astype(F32)
        low = proj - high
        pieces = []
        for piece in (high, low):
            for z in planes:
                pieces.append(jnp.where(plane == z, piece, 0.0))
        left = jnp.concatenate(pieces, axis=0).astype(BF16)
        gathered = jnp.concatenate(
            [rows[a * SPHERE + t * LANES : a * SPHERE + (t + 1) * LANES, :] for t in tiles], axis=0
        )
        g_high = gathered.astype(BF16)
        g_low = (gathered - g_high.astype(F32)).astype(BF16)
        both = jnp.concatenate([g_high, g_low], axis=1)
        product = jnp.dot(left, both, preferred_element_type=F32)
        total = product[:span, :LANES] + product[span:, :LANES] + product[:span, LANES:]
        acc = jnp.zeros((16, LANES), F32)
        for k, z in enumerate(planes):
            acc = acc + jnp.where(lane_plane == z, total[k * 16 : (k + 1) * 16, :], 0.0)
        parts.append(acc)
    summed = jnp.concatenate(parts, axis=0)
    band = lax.broadcasted_iota(jnp.int32, (BANDS, LANES), 0)
    lane_band = lax.broadcasted_iota(jnp.int32, (BANDS, LANES), 1) // CZ
    pick = (band == lane_band).astype(F32)
    return lax.dot_general(
        pick, summed, (((1,), (1,)), ((), ())), precision=HIGHEST, preferred_element_type=F32
    )


def table_kernel(x, table):
    for c in range(PLANE // LANES):
        cols = slice(c * LANES, (c + 1) * LANES)
        table[cols, :] = x[:, cols].T


def sort_kernel(
    sizes_in, offsets_in, projectors_in, pay, lists, sizes, offsets, projectors, sems
):
    pairs = ((sizes_in, sizes), (offsets_in, offsets), (projectors_in, projectors))
    copies = [pltpu.make_async_copy(a, b, sems.at[k]) for k, (a, b) in enumerate(pairs)]
    for copy in copies:
        copy.start()
    before = lax.broadcasted_iota(jnp.int32, (SPHERE, SPHERE), 0)
    after = lax.broadcasted_iota(jnp.int32, (SPHERE, SPHERE), 1)
    until = jnp.where(before <= after, 1.0, 0.0).astype(BF16)
    sub = lax.broadcasted_iota(jnp.int32, (ATOM_DEV, SPHERE), 0)
    lane = lax.broadcasted_iota(jnp.int32, (ATOM_DEV, SPHERE), 1)
    copies[0].wait()
    copies[1].wait()
    size = jnp.zeros((ATOM_DEV, SPHERE), jnp.int32)
    for a in range(ATOM_DEV):
        size = jnp.where(sub == a, sizes[a], size)
    live = lane < size
    off = offsets[...]
    plane = off >> 12
    point = off & (PLANE - 1)
    below = live & (plane < HALO)
    above = live & (plane >= HALO + CZ)
    own = live & (plane >= HALO) & (plane < HALO + CZ)
    flags = jnp.concatenate(
        [jnp.where(m, 1.0, 0.0) for m in (below, own, above)] + [jnp.zeros((8, SPHERE), F32)],
        axis=0,
    ).astype(BF16)
    rank = jnp.dot(flags, until, preferred_element_type=F32).astype(jnp.int32)
    n_below = jnp.max(rank[0:8], axis=1, keepdims=True)
    n_own = jnp.max(rank[8:16], axis=1, keepdims=True)
    n_above = jnp.max(rank[16:24], axis=1, keepdims=True)
    place = jnp.where(
        below,
        rank[0:8] - 1,
        jnp.where(own, n_below + rank[8:16] - 1, SPHERE - rank[16:24]),
    )
    place = jnp.where(live, (place >> 1) + (place & 1) * WORDS, -1)
    copies[2].wait()
    table = jnp.concatenate(
        [
            projectors[...],
            (point >> 6).astype(F32)[None],
            (point & 63).astype(F32)[None],
            plane.astype(F32)[None],
        ],
        axis=0,
    )
    table = jnp.transpose(table, (1, 0, 2))
    points = []
    for a in range(ATOM_DEV):
        high = table[a].astype(BF16)
        low = (table[a] - high.astype(F32)).astype(BF16)
        move = jnp.where(before == place[a : a + 1, :], 1.0, 0.0).astype(BF16)
        moved = lax.dot_general(
            jnp.concatenate([high, low], axis=0),
            move,
            (((1,), (1,)), ((), ())),
            preferred_element_type=F32,
        )
        moved = moved[0:16] + moved[16:32]
        first = a * TILES * 16
        for t in range(TILES):
            pay[first + t * 16 : first + (t + 1) * 16, :] = moved[:, t * LANES : (t + 1) * LANES]
        points.append(moved[13:14] * 64.0 + moved[14:15])
    points = jnp.concatenate(points, axis=0)
    words = points[:, :WORDS] + points[:, WORDS:] * float(PLANE)
    for t in range(WORDS // LANES):
        at = t * ATOM_DEV
        lists[at : at + ATOM_DEV, :] = words[:, t * LANES : (t + 1) * LANES].astype(jnp.int32)
        for start, shift in ((SORTED, 0), (SORTED + LIST, WORDS)):
            part = points[:, shift + t * LANES : shift + (t + 1) * LANES]
            pay[start + at : start + at + ATOM_DEV, :] = part
    at = LIST - ATOM_DEV
    lead = lane[:, :LANES] < LANES // 2
    pay[SORTED + at : SORTED + LIST, :] = jnp.where(lead, n_below, n_above).astype(F32)
    pay[SORTED + LIST + at : SORTED + 2 * LIST, :] = jnp.zeros((ATOM_DEV, LANES), F32)
    lists[at:LIST, :] = jnp.where(lead, n_below, n_below + n_own)


def words_of(pay):
    words = pay[SORTED : SORTED + LIST] + pay[SORTED + LIST :] * float(PLANE)
    return words.astype(jnp.int32).reshape(-1)


def own_points(atoms, lists, table, pay, rows):
    rows[...] = jnp.zeros_like(rows)
    step = 16
    for a in atoms:
        begin, end = counts(lists, a)
        first = begin // (2 * step)
        last = (end + (2 * step - 1)) // (2 * step)
        gather_rows(lists, a, first, last, step, table, rows)
    return project(pay, rows, -HALO, range(CZ), range(TILES), atoms)


def early_kernel(lists, table, pay, q, rows):
    q[...] = own_points(range(EARLY), lists, table, pay, rows)


def late_kernel(lists, occ, x, table, pay, after, packed, q, rows):
    del after
    for c in range(PLANE // LANES):
        cols = slice(c * LANES, (c + 1) * LANES)
        acc = jnp.zeros((CZ, LANES), F32)
        for n in range(BANDS):
            v = x[n * CZ : (n + 1) * CZ, cols]
            acc = acc + occ[n] * (v * v)
        packed[c // 2, (c % 2) * CZ : (c % 2 + 1) * CZ, :] = acc
    q[...] = own_points(range(EARLY, ATOM_DEV), lists, table, pay, rows)


def side_kernel(list_lo, list_hi, table, pay_lo, pay_hi, q_lo, q_hi, rows):
    rows[...] = jnp.zeros_like(rows)
    step = 8
    most = jnp.int32(0)
    for a in range(ATOM_DEV):
        most = jnp.maximum(most, jnp.maximum(counts(list_lo, a)[1], counts(list_hi, a)[0]))

    def from_below():
        for a in range(ATOM_DEV):
            first = (SPHERE - counts(list_lo, a)[1]) // (2 * step)
            gather_rows(list_lo, a, first, WORDS // step, step, table, rows)

    def from_above():
        for a in range(ATOM_DEV):
            last = (counts(list_hi, a)[0] + (2 * step - 1)) // (2 * step)
            gather_rows(list_hi, a, 0, last, step, table, rows)

    low, high = range(HALO), range(CZ - HALO, CZ)

    @pl.when(most <= WORDS)
    def _():
        from_below()
        from_above()
        q_lo[...] = project(pay_lo, rows, -HALO - CZ, low, (1, 3))
        q_hi[...] = project(pay_hi, rows, CZ - HALO, high, (0, 2))

    @pl.when(most > WORDS)
    def _():
        from_below()
        q_lo[...] = project(pay_lo, rows, -HALO - CZ, low, range(TILES))
        from_above()
        q_hi[...] = project(pay_hi, rows, CZ - HALO, high, range(TILES))


def matrix_kernel(q0, q1, q2, q3, occ, packed, out, block, sem):
    del packed
    proj = q0[...] + q1[...] + q2[...] + q3[...]
    weighted = proj * occ[...]
    full = lax.dot_general(
        weighted, proj, (((0,), (0,)), ((), ())), precision=HIGHEST, preferred_element_type=F32
    )
    lane_atom = lax.broadcasted_iota(jnp.int32, (16, LANES), 1) // 16
    acc = jnp.zeros((16, LANES), F32)
    for a in range(ATOM_DEV):
        acc = acc + jnp.where(lane_atom == a, full[a * 16 : (a + 1) * 16, :], 0.0)
    i = lax.broadcasted_iota(jnp.int32, (8, LANES), 0)
    j = lax.broadcasted_iota(jnp.int32, (8, LANES), 1) % 16
    corner = pltpu.roll(pltpu.roll(acc[8:16], 1, 0), LANES - 8, 1)
    half = jnp.where(j < i, corner, acc[0:8])
    for b in range(16):
        block[b] = half
    copy = pltpu.make_async_copy(block, out.at[:, pl.ds(16, 8), :], sem)
    copy.start()
    copy.wait()


def charge_kernel(start, recv, coupling, shapes, offsets, core, down, up, matrices):
    total = recv[0]
    for b in range(1, 16):
        total = total + recv[b]
    matrix = total[16:24]
    matrices[...] = matrix
    per_lane = jnp.concatenate(
        [jnp.sum(coupling[l] * matrix, axis=0, keepdims=True) for l in range(NL)], axis=0
    )
    atom = lax.broadcasted_iota(jnp.int32, (ATOM_DEV, LANES), 0)
    lane_atom = lax.broadcasted_iota(jnp.int32, (ATOM_DEV, LANES), 1) // 16
    pick = (atom == lane_atom).astype(F32)
    charges = lax.dot_general(
        pick, per_lane, (((1,), (1,)), ((), ())), precision=HIGHEST, preferred_element_type=F32
    )
    comp = jnp.zeros((ATOM_DEV, SPHERE), F32)
    for l in range(NL):
        comp = comp + charges[:, l : l + 1] * shapes[l]
    c1 = comp.astype(BF16).astype(F32)
    c2 = (comp - c1).astype(BF16).astype(F32)
    c3 = comp - c1 - c2
    plane = offsets[...] >> 12
    column = (offsets[...] & (PLANE - 1)) - start[0]
    row = lax.broadcasted_iota(jnp.int32, (24, SPHERE), 0)
    target = jnp.where(row < 8, row + HALO, jnp.where(row < 16, row - 11, row - 3))
    col = lax.broadcasted_iota(jnp.int32, (256, SPHERE), 0)
    acc = jnp.zeros((80, 256), F32)
    for a in range(ATOM_DEV):
        here = target == plane[a : a + 1, :]
        left = jnp.concatenate(
            [jnp.where(here, c[a : a + 1, :], 0.0) for c in (c1, c2, c3)]
            + [jnp.zeros((8, SPHERE), F32)],
            axis=0,
        ).astype(BF16)
        right = jnp.where(col == column[a : a + 1, :], 1.0, 0.0).astype(BF16)
        acc = acc + lax.dot_general(
            left, right, (((1,), (1,)), ((), ())), preferred_element_type=F32
        )
    placed = acc[0:24] + acc[24:48] + acc[48:72]
    core[...] = placed[0:8] + jnp.concatenate([total[0:8], total[8:16]], axis=1)
    down[...] = placed[8:16]
    up[...] = placed[16:24]


def shape(*dims):
    return jax.ShapeDtypeStruct(dims, F32)


def local(orbitals, occupations, projectors, shapes, coupling, sphere_offsets, sphere_sizes):
    slabs = lax.axis_size("slab")
    to_next = [(i, (i + 1) % slabs) for i in range(slabs)]
    to_prev = [((i + 1) % slabs, i) for i in range(slabs)]
    grid_values = orbitals.reshape(BANDS * CZ, PLANE)
    table = pl.pallas_call(
        table_kernel,
        out_shape=shape(PLANE, LANES),
        in_specs=[VM],
        out_specs=VM,
        compiler_params=params(),
        cost_estimate=pl.CostEstimate(flops=0, bytes_accessed=8 * 2**20, transcendentals=0),
        name="grid_table",
    )(grid_values)
    pay, lists = pl.pallas_call(
        sort_kernel,
        out_shape=(
            shape(SORTED + 2 * LIST, LANES),
            jax.ShapeDtypeStruct((LIST, LANES), jnp.int32),
        ),
        in_specs=[ANY] * 3,
        out_specs=(VM, VM),
        scratch_shapes=[
            pltpu.SMEM((ATOM_DEV,), jnp.int32),
            pltpu.VMEM((ATOM_DEV, SPHERE), jnp.int32),
            pltpu.VMEM((NI, ATOM_DEV, SPHERE), F32),
            pltpu.SemaphoreType.DMA((3,)),
        ],
        compiler_params=params(58 * 2**20),
        cost_estimate=pl.CostEstimate(flops=10**9, bytes_accessed=8 * 2**20, transcendentals=0),
        name="sort_points",
    )(sphere_sizes, sphere_offsets, projectors.transpose(1, 0, 2))
    pay_lo = lax.ppermute(pay, "slab", to_next)
    pay_hi = lax.ppermute(pay, "slab", to_prev)

    own_list = lists.reshape(-1)
    scratch = [pltpu.VMEM((ATOM_DEV * SPHERE, LANES), F32)]
    q_early = pl.pallas_call(
        early_kernel,
        out_shape=shape(BANDS, LANES),
        in_specs=[SM, VM, VM],
        out_specs=VM,
        scratch_shapes=scratch,
        compiler_params=params(),
        cost_estimate=pl.CostEstimate(flops=10**9, bytes_accessed=8 * 2**20, transcendentals=0),
        name="own_points_early",
    )(own_list, table, pay)

    q_lo, q_hi = pl.pallas_call(
        side_kernel,
        out_shape=(shape(BANDS, LANES), shape(BANDS, LANES)),
        in_specs=[SM, SM, VM, VM, VM],
        out_specs=(VM, VM),
        scratch_shapes=[pltpu.VMEM((ATOM_DEV * SPHERE, LANES), F32)],
        compiler_params=params(),
        name="side_points",
    )(
        words_of(pay_lo),
        words_of(pay_hi),
        table,
        pay_lo,
        pay_hi,
    )
    back_hi = lax.ppermute(q_lo, "slab", to_prev)
    back_lo = lax.ppermute(q_hi, "slab", to_next)

    packed, q_late = pl.pallas_call(
        late_kernel,
        out_shape=(shape(16, 24, LANES), shape(BANDS, LANES)),
        in_specs=[SM, SM, VM, VM, VM, ANY],
        out_specs=(VM, VM),
        scratch_shapes=scratch,
        compiler_params=params(),
        cost_estimate=pl.CostEstimate(flops=10**9, bytes_accessed=8 * 2**20, transcendentals=0),
        name="own_points_late",
    )(own_list, occupations, grid_values, table, pay, q_lo)

    packed = pl.pallas_call(
        matrix_kernel,
        out_shape=shape(16, 24, LANES),
        in_specs=[VM] * 5 + [ANY],
        out_specs=ANY,
        scratch_shapes=[pltpu.VMEM((16, 8, LANES), F32), pltpu.SemaphoreType.DMA],
        input_output_aliases={5: 0},
        compiler_params=params(),
        name="partial_matrices",
    )(
        q_early,
        q_late,
        back_hi,
        back_lo,
        jnp.broadcast_to(occupations[:, None], (BANDS, LANES)),
        packed,
    )
    packed, coupling = lax.optimization_barrier((packed, coupling))
    recv = lax.all_to_all(packed, "band", 0, 0)

    unpack = np.zeros((8, 16, NI, NI), np.float32)
    for i in range(NI):
        for j in range(NI):
            r, c = min(i, j), max(i, j)
            p, q = (r, c) if r < 8 else (c - 7, r - 8)
            unpack[p, q, i, j] = 1.0
    coupling_packed = jnp.einsum("lij,pqij->lpq", coupling, unpack, precision=HIGHEST)
    coupling_lanes = jnp.tile(coupling_packed, (1, 1, ATOM_DEV))
    live = jnp.arange(SPHERE, dtype=jnp.int32)[None, :] < sphere_sizes[:, None]
    shapes_live = jnp.where(live[:, None, :], shapes, 0.0).transpose(1, 0, 2)
    width = PLANE // lax.axis_size("band")
    start = (lax.axis_index("band") * width).astype(jnp.int32).reshape(1)
    core, down, up, matrices = pl.pallas_call(
        charge_kernel,
        out_shape=(shape(CZ, 256), shape(CZ, 256), shape(CZ, 256), shape(8, LANES)),
        in_specs=[SM, VM, VM, VM, VM],
        out_specs=(VM, VM, VM, VM),
        compiler_params=params(),
        name="charges",
    )(start, recv, coupling_lanes, shapes_live, sphere_offsets)
    from_above = lax.ppermute(down, "slab", to_prev)
    from_below = lax.ppermute(up, "slab", to_next)
    density = core + from_above + from_below
    density_matrices = jnp.einsum(
        "paq,pqij->aij", matrices.reshape(8, ATOM_DEV, 16), unpack, precision=HIGHEST
    )
    return (density, density_matrices)


def solution(mesh):
    placed = (
        P("band", "slab", None),
        P("band"),
        P("slab", None, None),
        P("slab", None, None),
        P(),
        P("slab", None),
        P("slab"),
    )
    return jax.shard_map(
        local,
        mesh=mesh,
        in_specs=placed,
        out_specs=(P("slab", "band"), P("slab", None, None)),
        check_vma=False,
    )
```

```python
import jax
import jax.numpy as jnp
import numpy as np
from jax import lax
from jax.experimental import pallas as pl
from jax.experimental.pallas import tpu as pltpu
from jax.sharding import PartitionSpec as P

HALO = 5
PLANE = 4096
CZ = 8
ATOM_DEV = 8
SPHERE = 512
NI = 13
NL = 9
BANDS = 16
LANES = 128
EARLY = 5
TILES = SPHERE // LANES
WORDS = SPHERE // 2
SORTED = TILES * ATOM_DEV * 16
LIST = WORDS // LANES * ATOM_DEV + ATOM_DEV
HIGHEST = lax.Precision.HIGHEST
F32 = jnp.float32
BF16 = jnp.bfloat16

VM = pl.BlockSpec(memory_space=pltpu.VMEM)
SM = pl.BlockSpec(memory_space=pltpu.SMEM)
ANY = pl.BlockSpec(memory_space=pl.ANY)


def params(limit=48 * 2**20):
    return pltpu.CompilerParams(vmem_limit_bytes=limit)


def gather_rows(points, atom, first, last, step, table, rows):
    base = atom * SPHERE

    def body(s, carry):
        i = pl.multiple_of(s * step, step)
        at = (i >> 7) * (ATOM_DEV * LANES) + atom * LANES + (i & (LANES - 1))
        for u in range(step):
            word = points[at + u]
            rows[pl.ds(base + i + u, 1), :] = table[pl.ds(word & (PLANE - 1), 1), :]
            rows[pl.ds(base + WORDS + i + u, 1), :] = table[pl.ds(word >> 12, 1), :]
        return carry

    lax.fori_loop(first, last, body, 0)


def counts(points, atom):
    at = WORDS * ATOM_DEV + atom * LANES
    return points[at], points[at + LANES - 1]


def project(pay, rows, shift, planes, tiles, atoms=range(ATOM_DEV)):
    width = len(tiles) * LANES
    span = len(planes) * 16
    lane_plane = lax.broadcasted_iota(jnp.int32, (16, LANES), 1) % CZ
    sub = lax.broadcasted_iota(jnp.int32, (16, width), 0)
    parts = []
    for a in range(ATOM_DEV):
        if a not in atoms:
            parts.append(jnp.zeros((16, LANES), F32))
            continue
        block = jnp.concatenate(
            [pay[(a * TILES + t) * 16 : (a * TILES + t + 1) * 16, :] for t in tiles], axis=1
        )
        plane = block[15:16, :].astype(jnp.int32) + shift
        proj = jnp.where(sub < NI, block, 0.0)
        high = proj.astype(BF16).astype(F32)
        low = proj - high
        pieces = []
        for piece in (high, low):
            for z in planes:
                pieces.append(jnp.where(plane == z, piece, 0.0))
        left = jnp.concatenate(pieces, axis=0).astype(BF16)
        gathered = jnp.concatenate(
            [rows[a * SPHERE + t * LANES : a * SPHERE + (t + 1) * LANES, :] for t in tiles], axis=0
        )
        g_high = gathered.astype(BF16)
        g_low = (gathered - g_high.astype(F32)).astype(BF16)
        both = jnp.concatenate([g_high, g_low], axis=1)
        product = jnp.dot(left, both, preferred_element_type=F32)
        total = product[:span, :LANES] + product[span:, :LANES] + product[:span, LANES:]
        acc = jnp.zeros((16, LANES), F32)
        for k, z in enumerate(planes):
            acc = acc + jnp.where(lane_plane == z, total[k * 16 : (k + 1) * 16, :], 0.0)
        parts.append(acc)
    summed = jnp.concatenate(parts, axis=0)
    band = lax.broadcasted_iota(jnp.int32, (BANDS, LANES), 0)
    lane_band = lax.broadcasted_iota(jnp.int32, (BANDS, LANES), 1) // CZ
    pick = (band == lane_band).astype(F32)
    return lax.dot_general(
        pick, summed, (((1,), (1,)), ((), ())), precision=HIGHEST, preferred_element_type=F32
    )


def table_kernel(x, table):
    for c in range(PLANE // LANES):
        cols = slice(c * LANES, (c + 1) * LANES)
        table[cols, :] = x[:, cols].T


def sort_kernel(
    sizes_in, offsets_in, projectors_in, pay, lists, sizes, offsets, projectors, sems
):
    pairs = ((sizes_in, sizes), (offsets_in, offsets), (projectors_in, projectors))
    copies = [pltpu.make_async_copy(a, b, sems.at[k]) for k, (a, b) in enumerate(pairs)]
    for copy in copies:
        copy.start()
    before = lax.broadcasted_iota(jnp.int32, (SPHERE, SPHERE), 0)
    after = lax.broadcasted_iota(jnp.int32, (SPHERE, SPHERE), 1)
    until = jnp.where(before <= after, 1.0, 0.0).astype(BF16)
    sub = lax.broadcasted_iota(jnp.int32, (ATOM_DEV, SPHERE), 0)
    lane = lax.broadcasted_iota(jnp.int32, (ATOM_DEV, SPHERE), 1)
    copies[0].wait()
    copies[1].wait()
    size = jnp.zeros((ATOM_DEV, SPHERE), jnp.int32)
    for a in range(ATOM_DEV):
        size = jnp.where(sub == a, sizes[a], size)
    live = lane < size
    off = offsets[...]
    plane = off >> 12
    point = off & (PLANE - 1)
    below = live & (plane < HALO)
    above = live & (plane >= HALO + CZ)
    own = live & (plane >= HALO) & (plane < HALO + CZ)
    flags = jnp.concatenate(
        [jnp.where(m, 1.0, 0.0) for m in (below, own, above)] + [jnp.zeros((8, SPHERE), F32)],
        axis=0,
    ).astype(BF16)
    rank = jnp.dot(flags, until, preferred_element_type=F32).astype(jnp.int32)
    n_below = jnp.max(rank[0:8], axis=1, keepdims=True)
    n_own = jnp.max(rank[8:16], axis=1, keepdims=True)
    n_above = jnp.max(rank[16:24], axis=1, keepdims=True)
    place = jnp.where(
        below,
        rank[0:8] - 1,
        jnp.where(own, n_below + rank[8:16] - 1, SPHERE - rank[16:24]),
    )
    place = jnp.where(live, (place >> 1) + (place & 1) * WORDS, -1)
    copies[2].wait()
    table = jnp.concatenate(
        [
            projectors[...],
            (point >> 6).astype(F32)[None],
            (point & 63).astype(F32)[None],
            plane.astype(F32)[None],
        ],
        axis=0,
    )
    table = jnp.transpose(table, (1, 0, 2))
    points = []
    for a in range(ATOM_DEV):
        high = table[a].astype(BF16)
        low = (table[a] - high.astype(F32)).astype(BF16)
        move = jnp.where(before == place[a : a + 1, :], 1.0, 0.0).astype(BF16)
        moved = lax.dot_general(
            jnp.concatenate([high, low], axis=0),
            move,
            (((1,), (1,)), ((), ())),
            preferred_element_type=F32,
        )
        moved = moved[0:16] + moved[16:32]
        first = a * TILES * 16
        for t in range(TILES):
            pay[first + t * 16 : first + (t + 1) * 16, :] = moved[:, t * LANES : (t + 1) * LANES]
        points.append(moved[13:14] * 64.0 + moved[14:15])
    points = jnp.concatenate(points, axis=0)
    words = points[:, :WORDS] + points[:, WORDS:] * float(PLANE)
    for t in range(WORDS // LANES):
        at = t * ATOM_DEV
        lists[at : at + ATOM_DEV, :] = words[:, t * LANES : (t + 1) * LANES].astype(jnp.int32)
        for start, shift in ((SORTED, 0), (SORTED + LIST, WORDS)):
            part = points[:, shift + t * LANES : shift + (t + 1) * LANES]
            pay[start + at : start + at + ATOM_DEV, :] = part
    at = LIST - ATOM_DEV
    lead = lane[:, :LANES] < LANES // 2
    pay[SORTED + at : SORTED + LIST, :] = jnp.where(lead, n_below, n_above).astype(F32)
    pay[SORTED + LIST + at : SORTED + 2 * LIST, :] = jnp.zeros((ATOM_DEV, LANES), F32)
    lists[at:LIST, :] = jnp.where(lead, n_below, n_below + n_own)


def words_of(pay):
    words = pay[SORTED : SORTED + LIST] + pay[SORTED + LIST :] * float(PLANE)
    return words.astype(jnp.int32).reshape(-1)


def own_points(atoms, lists, table, pay, rows):
    rows[...] = jnp.zeros_like(rows)
    step = 16
    for a in atoms:
        begin, end = counts(lists, a)
        first = begin // (2 * step)
        last = (end + (2 * step - 1)) // (2 * step)
        gather_rows(lists, a, first, last, step, table, rows)
    return project(pay, rows, -HALO, range(CZ), range(TILES), atoms)


def early_kernel(lists, table, pay, q, rows):
    q[...] = own_points(range(EARLY), lists, table, pay, rows)


def late_kernel(lists, occ, x, table, pay, after, packed, q, rows):
    del after
    for c in range(PLANE // LANES):
        cols = slice(c * LANES, (c + 1) * LANES)
        acc = jnp.zeros((CZ, LANES), F32)
        for n in range(BANDS):
            v = x[n * CZ : (n + 1) * CZ, cols]
            acc = acc + occ[n] * (v * v)
        packed[c // 2, (c % 2) * CZ : (c % 2 + 1) * CZ, :] = acc
    q[...] = own_points(range(EARLY, ATOM_DEV), lists, table, pay, rows)


def side_kernel(list_lo, list_hi, table, pay_lo, pay_hi, q_lo, q_hi, rows):
    rows[...] = jnp.zeros_like(rows)
    step = 8
    most = jnp.int32(0)
    for a in range(ATOM_DEV):
        most = jnp.maximum(most, jnp.maximum(counts(list_lo, a)[1], counts(list_hi, a)[0]))

    def from_below():
        for a in range(ATOM_DEV):
            first = (SPHERE - counts(list_lo, a)[1]) // (2 * step)
            gather_rows(list_lo, a, first, WORDS // step, step, table, rows)

    def from_above():
        for a in range(ATOM_DEV):
            last = (counts(list_hi, a)[0] + (2 * step - 1)) // (2 * step)
            gather_rows(list_hi, a, 0, last, step, table, rows)

    low, high = range(HALO), range(CZ - HALO, CZ)

    @pl.when(most <= WORDS)
    def _():
        from_below()
        from_above()
        q_lo[...] = project(pay_lo, rows, -HALO - CZ, low, (1, 3))
        q_hi[...] = project(pay_hi, rows, CZ - HALO, high, (0, 2))

    @pl.when(most > WORDS)
    def _():
        from_below()
        q_lo[...] = project(pay_lo, rows, -HALO - CZ, low, range(TILES))
        from_above()
        q_hi[...] = project(pay_hi, rows, CZ - HALO, high, range(TILES))


def matrix_kernel(q0, q1, q2, q3, occ, packed, out, block, sem):
    del packed
    proj = q0[...] + q1[...] + q2[...] + q3[...]
    weighted = proj * occ[...]
    full = lax.dot_general(
        weighted, proj, (((0,), (0,)), ((), ())), precision=HIGHEST, preferred_element_type=F32
    )
    lane_atom = lax.broadcasted_iota(jnp.int32, (16, LANES), 1) // 16
    acc = jnp.zeros((16, LANES), F32)
    for a in range(ATOM_DEV):
        acc = acc + jnp.where(lane_atom == a, full[a * 16 : (a + 1) * 16, :], 0.0)
    i = lax.broadcasted_iota(jnp.int32, (8, LANES), 0)
    j = lax.broadcasted_iota(jnp.int32, (8, LANES), 1) % 16
    corner = pltpu.roll(pltpu.roll(acc[8:16], 1, 0), LANES - 8, 1)
    half = jnp.where(j < i, corner, acc[0:8])
    for b in range(16):
        block[b] = half
    copy = pltpu.make_async_copy(block, out.at[:, pl.ds(16, 8), :], sem)
    copy.start()
    copy.wait()


def charge_kernel(start, recv, coupling, shapes, offsets, core, down, up, matrices):
    total = recv[0]
    for b in range(1, 16):
        total = total + recv[b]
    matrix = total[16:24]
    matrices[...] = matrix
    per_lane = jnp.concatenate(
        [jnp.sum(coupling[l] * matrix, axis=0, keepdims=True) for l in range(NL)], axis=0
    )
    atom = lax.broadcasted_iota(jnp.int32, (ATOM_DEV, LANES), 0)
    lane_atom = lax.broadcasted_iota(jnp.int32, (ATOM_DEV, LANES), 1) // 16
    pick = (atom == lane_atom).astype(F32)
    charges = lax.dot_general(
        pick, per_lane, (((1,), (1,)), ((), ())), precision=HIGHEST, preferred_element_type=F32
    )
    comp = jnp.zeros((ATOM_DEV, SPHERE), F32)
    for l in range(NL):
        comp = comp + charges[:, l : l + 1] * shapes[l]
    c1 = comp.astype(BF16).astype(F32)
    c2 = (comp - c1).astype(BF16).astype(F32)
    c3 = comp - c1 - c2
    plane = offsets[...] >> 12
    column = (offsets[...] & (PLANE - 1)) - start[0]
    row = lax.broadcasted_iota(jnp.int32, (24, SPHERE), 0)
    target = jnp.where(row < 8, row + HALO, jnp.where(row < 16, row - 11, row - 3))
    col = lax.broadcasted_iota(jnp.int32, (256, SPHERE), 0)
    acc = jnp.zeros((80, 256), F32)
    for a in range(ATOM_DEV):
        here = target == plane[a : a + 1, :]
        left = jnp.concatenate(
            [jnp.where(here, c[a : a + 1, :], 0.0) for c in (c1, c2, c3)]
            + [jnp.zeros((8, SPHERE), F32)],
            axis=0,
        ).astype(BF16)
        right = jnp.where(col == column[a : a + 1, :], 1.0, 0.0).astype(BF16)
        acc = acc + lax.dot_general(
            left, right, (((1,), (1,)), ((), ())), preferred_element_type=F32
        )
    placed = acc[0:24] + acc[24:48] + acc[48:72]
    core[...] = placed[0:8] + jnp.concatenate([total[0:8], total[8:16]], axis=1)
    down[...] = placed[8:16]
    up[...] = placed[16:24]


def shape(*dims):
    return jax.ShapeDtypeStruct(dims, F32)


def local(orbitals, occupations, projectors, shapes, coupling, sphere_offsets, sphere_sizes):
    slabs = lax.axis_size("slab")
    to_next = [(i, (i + 1) % slabs) for i in range(slabs)]
    to_prev = [((i + 1) % slabs, i) for i in range(slabs)]
    grid_values = orbitals.reshape(BANDS * CZ, PLANE)
    table = pl.pallas_call(
        table_kernel,
        out_shape=shape(PLANE, LANES),
        in_specs=[VM],
        out_specs=VM,
        compiler_params=params(),
        cost_estimate=pl.CostEstimate(flops=0, bytes_accessed=8 * 2**20, transcendentals=0),
        name="grid_table",
    )(grid_values)
    pay, lists = pl.pallas_call(
        sort_kernel,
        out_shape=(
            shape(SORTED + 2 * LIST, LANES),
            jax.ShapeDtypeStruct((LIST, LANES), jnp.int32),
        ),
        in_specs=[ANY] * 3,
        out_specs=(VM, VM),
        scratch_shapes=[
            pltpu.SMEM((ATOM_DEV,), jnp.int32),
            pltpu.VMEM((ATOM_DEV, SPHERE), jnp.int32),
            pltpu.VMEM((NI, ATOM_DEV, SPHERE), F32),
            pltpu.SemaphoreType.DMA((3,)),
        ],
        compiler_params=params(58 * 2**20),
        cost_estimate=pl.CostEstimate(flops=10**9, bytes_accessed=8 * 2**20, transcendentals=0),
        name="sort_points",
    )(sphere_sizes, sphere_offsets, projectors.transpose(1, 0, 2))
    pay_lo = lax.ppermute(pay, "slab", to_next)
    pay_hi = lax.ppermute(pay, "slab", to_prev)

    own_list = lists.reshape(-1)
    scratch = [pltpu.VMEM((ATOM_DEV * SPHERE, LANES), F32)]
    q_early = pl.pallas_call(
        early_kernel,
        out_shape=shape(BANDS, LANES),
        in_specs=[SM, VM, VM],
        out_specs=VM,
        scratch_shapes=scratch,
        compiler_params=params(),
        cost_estimate=pl.CostEstimate(flops=10**9, bytes_accessed=8 * 2**20, transcendentals=0),
        name="own_points_early",
    )(own_list, table, pay)

    q_lo, q_hi = pl.pallas_call(
        side_kernel,
        out_shape=(shape(BANDS, LANES), shape(BANDS, LANES)),
        in_specs=[SM, SM, VM, VM, VM],
        out_specs=(VM, VM),
        scratch_shapes=[pltpu.VMEM((ATOM_DEV * SPHERE, LANES), F32)],
        compiler_params=params(),
        name="side_points",
    )(
        words_of(pay_lo),
        words_of(pay_hi),
        table,
        pay_lo,
        pay_hi,
    )
    back_hi = lax.ppermute(q_lo, "slab", to_prev)
    back_lo = lax.ppermute(q_hi, "slab", to_next)

    packed, q_late = pl.pallas_call(
        late_kernel,
        out_shape=(shape(16, 24, LANES), shape(BANDS, LANES)),
        in_specs=[SM, SM, VM, VM, VM, ANY],
        out_specs=(VM, VM),
        scratch_shapes=scratch,
        compiler_params=params(),
        cost_estimate=pl.CostEstimate(flops=10**9, bytes_accessed=8 * 2**20, transcendentals=0),
        name="own_points_late",
    )(own_list, occupations, grid_values, table, pay, q_lo)

    packed = pl.pallas_call(
        matrix_kernel,
        out_shape=shape(16, 24, LANES),
        in_specs=[VM] * 5 + [ANY],
        out_specs=ANY,
        scratch_shapes=[pltpu.VMEM((16, 8, LANES), F32), pltpu.SemaphoreType.DMA],
        input_output_aliases={5: 0},
        compiler_params=params(),
        name="partial_matrices",
    )(
        q_early,
        q_late,
        back_hi,
        back_lo,
        jnp.broadcast_to(occupations[:, None], (BANDS, LANES)),
        packed,
    )
    recv = lax.all_to_all(packed, "band", 0, 0)

    unpack = np.zeros((8, 16, NI, NI), np.float32)
    for i in range(NI):
        for j in range(NI):
            r, c = min(i, j), max(i, j)
            p, q = (r, c) if r < 8 else (c - 7, r - 8)
            unpack[p, q, i, j] = 1.0
    both_ways = jnp.where(np.eye(NI, dtype=bool), coupling, coupling + coupling.transpose(0, 2, 1))
    top = jnp.pad(both_ways[:, :8], ((0, 0), (0, 0), (0, 3)))
    low = jnp.pad(both_ways[:, 8:, 8:], ((0, 0), (1, 2), (0, 11)))
    coupling_packed = jnp.where(np.tri(8, 16, -1, dtype=bool), low, top)
    coupling_lanes = jnp.tile(coupling_packed, (1, 1, ATOM_DEV))
    live = jnp.arange(SPHERE, dtype=jnp.int32)[None, :] < sphere_sizes[:, None]
    shapes_live = jnp.where(live[:, None, :], shapes, 0.0).transpose(1, 0, 2)
    width = PLANE // lax.axis_size("band")
    start = (lax.axis_index("band") * width).astype(jnp.int32).reshape(1)
    core, down, up, matrices = pl.pallas_call(
        charge_kernel,
        out_shape=(shape(CZ, 256), shape(CZ, 256), shape(CZ, 256), shape(8, LANES)),
        in_specs=[SM, VM, VM, VM, VM],
        out_specs=(VM, VM, VM, VM),
        compiler_params=params(),
        name="charges",
    )(start, recv, coupling_lanes, shapes_live, sphere_offsets)
    from_above = lax.ppermute(down, "slab", to_prev)
    from_below = lax.ppermute(up, "slab", to_next)
    density = core + from_above + from_below
    density_matrices = jnp.einsum(
        "paq,pqij->aij", matrices.reshape(8, ATOM_DEV, 16), unpack, precision=HIGHEST
    )
    return (density, density_matrices)


def solution(mesh):
    placed = (
        P("band", "slab", None),
        P("band"),
        P("slab", None, None),
        P("slab", None, None),
        P(),
        P("slab", None),
        P("slab"),
    )
    return jax.shard_map(
        local,
        mesh=mesh,
        in_specs=placed,
        out_specs=(P("slab", "band"), P("slab", None, None)),
        check_vma=False,
    )
```

```python
import jax
import jax.numpy as jnp
import numpy as np
from jax import lax
from jax.experimental import pallas as pl
from jax.experimental.pallas import tpu as pltpu
from jax.sharding import PartitionSpec as P

HALO = 5
PLANE = 4096
CZ = 8
ATOM_DEV = 8
SPHERE = 512
NI = 13
NL = 9
BANDS = 16
LANES = 128
EARLY = 5
TILES = SPHERE // LANES
WORDS = SPHERE // 2
SORTED = TILES * ATOM_DEV * 16
LIST = WORDS // LANES * ATOM_DEV + ATOM_DEV
HIGHEST = lax.Precision.HIGHEST
F32 = jnp.float32
BF16 = jnp.bfloat16

VM = pl.BlockSpec(memory_space=pltpu.VMEM)
SM = pl.BlockSpec(memory_space=pltpu.SMEM)
ANY = pl.BlockSpec(memory_space=pl.ANY)


def params(limit=48 * 2**20):
    return pltpu.CompilerParams(vmem_limit_bytes=limit)


def gather_rows(points, atom, first, last, step, table, rows):
    base = atom * SPHERE

    def body(s, carry):
        i = pl.multiple_of(s * step, step)
        at = (i >> 7) * (ATOM_DEV * LANES) + atom * LANES + (i & (LANES - 1))
        for u in range(step):
            word = points[at + u]
            rows[pl.ds(base + i + u, 1), :] = table[pl.ds(word & (PLANE - 1), 1), :]
            rows[pl.ds(base + WORDS + i + u, 1), :] = table[pl.ds(word >> 12, 1), :]
        return carry

    lax.fori_loop(first, last, body, 0)


def counts(points, atom):
    at = WORDS * ATOM_DEV + atom * LANES
    return points[at], points[at + LANES - 1]


def one_hot(values):
    wide = jnp.broadcast_to(values, (16, values.shape[1])).astype(BF16)
    row = lax.broadcasted_iota(jnp.int32, wide.shape, 0)
    one, zero = jnp.ones_like(wide), jnp.zeros_like(wide)
    return jnp.concatenate(
        [jnp.where(wide == (row + k).astype(F32).astype(BF16), one, zero) for k in range(0, 256, 16)],
        axis=0,
    )


def project(pay, rows, shift, planes, tiles, atoms=range(ATOM_DEV)):
    width = len(tiles) * LANES
    span = len(planes) * 16
    lane_plane = lax.broadcasted_iota(jnp.int32, (16, LANES), 1) % CZ
    sub = lax.broadcasted_iota(jnp.int32, (16, width), 0)
    parts = []
    for a in range(ATOM_DEV):
        if a not in atoms:
            parts.append(jnp.zeros((16, LANES), F32))
            continue
        block = jnp.concatenate(
            [pay[(a * TILES + t) * 16 : (a * TILES + t + 1) * 16, :] for t in tiles], axis=1
        )
        plane = jnp.broadcast_to(block[15:16, :] + float(shift), (16, width)).astype(BF16)
        proj = jnp.where(sub < NI, block, 0.0)
        high = proj.astype(BF16)
        low = (proj - high.astype(F32)).astype(BF16)
        pieces = []
        for piece in (high, low):
            for z in planes:
                pieces.append(jnp.where(plane == jnp.full_like(plane, z), piece, jnp.zeros_like(piece)))
        left = jnp.concatenate(pieces, axis=0)
        gathered = jnp.concatenate(
            [rows[a * SPHERE + t * LANES : a * SPHERE + (t + 1) * LANES, :] for t in tiles], axis=0
        )
        g_high = gathered.astype(BF16)
        g_low = (gathered - g_high.astype(F32)).astype(BF16)
        both = jnp.concatenate([g_high, g_low], axis=1)
        product = jnp.dot(left, both, preferred_element_type=F32)
        total = product[:span, :LANES] + product[span:, :LANES] + product[:span, LANES:]
        acc = jnp.zeros((16, LANES), F32)
        for k, z in enumerate(planes):
            acc = acc + jnp.where(lane_plane == z, total[k * 16 : (k + 1) * 16, :], 0.0)
        parts.append(acc)
    summed = jnp.concatenate(parts, axis=0)
    band = lax.broadcasted_iota(jnp.int32, (BANDS, LANES), 0)
    lane_band = lax.broadcasted_iota(jnp.int32, (BANDS, LANES), 1) // CZ
    pick = (band == lane_band).astype(F32)
    return lax.dot_general(
        pick, summed, (((1,), (1,)), ((), ())), precision=HIGHEST, preferred_element_type=F32
    )


def table_kernel(x, table):
    for c in range(PLANE // LANES):
        cols = slice(c * LANES, (c + 1) * LANES)
        table[cols, :] = x[:, cols].T


def sort_kernel(
    sizes_in, offsets_in, projectors_in, pay, lists, sizes, offsets, projectors, sems
):
    pairs = ((sizes_in, sizes), (offsets_in, offsets), (projectors_in, projectors))
    copies = [pltpu.make_async_copy(a, b, sems.at[k]) for k, (a, b) in enumerate(pairs)]
    for copy in copies:
        copy.start()
    before = lax.broadcasted_iota(jnp.int32, (SPHERE, SPHERE), 0)
    after = lax.broadcasted_iota(jnp.int32, (SPHERE, SPHERE), 1)
    until = jnp.where(before <= after, 1.0, 0.0).astype(BF16)
    sub = lax.broadcasted_iota(jnp.int32, (ATOM_DEV, SPHERE), 0)
    lane = lax.broadcasted_iota(jnp.int32, (ATOM_DEV, SPHERE), 1)
    copies[0].wait()
    copies[1].wait()
    size = jnp.zeros((ATOM_DEV, SPHERE), jnp.int32)
    for a in range(ATOM_DEV):
        size = jnp.where(sub == a, sizes[a], size)
    live = lane < size
    off = offsets[...]
    plane = off >> 12
    point = off & (PLANE - 1)
    below = live & (plane < HALO)
    above = live & (plane >= HALO + CZ)
    own = live & (plane >= HALO) & (plane < HALO + CZ)
    flags = jnp.concatenate(
        [jnp.where(m, 1.0, 0.0) for m in (below, own, above)] + [jnp.zeros((8, SPHERE), F32)],
        axis=0,
    ).astype(BF16)
    rank = jnp.dot(flags, until, preferred_element_type=F32).astype(jnp.int32)
    n_below = jnp.max(rank[0:8], axis=1, keepdims=True)
    n_own = jnp.max(rank[8:16], axis=1, keepdims=True)
    n_above = jnp.max(rank[16:24], axis=1, keepdims=True)
    place = jnp.where(
        below,
        rank[0:8] - 1,
        jnp.where(own, n_below + rank[8:16] - 1, SPHERE - rank[16:24]),
    )
    place = jnp.where(live, (place >> 1) + (place & 1) * WORDS, -1)
    halves = [jnp.where(place >> 8 == h, place & 255, -1).astype(F32) for h in range(SPHERE // 256)]
    copies[2].wait()
    table = jnp.concatenate(
        [
            projectors[...],
            (point >> 6).astype(F32)[None],
            (point & 63).astype(F32)[None],
            plane.astype(F32)[None],
        ],
        axis=0,
    )
    table = jnp.transpose(table, (1, 0, 2))
    points = []
    for a in range(ATOM_DEV):
        high = table[a].astype(BF16)
        low = (table[a] - high.astype(F32)).astype(BF16)
        move = jnp.concatenate([one_hot(v[a : a + 1, :]) for v in halves], axis=0)
        moved = lax.dot_general(
            jnp.concatenate([high, low], axis=0),
            move,
            (((1,), (1,)), ((), ())),
            preferred_element_type=F32,
        )
        moved = moved[0:16] + moved[16:32]
        first = a * TILES * 16
        for t in range(TILES):
            pay[first + t * 16 : first + (t + 1) * 16, :] = moved[:, t * LANES : (t + 1) * LANES]
        points.append(moved[13:14] * 64.0 + moved[14:15])
    points = jnp.concatenate(points, axis=0)
    words = points[:, :WORDS] + points[:, WORDS:] * float(PLANE)
    for t in range(WORDS // LANES):
        at = t * ATOM_DEV
        lists[at : at + ATOM_DEV, :] = words[:, t * LANES : (t + 1) * LANES].astype(jnp.int32)
        for start, shift in ((SORTED, 0), (SORTED + LIST, WORDS)):
            part = points[:, shift + t * LANES : shift + (t + 1) * LANES]
            pay[start + at : start + at + ATOM_DEV, :] = part
    at = LIST - ATOM_DEV
    lead = lane[:, :LANES] < LANES // 2
    pay[SORTED + at : SORTED + LIST, :] = jnp.where(lead, n_below, n_above).astype(F32)
    pay[SORTED + LIST + at : SORTED + 2 * LIST, :] = jnp.zeros((ATOM_DEV, LANES), F32)
    lists[at:LIST, :] = jnp.where(lead, n_below, n_below + n_own)


def words_of(pay):
    words = pay[SORTED : SORTED + LIST] + pay[SORTED + LIST :] * float(PLANE)
    return words.astype(jnp.int32).reshape(-1)


def own_points(atoms, lists, table, pay, rows):
    rows[...] = jnp.zeros_like(rows)
    step = 16
    for a in atoms:
        begin, end = counts(lists, a)
        first = begin // (2 * step)
        last = (end + (2 * step - 1)) // (2 * step)
        gather_rows(lists, a, first, last, step, table, rows)
    return project(pay, rows, -HALO, range(CZ), range(TILES), atoms)


def early_kernel(lists, table, pay, q, rows):
    q[...] = own_points(range(EARLY), lists, table, pay, rows)


def late_kernel(lists, occ, x, table, pay, after, packed, q, rows):
    del after
    for c in range(PLANE // LANES):
        cols = slice(c * LANES, (c + 1) * LANES)
        acc = jnp.zeros((CZ, LANES), F32)
        for n in range(BANDS):
            v = x[n * CZ : (n + 1) * CZ, cols]
            acc = acc + occ[n] * (v * v)
        packed[c // 2, (c % 2) * CZ : (c % 2 + 1) * CZ, :] = acc
    q[...] = own_points(range(EARLY, ATOM_DEV), lists, table, pay, rows)


def side_kernel(list_lo, list_hi, table, pay_lo, pay_hi, q_lo, q_hi, rows):
    rows[...] = jnp.zeros_like(rows)
    step = 8
    most = jnp.int32(0)
    for a in range(ATOM_DEV):
        most = jnp.maximum(most, jnp.maximum(counts(list_lo, a)[1], counts(list_hi, a)[0]))

    def from_below():
        for a in range(ATOM_DEV):
            first = (SPHERE - counts(list_lo, a)[1]) // (2 * step)
            gather_rows(list_lo, a, first, WORDS // step, step, table, rows)

    def from_above():
        for a in range(ATOM_DEV):
            last = (counts(list_hi, a)[0] + (2 * step - 1)) // (2 * step)
            gather_rows(list_hi, a, 0, last, step, table, rows)

    low, high = range(HALO), range(CZ - HALO, CZ)

    @pl.when(most <= WORDS)
    def _():
        from_below()
        from_above()
        q_lo[...] = project(pay_lo, rows, -HALO - CZ, low, (1, 3))
        q_hi[...] = project(pay_hi, rows, CZ - HALO, high, (0, 2))

    @pl.when(most > WORDS)
    def _():
        from_below()
        q_lo[...] = project(pay_lo, rows, -HALO - CZ, low, range(TILES))
        from_above()
        q_hi[...] = project(pay_hi, rows, CZ - HALO, high, range(TILES))


def matrix_kernel(q0, q1, q2, q3, occ, packed, out, block, sem):
    del packed
    proj = q0[...] + q1[...] + q2[...] + q3[...]
    weighted = proj * occ[...]
    full = lax.dot_general(
        weighted, proj, (((0,), (0,)), ((), ())), precision=HIGHEST, preferred_element_type=F32
    )
    lane_atom = lax.broadcasted_iota(jnp.int32, (16, LANES), 1) // 16
    acc = jnp.zeros((16, LANES), F32)
    for a in range(ATOM_DEV):
        acc = acc + jnp.where(lane_atom == a, full[a * 16 : (a + 1) * 16, :], 0.0)
    i = lax.broadcasted_iota(jnp.int32, (8, LANES), 0)
    j = lax.broadcasted_iota(jnp.int32, (8, LANES), 1) % 16
    corner = pltpu.roll(pltpu.roll(acc[8:16], 1, 0), LANES - 8, 1)
    half = jnp.where(j < i, corner, acc[0:8])
    for b in range(16):
        block[b] = half
    copy = pltpu.make_async_copy(block, out.at[:, pl.ds(16, 8), :], sem)
    copy.start()
    copy.wait()


def charge_kernel(start, recv, coupling, shapes, offsets, core, down, up, matrices):
    total = recv[0]
    for b in range(1, 16):
        total = total + recv[b]
    matrix = total[16:24]
    matrices[...] = matrix
    per_lane = jnp.concatenate(
        [jnp.sum(coupling[l] * matrix, axis=0, keepdims=True) for l in range(NL)], axis=0
    )
    atom = lax.broadcasted_iota(jnp.int32, (ATOM_DEV, LANES), 0)
    lane_atom = lax.broadcasted_iota(jnp.int32, (ATOM_DEV, LANES), 1) // 16
    pick = (atom == lane_atom).astype(F32)
    charges = lax.dot_general(
        pick, per_lane, (((1,), (1,)), ((), ())), precision=HIGHEST, preferred_element_type=F32
    )
    comp = jnp.zeros((ATOM_DEV, SPHERE), F32)
    for l in range(NL):
        comp = comp + charges[:, l : l + 1] * shapes[l]
    c1 = comp.astype(BF16).astype(F32)
    c2 = (comp - c1).astype(BF16).astype(F32)
    c3 = comp - c1 - c2
    plane = offsets[...] >> 12
    column = (offsets[...] & (PLANE - 1)) - start[0]
    column = jnp.where((column >= 0) & (column < 256), column, -1).astype(F32)
    row = lax.broadcasted_iota(jnp.int32, (24, SPHERE), 0)
    target = jnp.where(row < 8, row + HALO, jnp.where(row < 16, row - 11, row - 3))
    acc = jnp.zeros((80, 256), F32)
    for a in range(ATOM_DEV):
        here = target == plane[a : a + 1, :]
        left = jnp.concatenate(
            [jnp.where(here, c[a : a + 1, :], 0.0) for c in (c1, c2, c3)]
            + [jnp.zeros((8, SPHERE), F32)],
            axis=0,
        ).astype(BF16)
        right = one_hot(column[a : a + 1, :])
        acc = acc + lax.dot_general(
            left, right, (((1,), (1,)), ((), ())), preferred_element_type=F32
        )
    placed = acc[0:24] + acc[24:48] + acc[48:72]
    core[...] = placed[0:8] + jnp.concatenate([total[0:8], total[8:16]], axis=1)
    down[...] = placed[8:16]
    up[...] = placed[16:24]


def shape(*dims):
    return jax.ShapeDtypeStruct(dims, F32)


def local(orbitals, occupations, projectors, shapes, coupling, sphere_offsets, sphere_sizes):
    slabs = lax.axis_size("slab")
    to_next = [(i, (i + 1) % slabs) for i in range(slabs)]
    to_prev = [((i + 1) % slabs, i) for i in range(slabs)]
    grid_values = orbitals.reshape(BANDS * CZ, PLANE)
    table = pl.pallas_call(
        table_kernel,
        out_shape=shape(PLANE, LANES),
        in_specs=[VM],
        out_specs=VM,
        compiler_params=params(),
        cost_estimate=pl.CostEstimate(flops=0, bytes_accessed=8 * 2**20, transcendentals=0),
        name="grid_table",
    )(grid_values)
    pay, lists = pl.pallas_call(
        sort_kernel,
        out_shape=(
            shape(SORTED + 2 * LIST, LANES),
            jax.ShapeDtypeStruct((LIST, LANES), jnp.int32),
        ),
        in_specs=[ANY] * 3,
        out_specs=(VM, VM),
        scratch_shapes=[
            pltpu.SMEM((ATOM_DEV,), jnp.int32),
            pltpu.VMEM((ATOM_DEV, SPHERE), jnp.int32),
            pltpu.VMEM((NI, ATOM_DEV, SPHERE), F32),
            pltpu.SemaphoreType.DMA((3,)),
        ],
        compiler_params=params(58 * 2**20),
        cost_estimate=pl.CostEstimate(flops=10**9, bytes_accessed=8 * 2**20, transcendentals=0),
        name="sort_points",
    )(sphere_sizes, sphere_offsets, projectors.transpose(1, 0, 2))
    pay_lo = lax.ppermute(pay, "slab", to_next)
    pay_hi = lax.ppermute(pay, "slab", to_prev)

    own_list = lists.reshape(-1)
    scratch = [pltpu.VMEM((ATOM_DEV * SPHERE, LANES), F32)]
    q_early = pl.pallas_call(
        early_kernel,
        out_shape=shape(BANDS, LANES),
        in_specs=[SM, VM, VM],
        out_specs=VM,
        scratch_shapes=scratch,
        compiler_params=params(),
        cost_estimate=pl.CostEstimate(flops=10**9, bytes_accessed=8 * 2**20, transcendentals=0),
        name="own_points_early",
    )(own_list, table, pay)

    q_lo, q_hi = pl.pallas_call(
        side_kernel,
        out_shape=(shape(BANDS, LANES), shape(BANDS, LANES)),
        in_specs=[SM, SM, VM, VM, VM],
        out_specs=(VM, VM),
        scratch_shapes=[pltpu.VMEM((ATOM_DEV * SPHERE, LANES), F32)],
        compiler_params=params(),
        name="side_points",
    )(
        words_of(pay_lo),
        words_of(pay_hi),
        table,
        pay_lo,
        pay_hi,
    )
    back_hi = lax.ppermute(q_lo, "slab", to_prev)
    back_lo = lax.ppermute(q_hi, "slab", to_next)

    packed, q_late = pl.pallas_call(
        late_kernel,
        out_shape=(shape(16, 24, LANES), shape(BANDS, LANES)),
        in_specs=[SM, SM, VM, VM, VM, ANY],
        out_specs=(VM, VM),
        scratch_shapes=scratch,
        compiler_params=params(),
        cost_estimate=pl.CostEstimate(flops=10**9, bytes_accessed=8 * 2**20, transcendentals=0),
        name="own_points_late",
    )(own_list, occupations, grid_values, table, pay, q_lo)

    packed = pl.pallas_call(
        matrix_kernel,
        out_shape=shape(16, 24, LANES),
        in_specs=[VM] * 5 + [ANY],
        out_specs=ANY,
        scratch_shapes=[pltpu.VMEM((16, 8, LANES), F32), pltpu.SemaphoreType.DMA],
        input_output_aliases={5: 0},
        compiler_params=params(),
        name="partial_matrices",
    )(
        q_early,
        q_late,
        back_hi,
        back_lo,
        jnp.broadcast_to(occupations[:, None], (BANDS, LANES)),
        packed,
    )
    recv = lax.all_to_all(packed, "band", 0, 0)

    unpack = np.zeros((8, 16, NI, NI), np.float32)
    for i in range(NI):
        for j in range(NI):
            r, c = min(i, j), max(i, j)
            p, q = (r, c) if r < 8 else (c - 7, r - 8)
            unpack[p, q, i, j] = 1.0
    both_ways = jnp.where(np.eye(NI, dtype=bool), coupling, coupling + coupling.transpose(0, 2, 1))
    top = jnp.pad(both_ways[:, :8], ((0, 0), (0, 0), (0, 3)))
    low = jnp.pad(both_ways[:, 8:, 8:], ((0, 0), (1, 2), (0, 11)))
    coupling_packed = jnp.where(np.tri(8, 16, -1, dtype=bool), low, top)
    coupling_lanes = jnp.tile(coupling_packed, (1, 1, ATOM_DEV))
    live = jnp.arange(SPHERE, dtype=jnp.int32)[None, :] < sphere_sizes[:, None]
    shapes_live = jnp.where(live[:, None, :], shapes, 0.0).transpose(1, 0, 2)
    width = PLANE // lax.axis_size("band")
    start = (lax.axis_index("band") * width).astype(jnp.int32).reshape(1)
    core, down, up, matrices = pl.pallas_call(
        charge_kernel,
        out_shape=(shape(CZ, 256), shape(CZ, 256), shape(CZ, 256), shape(8, LANES)),
        in_specs=[SM, VM, VM, VM, VM],
        out_specs=(VM, VM, VM, VM),
        compiler_params=params(),
        name="charges",
    )(start, recv, coupling_lanes, shapes_live, sphere_offsets)
    from_above = lax.ppermute(down, "slab", to_prev)
    from_below = lax.ppermute(up, "slab", to_next)
    density = core + from_above + from_below
    density_matrices = jnp.einsum(
        "paq,pqij->aij", matrices.reshape(8, ATOM_DEV, 16), unpack, precision=HIGHEST
    )
    return (density, density_matrices)


def solution(mesh):
    placed = (
        P("band", "slab", None),
        P("band"),
        P("slab", None, None),
        P("slab", None, None),
        P(),
        P("slab", None),
        P("slab"),
    )
    return jax.shard_map(
        local,
        mesh=mesh,
        in_specs=placed,
        out_specs=(P("slab", "band"), P("slab", None, None)),
        check_vma=False,
    )
```

```python
import jax
import jax.numpy as jnp
import numpy as np
from jax import lax
from jax.experimental import pallas as pl
from jax.experimental.pallas import tpu as pltpu
from jax.sharding import PartitionSpec as P

HALO = 5
PLANE = 4096
CZ = 8
ATOM_DEV = 8
SPHERE = 512
NI = 13
NL = 9
BANDS = 16
LANES = 128
EARLY = 5
TILES = SPHERE // LANES
WORDS = SPHERE // 2
SORTED = TILES * ATOM_DEV * 16
LIST = WORDS // LANES * ATOM_DEV + ATOM_DEV
HIGHEST = lax.Precision.HIGHEST
F32 = jnp.float32
BF16 = jnp.bfloat16

VM = pl.BlockSpec(memory_space=pltpu.VMEM)
SM = pl.BlockSpec(memory_space=pltpu.SMEM)
ANY = pl.BlockSpec(memory_space=pl.ANY)


def params(limit=48 * 2**20):
    return pltpu.CompilerParams(vmem_limit_bytes=limit)


def gather_rows(points, atom, first, last, step, table, rows):
    base = atom * SPHERE

    def body(s, carry):
        i = pl.multiple_of(s * step, step)
        at = (i >> 7) * (ATOM_DEV * LANES) + atom * LANES + (i & (LANES - 1))
        for u in range(step):
            word = points[at + u]
            rows[pl.ds(base + i + u, 1), :] = table[pl.ds(word & (PLANE - 1), 1), :]
            rows[pl.ds(base + WORDS + i + u, 1), :] = table[pl.ds(word >> 12, 1), :]
        return carry

    lax.fori_loop(first, last, body, 0)


def counts(points, atom):
    at = WORDS * ATOM_DEV + atom * LANES
    return points[at], points[at + LANES - 1]


def one_hot(column, width):
    place = lax.broadcasted_iota(jnp.int32, (column.shape[0], width), 1).astype(F32)
    return jnp.where(column == place, 1.0, 0.0).astype(BF16)


def project(pay, rows, shift, planes, tiles, atoms=range(ATOM_DEV)):
    width = len(tiles) * LANES
    span = len(planes) * 16
    lane_plane = lax.broadcasted_iota(jnp.int32, (16, LANES), 1) % CZ
    sub = lax.broadcasted_iota(jnp.int32, (16, width), 0)
    parts = []
    for a in range(ATOM_DEV):
        if a not in atoms:
            parts.append(jnp.zeros((16, LANES), F32))
            continue
        block = jnp.concatenate(
            [pay[(a * TILES + t) * 16 : (a * TILES + t + 1) * 16, :] for t in tiles], axis=1
        )
        plane = jnp.broadcast_to(block[15:16, :] + float(shift), (16, width)).astype(BF16)
        proj = jnp.where(sub < NI, block, 0.0)
        high = proj.astype(BF16)
        low = (proj - high.astype(F32)).astype(BF16)
        pieces = []
        for piece in (high, low):
            for z in planes:
                pieces.append(jnp.where(plane == jnp.full_like(plane, z), piece, jnp.zeros_like(piece)))
        left = jnp.concatenate(pieces, axis=0)
        gathered = jnp.concatenate(
            [rows[a * SPHERE + t * LANES : a * SPHERE + (t + 1) * LANES, :] for t in tiles], axis=0
        )
        g_high = gathered.astype(BF16)
        g_low = (gathered - g_high.astype(F32)).astype(BF16)
        both = jnp.concatenate([g_high, g_low], axis=1)
        product = jnp.dot(left, both, preferred_element_type=F32)
        total = product[:span, :LANES] + product[span:, :LANES] + product[:span, LANES:]
        acc = jnp.zeros((16, LANES), F32)
        for k, z in enumerate(planes):
            acc = acc + jnp.where(lane_plane == z, total[k * 16 : (k + 1) * 16, :], 0.0)
        parts.append(acc)
    summed = jnp.concatenate(parts, axis=0)
    band = lax.broadcasted_iota(jnp.int32, (BANDS, LANES), 0)
    lane_band = lax.broadcasted_iota(jnp.int32, (BANDS, LANES), 1) // CZ
    pick = (band == lane_band).astype(F32)
    return lax.dot_general(
        pick, summed, (((1,), (1,)), ((), ())), precision=HIGHEST, preferred_element_type=F32
    )


def table_kernel(x, table):
    for c in range(PLANE // LANES):
        cols = slice(c * LANES, (c + 1) * LANES)
        table[cols, :] = x[:, cols].T


def sort_kernel(
    sizes_in, offsets_in, projectors_in, pay, lists, sizes, offsets, projectors, sems
):
    pairs = ((sizes_in, sizes), (offsets_in, offsets), (projectors_in, projectors))
    copies = [pltpu.make_async_copy(a, b, sems.at[k]) for k, (a, b) in enumerate(pairs)]
    for copy in copies:
        copy.start()
    before = lax.broadcasted_iota(jnp.int32, (SPHERE, SPHERE), 0)
    after = lax.broadcasted_iota(jnp.int32, (SPHERE, SPHERE), 1)
    until = jnp.where(before <= after, 1.0, 0.0).astype(BF16)
    sub = lax.broadcasted_iota(jnp.int32, (ATOM_DEV, SPHERE), 0)
    lane = lax.broadcasted_iota(jnp.int32, (ATOM_DEV, SPHERE), 1)
    copies[0].wait()
    copies[1].wait()
    size = jnp.zeros((ATOM_DEV, SPHERE), jnp.int32)
    for a in range(ATOM_DEV):
        size = jnp.where(sub == a, sizes[a], size)
    live = lane < size
    off = offsets[...]
    plane = off >> 12
    point = off & (PLANE - 1)
    below = live & (plane < HALO)
    above = live & (plane >= HALO + CZ)
    own = live & (plane >= HALO) & (plane < HALO + CZ)
    flags = jnp.concatenate(
        [jnp.where(m, 1.0, 0.0) for m in (below, own, above)] + [jnp.zeros((8, SPHERE), F32)],
        axis=0,
    ).astype(BF16)
    rank = jnp.dot(flags, until, preferred_element_type=F32).astype(jnp.int32)
    n_below = jnp.max(rank[0:8], axis=1, keepdims=True)
    n_own = jnp.max(rank[8:16], axis=1, keepdims=True)
    n_above = jnp.max(rank[16:24], axis=1, keepdims=True)
    place = jnp.where(
        below,
        rank[0:8] - 1,
        jnp.where(own, n_below + rank[8:16] - 1, SPHERE - rank[16:24]),
    )
    place = jnp.where(live, (place >> 1) + (place & 1) * WORDS, -1)
    place = jnp.transpose(place.astype(F32))
    copies[2].wait()
    table = jnp.concatenate(
        [
            projectors[...],
            (point >> 6).astype(F32)[None],
            (point & 63).astype(F32)[None],
            plane.astype(F32)[None],
        ],
        axis=0,
    )
    table = jnp.transpose(table, (1, 0, 2))
    points = []
    for a in range(ATOM_DEV):
        high = table[a].astype(BF16)
        low = (table[a] - high.astype(F32)).astype(BF16)
        move = one_hot(place[:, a : a + 1], SPHERE)
        moved = jnp.dot(
            jnp.concatenate([high, low], axis=0), move, preferred_element_type=F32
        )
        moved = moved[0:16] + moved[16:32]
        first = a * TILES * 16
        for t in range(TILES):
            pay[first + t * 16 : first + (t + 1) * 16, :] = moved[:, t * LANES : (t + 1) * LANES]
        points.append(moved[13:14] * 64.0 + moved[14:15])
    points = jnp.concatenate(points, axis=0)
    words = points[:, :WORDS] + points[:, WORDS:] * float(PLANE)
    for t in range(WORDS // LANES):
        at = t * ATOM_DEV
        lists[at : at + ATOM_DEV, :] = words[:, t * LANES : (t + 1) * LANES].astype(jnp.int32)
        for start, shift in ((SORTED, 0), (SORTED + LIST, WORDS)):
            part = points[:, shift + t * LANES : shift + (t + 1) * LANES]
            pay[start + at : start + at + ATOM_DEV, :] = part
    at = LIST - ATOM_DEV
    lead = lane[:, :LANES] < LANES // 2
    pay[SORTED + at : SORTED + LIST, :] = jnp.where(lead, n_below, n_above).astype(F32)
    pay[SORTED + LIST + at : SORTED + 2 * LIST, :] = jnp.zeros((ATOM_DEV, LANES), F32)
    lists[at:LIST, :] = jnp.where(lead, n_below, n_below + n_own)


def words_of(pay):
    words = pay[SORTED : SORTED + LIST] + pay[SORTED + LIST :] * float(PLANE)
    return words.astype(jnp.int32).reshape(-1)


def own_points(atoms, lists, table, pay, rows):
    rows[...] = jnp.zeros_like(rows)
    step = 16
    for a in atoms:
        begin, end = counts(lists, a)
        first = begin // (2 * step)
        last = (end + (2 * step - 1)) // (2 * step)
        gather_rows(lists, a, first, last, step, table, rows)
    return project(pay, rows, -HALO, range(CZ), range(TILES), atoms)


def early_kernel(lists, table, pay, q, rows):
    q[...] = own_points(range(EARLY), lists, table, pay, rows)


def late_kernel(lists, occ, x, table, pay, after, packed, q, rows):
    del after
    for c in range(PLANE // LANES):
        cols = slice(c * LANES, (c + 1) * LANES)
        acc = jnp.zeros((CZ, LANES), F32)
        for n in range(BANDS):
            v = x[n * CZ : (n + 1) * CZ, cols]
            acc = acc + occ[n] * (v * v)
        packed[c // 2, (c % 2) * CZ : (c % 2 + 1) * CZ, :] = acc
    q[...] = own_points(range(EARLY, ATOM_DEV), lists, table, pay, rows)


def side_kernel(list_lo, list_hi, table, pay_lo, pay_hi, q_lo, q_hi, rows):
    rows[...] = jnp.zeros_like(rows)
    step = 8
    most = jnp.int32(0)
    for a in range(ATOM_DEV):
        most = jnp.maximum(most, jnp.maximum(counts(list_lo, a)[1], counts(list_hi, a)[0]))

    def from_below():
        for a in range(ATOM_DEV):
            first = (SPHERE - counts(list_lo, a)[1]) // (2 * step)
            gather_rows(list_lo, a, first, WORDS // step, step, table, rows)

    def from_above():
        for a in range(ATOM_DEV):
            last = (counts(list_hi, a)[0] + (2 * step - 1)) // (2 * step)
            gather_rows(list_hi, a, 0, last, step, table, rows)

    low, high = range(HALO), range(CZ - HALO, CZ)

    @pl.when(most <= WORDS)
    def _():
        from_below()
        from_above()
        q_lo[...] = project(pay_lo, rows, -HALO - CZ, low, (1, 3))
        q_hi[...] = project(pay_hi, rows, CZ - HALO, high, (0, 2))

    @pl.when(most > WORDS)
    def _():
        from_below()
        q_lo[...] = project(pay_lo, rows, -HALO - CZ, low, range(TILES))
        from_above()
        q_hi[...] = project(pay_hi, rows, CZ - HALO, high, range(TILES))


def matrix_kernel(q0, q1, q2, q3, occ, packed, out, block, sem):
    del packed
    proj = q0[...] + q1[...] + q2[...] + q3[...]
    weighted = proj * occ[...]
    full = lax.dot_general(
        weighted, proj, (((0,), (0,)), ((), ())), precision=HIGHEST, preferred_element_type=F32
    )
    lane_atom = lax.broadcasted_iota(jnp.int32, (16, LANES), 1) // 16
    acc = jnp.zeros((16, LANES), F32)
    for a in range(ATOM_DEV):
        acc = acc + jnp.where(lane_atom == a, full[a * 16 : (a + 1) * 16, :], 0.0)
    i = lax.broadcasted_iota(jnp.int32, (8, LANES), 0)
    j = lax.broadcasted_iota(jnp.int32, (8, LANES), 1) % 16
    corner = pltpu.roll(pltpu.roll(acc[8:16], 1, 0), LANES - 8, 1)
    half = jnp.where(j < i, corner, acc[0:8])
    for b in range(16):
        block[b] = half
    copy = pltpu.make_async_copy(block, out.at[:, pl.ds(16, 8), :], sem)
    copy.start()
    copy.wait()


def charge_kernel(start, recv, coupling, shapes, offsets, core, down, up, matrices):
    total = recv[0]
    for b in range(1, 16):
        total = total + recv[b]
    matrix = total[16:24]
    matrices[...] = matrix
    per_lane = jnp.concatenate(
        [jnp.sum(coupling[l] * matrix, axis=0, keepdims=True) for l in range(NL)], axis=0
    )
    atom = lax.broadcasted_iota(jnp.int32, (ATOM_DEV, LANES), 0)
    lane_atom = lax.broadcasted_iota(jnp.int32, (ATOM_DEV, LANES), 1) // 16
    pick = (atom == lane_atom).astype(F32)
    charges = lax.dot_general(
        pick, per_lane, (((1,), (1,)), ((), ())), precision=HIGHEST, preferred_element_type=F32
    )
    comp = jnp.zeros((ATOM_DEV, SPHERE), F32)
    for l in range(NL):
        comp = comp + charges[:, l : l + 1] * shapes[l]
    c1 = comp.astype(BF16).astype(F32)
    c2 = (comp - c1).astype(BF16).astype(F32)
    c3 = comp - c1 - c2
    plane = offsets[...] >> 12
    column = (offsets[...] & (PLANE - 1)) - start[0]
    column = jnp.transpose(column.astype(F32))
    row = lax.broadcasted_iota(jnp.int32, (24, SPHERE), 0)
    target = jnp.where(row < 8, row + HALO, jnp.where(row < 16, row - 11, row - 3))
    acc = jnp.zeros((80, 256), F32)
    for a in range(ATOM_DEV):
        here = target == plane[a : a + 1, :]
        left = jnp.concatenate(
            [jnp.where(here, c[a : a + 1, :], 0.0) for c in (c1, c2, c3)]
            + [jnp.zeros((8, SPHERE), F32)],
            axis=0,
        ).astype(BF16)
        right = one_hot(column[:, a : a + 1], 256)
        acc = acc + jnp.dot(left, right, preferred_element_type=F32)
    placed = acc[0:24] + acc[24:48] + acc[48:72]
    core[...] = placed[0:8] + jnp.concatenate([total[0:8], total[8:16]], axis=1)
    down[...] = placed[8:16]
    up[...] = placed[16:24]


def shape(*dims):
    return jax.ShapeDtypeStruct(dims, F32)


def local(orbitals, occupations, projectors, shapes, coupling, sphere_offsets, sphere_sizes):
    slabs = lax.axis_size("slab")
    to_next = [(i, (i + 1) % slabs) for i in range(slabs)]
    to_prev = [((i + 1) % slabs, i) for i in range(slabs)]
    grid_values = orbitals.reshape(BANDS * CZ, PLANE)
    table = pl.pallas_call(
        table_kernel,
        out_shape=shape(PLANE, LANES),
        in_specs=[VM],
        out_specs=VM,
        compiler_params=params(),
        cost_estimate=pl.CostEstimate(flops=0, bytes_accessed=8 * 2**20, transcendentals=0),
        name="grid_table",
    )(grid_values)
    pay, lists = pl.pallas_call(
        sort_kernel,
        out_shape=(
            shape(SORTED + 2 * LIST, LANES),
            jax.ShapeDtypeStruct((LIST, LANES), jnp.int32),
        ),
        in_specs=[ANY] * 3,
        out_specs=(VM, VM),
        scratch_shapes=[
            pltpu.SMEM((ATOM_DEV,), jnp.int32),
            pltpu.VMEM((ATOM_DEV, SPHERE), jnp.int32),
            pltpu.VMEM((NI, ATOM_DEV, SPHERE), F32),
            pltpu.SemaphoreType.DMA((3,)),
        ],
        compiler_params=params(58 * 2**20),
        cost_estimate=pl.CostEstimate(flops=10**9, bytes_accessed=8 * 2**20, transcendentals=0),
        name="sort_points",
    )(sphere_sizes, sphere_offsets, projectors.transpose(1, 0, 2))
    pay_lo = lax.ppermute(pay, "slab", to_next)
    pay_hi = lax.ppermute(pay, "slab", to_prev)

    own_list = lists.reshape(-1)
    scratch = [pltpu.VMEM((ATOM_DEV * SPHERE, LANES), F32)]
    q_early = pl.pallas_call(
        early_kernel,
        out_shape=shape(BANDS, LANES),
        in_specs=[SM, VM, VM],
        out_specs=VM,
        scratch_shapes=scratch,
        compiler_params=params(),
        cost_estimate=pl.CostEstimate(flops=10**9, bytes_accessed=8 * 2**20, transcendentals=0),
        name="own_points_early",
    )(own_list, table, pay)

    q_lo, q_hi = pl.pallas_call(
        side_kernel,
        out_shape=(shape(BANDS, LANES), shape(BANDS, LANES)),
        in_specs=[SM, SM, VM, VM, VM],
        out_specs=(VM, VM),
        scratch_shapes=[pltpu.VMEM((ATOM_DEV * SPHERE, LANES), F32)],
        compiler_params=params(),
        name="side_points",
    )(
        words_of(pay_lo),
        words_of(pay_hi),
        table,
        pay_lo,
        pay_hi,
    )
    back_hi = lax.ppermute(q_lo, "slab", to_prev)
    back_lo = lax.ppermute(q_hi, "slab", to_next)

    packed, q_late = pl.pallas_call(
        late_kernel,
        out_shape=(shape(16, 24, LANES), shape(BANDS, LANES)),
        in_specs=[SM, SM, VM, VM, VM, ANY],
        out_specs=(VM, VM),
        scratch_shapes=scratch,
        compiler_params=params(),
        cost_estimate=pl.CostEstimate(flops=10**9, bytes_accessed=8 * 2**20, transcendentals=0),
        name="own_points_late",
    )(own_list, occupations, grid_values, table, pay, q_lo)

    packed = pl.pallas_call(
        matrix_kernel,
        out_shape=shape(16, 24, LANES),
        in_specs=[VM] * 5 + [ANY],
        out_specs=ANY,
        scratch_shapes=[pltpu.VMEM((16, 8, LANES), F32), pltpu.SemaphoreType.DMA],
        input_output_aliases={5: 0},
        compiler_params=params(),
        name="partial_matrices",
    )(
        q_early,
        q_late,
        back_hi,
        back_lo,
        jnp.broadcast_to(occupations[:, None], (BANDS, LANES)),
        packed,
    )
    recv = lax.all_to_all(packed, "band", 0, 0)

    unpack = np.zeros((8, 16, NI, NI), np.float32)
    for i in range(NI):
        for j in range(NI):
            r, c = min(i, j), max(i, j)
            p, q = (r, c) if r < 8 else (c - 7, r - 8)
            unpack[p, q, i, j] = 1.0
    both_ways = jnp.where(np.eye(NI, dtype=bool), coupling, coupling + coupling.transpose(0, 2, 1))
    top = jnp.pad(both_ways[:, :8], ((0, 0), (0, 0), (0, 3)))
    low = jnp.pad(both_ways[:, 8:, 8:], ((0, 0), (1, 2), (0, 11)))
    coupling_packed = jnp.where(np.tri(8, 16, -1, dtype=bool), low, top)
    coupling_lanes = jnp.tile(coupling_packed, (1, 1, ATOM_DEV))
    live = jnp.arange(SPHERE, dtype=jnp.int32)[None, :] < sphere_sizes[:, None]
    shapes_live = jnp.where(live[:, None, :], shapes, 0.0).transpose(1, 0, 2)
    width = PLANE // lax.axis_size("band")
    start = (lax.axis_index("band") * width).astype(jnp.int32).reshape(1)
    core, down, up, matrices = pl.pallas_call(
        charge_kernel,
        out_shape=(shape(CZ, 256), shape(CZ, 256), shape(CZ, 256), shape(8, LANES)),
        in_specs=[SM, VM, VM, VM, VM],
        out_specs=(VM, VM, VM, VM),
        compiler_params=params(),
        name="charges",
    )(start, recv, coupling_lanes, shapes_live, sphere_offsets)
    from_above = lax.ppermute(down, "slab", to_prev)
    from_below = lax.ppermute(up, "slab", to_next)
    density = core + from_above + from_below
    density_matrices = jnp.einsum(
        "paq,pqij->aij", matrices.reshape(8, ATOM_DEV, 16), unpack, precision=HIGHEST
    )
    return (density, density_matrices)


def solution(mesh):
    placed = (
        P("band", "slab", None),
        P("band"),
        P("slab", None, None),
        P("slab", None, None),
        P(),
        P("slab", None),
        P("slab"),
    )
    return jax.shard_map(
        local,
        mesh=mesh,
        in_specs=placed,
        out_specs=(P("slab", "band"), P("slab", None, None)),
        check_vma=False,
    )
```

```python
import functools

import jax
import jax.numpy as jnp
import numpy as np
from jax import lax
from jax.experimental import pallas as pl
from jax.experimental.pallas import tpu as pltpu
from jax.sharding import PartitionSpec as P

HALO = 5
PLANE = 4096
CZ = 8
ATOM_DEV = 8
SPHERE = 512
NI = 13
NL = 9
BANDS = 16
LANES = 128
EARLY = 5
TILES = SPHERE // LANES
WORDS = SPHERE // 2
SORTED = TILES * ATOM_DEV * 16
LIST = WORDS // LANES * ATOM_DEV + ATOM_DEV
HIGHEST = lax.Precision.HIGHEST
F32 = jnp.float32
BF16 = jnp.bfloat16

VM = pl.BlockSpec(memory_space=pltpu.VMEM)
SM = pl.BlockSpec(memory_space=pltpu.SMEM)
ANY = pl.BlockSpec(memory_space=pl.ANY)


def params(limit=48 * 2**20):
    return pltpu.CompilerParams(vmem_limit_bytes=limit)


def gather_rows(points, atom, first, last, step, table, rows):
    base = atom * SPHERE

    def body(s, carry):
        i = pl.multiple_of(s * step, step)
        at = (i >> 7) * (ATOM_DEV * LANES) + atom * LANES + (i & (LANES - 1))
        for u in range(step):
            word = points[at + u]
            rows[pl.ds(base + i + u, 1), :] = table[pl.ds(word & (PLANE - 1), 1), :]
            rows[pl.ds(base + WORDS + i + u, 1), :] = table[pl.ds(word >> 12, 1), :]
        return carry

    lax.fori_loop(first, last, body, 0)


def counts(points, atom):
    at = WORDS * ATOM_DEV + atom * LANES
    return points[at], points[at + LANES - 1]


def one_hot(column, width):
    place = lax.broadcasted_iota(jnp.int32, (column.shape[0], width), 1).astype(F32)
    return jnp.where(column == place, 1.0, 0.0).astype(BF16)


def project(pay, rows, shift, planes, tiles, atoms=range(ATOM_DEV)):
    width = len(tiles) * LANES
    span = len(planes) * 16
    lane_plane = lax.broadcasted_iota(jnp.int32, (16, LANES), 1) % CZ
    sub = lax.broadcasted_iota(jnp.int32, (16, width), 0)
    parts = []
    for a in range(ATOM_DEV):
        if a not in atoms:
            parts.append(jnp.zeros((16, LANES), F32))
            continue
        block = jnp.concatenate(
            [pay[(a * TILES + t) * 16 : (a * TILES + t + 1) * 16, :] for t in tiles], axis=1
        )
        plane = jnp.broadcast_to(block[15:16, :] + float(shift), (16, width)).astype(BF16)
        proj = jnp.where(sub < NI, block, 0.0)
        high = proj.astype(BF16)
        low = (proj - high.astype(F32)).astype(BF16)
        pieces = []
        for piece in (high, low):
            for z in planes:
                pieces.append(jnp.where(plane == jnp.full_like(plane, z), piece, jnp.zeros_like(piece)))
        left = jnp.concatenate(pieces, axis=0)
        gathered = jnp.concatenate(
            [rows[a * SPHERE + t * LANES : a * SPHERE + (t + 1) * LANES, :] for t in tiles], axis=0
        )
        g_high = gathered.astype(BF16)
        g_low = (gathered - g_high.astype(F32)).astype(BF16)
        both = jnp.concatenate([g_high, g_low], axis=1)
        product = jnp.dot(left, both, preferred_element_type=F32)
        total = product[:span, :LANES] + product[span:, :LANES] + product[:span, LANES:]
        acc = jnp.zeros((16, LANES), F32)
        for k, z in enumerate(planes):
            acc = acc + jnp.where(lane_plane == z, total[k * 16 : (k + 1) * 16, :], 0.0)
        parts.append(acc)
    summed = jnp.concatenate(parts, axis=0)
    band = lax.broadcasted_iota(jnp.int32, (BANDS, LANES), 0)
    lane_band = lax.broadcasted_iota(jnp.int32, (BANDS, LANES), 1) // CZ
    pick = (band == lane_band).astype(F32)
    return lax.dot_general(
        pick, summed, (((1,), (1,)), ((), ())), precision=HIGHEST, preferred_element_type=F32
    )


def table_kernel(x, table):
    for c in range(PLANE // LANES):
        cols = slice(c * LANES, (c + 1) * LANES)
        table[cols, :] = x[:, cols].T


def sort_kernel(
    sizes_in, offsets_in, projectors_in, pay, lists, sizes, offsets, projectors, sems
):
    pairs = ((sizes_in, sizes), (offsets_in, offsets), (projectors_in, projectors))
    copies = [pltpu.make_async_copy(a, b, sems.at[k]) for k, (a, b) in enumerate(pairs)]
    for copy in copies:
        copy.start()
    before = lax.broadcasted_iota(jnp.int32, (SPHERE, SPHERE), 0)
    after = lax.broadcasted_iota(jnp.int32, (SPHERE, SPHERE), 1)
    until = jnp.where(before <= after, 1.0, 0.0).astype(BF16)
    sub = lax.broadcasted_iota(jnp.int32, (ATOM_DEV, SPHERE), 0)
    lane = lax.broadcasted_iota(jnp.int32, (ATOM_DEV, SPHERE), 1)
    copies[0].wait()
    copies[1].wait()
    size = jnp.zeros((ATOM_DEV, SPHERE), jnp.int32)
    for a in range(ATOM_DEV):
        size = jnp.where(sub == a, sizes[a], size)
    live = lane < size
    off = offsets[...]
    plane = off >> 12
    point = off & (PLANE - 1)
    below = live & (plane < HALO)
    above = live & (plane >= HALO + CZ)
    own = live & (plane >= HALO) & (plane < HALO + CZ)
    flags = jnp.concatenate(
        [jnp.where(m, 1.0, 0.0) for m in (below, own, above)] + [jnp.zeros((8, SPHERE), F32)],
        axis=0,
    ).astype(BF16)
    rank = jnp.dot(flags, until, preferred_element_type=F32).astype(jnp.int32)
    n_below = jnp.max(rank[0:8], axis=1, keepdims=True)
    n_own = jnp.max(rank[8:16], axis=1, keepdims=True)
    n_above = jnp.max(rank[16:24], axis=1, keepdims=True)
    place = jnp.where(
        below,
        rank[0:8] - 1,
        jnp.where(own, n_below + rank[8:16] - 1, SPHERE - rank[16:24]),
    )
    place = jnp.where(live, (place >> 1) + (place & 1) * WORDS, -1)
    place = jnp.transpose(place.astype(F32))
    copies[2].wait()
    table = jnp.concatenate(
        [
            projectors[...],
            (point >> 6).astype(F32)[None],
            (point & 63).astype(F32)[None],
            plane.astype(F32)[None],
        ],
        axis=0,
    )
    table = jnp.transpose(table, (1, 0, 2))
    points = []
    for a in range(ATOM_DEV):
        high = table[a].astype(BF16)
        low = (table[a] - high.astype(F32)).astype(BF16)
        move = one_hot(place[:, a : a + 1], SPHERE)
        moved = jnp.dot(
            jnp.concatenate([high, low], axis=0), move, preferred_element_type=F32
        )
        moved = moved[0:16] + moved[16:32]
        first = a * TILES * 16
        for t in range(TILES):
            pay[first + t * 16 : first + (t + 1) * 16, :] = moved[:, t * LANES : (t + 1) * LANES]
        points.append(moved[13:14] * 64.0 + moved[14:15])
    points = jnp.concatenate(points, axis=0)
    words = points[:, :WORDS] + points[:, WORDS:] * float(PLANE)
    for t in range(WORDS // LANES):
        at = t * ATOM_DEV
        lists[at : at + ATOM_DEV, :] = words[:, t * LANES : (t + 1) * LANES].astype(jnp.int32)
        for start, shift in ((SORTED, 0), (SORTED + LIST, WORDS)):
            part = points[:, shift + t * LANES : shift + (t + 1) * LANES]
            pay[start + at : start + at + ATOM_DEV, :] = part
    at = LIST - ATOM_DEV
    lead = lane[:, :LANES] < LANES // 2
    pay[SORTED + at : SORTED + LIST, :] = jnp.where(lead, n_below, n_above).astype(F32)
    pay[SORTED + LIST + at : SORTED + 2 * LIST, :] = jnp.zeros((ATOM_DEV, LANES), F32)
    lists[at:LIST, :] = jnp.where(lead, n_below, n_below + n_own)


def words_of(pay):
    words = pay[SORTED : SORTED + LIST] + pay[SORTED + LIST :] * float(PLANE)
    return words.astype(jnp.int32).reshape(-1)


def own_points(atoms, lists, table, pay, rows):
    rows[...] = jnp.zeros_like(rows)
    step = 16
    for a in atoms:
        begin, end = counts(lists, a)
        first = begin // (2 * step)
        last = (end + (2 * step - 1)) // (2 * step)
        gather_rows(lists, a, first, last, step, table, rows)
    return project(pay, rows, -HALO, range(CZ), range(TILES), atoms)


def early_kernel(lists, table, pay, q, rows):
    q[...] = own_points(range(EARLY), lists, table, pay, rows)


def late_kernel(lists, occ, x, table, pay, after, packed, q, rows):
    del after
    for c in range(PLANE // LANES):
        cols = slice(c * LANES, (c + 1) * LANES)
        acc = jnp.zeros((CZ, LANES), F32)
        for n in range(BANDS):
            v = x[n * CZ : (n + 1) * CZ, cols]
            acc = acc + occ[n] * (v * v)
        packed[c // 2, (c % 2) * CZ : (c % 2 + 1) * CZ, :] = acc
    q[...] = own_points(range(EARLY, ATOM_DEV), lists, table, pay, rows)


def side_kernel(prev, points, table, pay, after, q, rows):
    del after
    rows[...] = jnp.zeros_like(rows)
    step = 8
    most = jnp.int32(0)
    for a in range(ATOM_DEV):
        most = jnp.maximum(most, counts(points, a)[1 if prev else 0])

    for a in range(ATOM_DEV):
        first, last = 0, WORDS // step
        if prev:
            first = (SPHERE - counts(points, a)[1]) // (2 * step)
        else:
            last = (counts(points, a)[0] + (2 * step - 1)) // (2 * step)
        gather_rows(points, a, first, last, step, table, rows)

    shift = -HALO - CZ if prev else CZ - HALO
    planes = range(HALO) if prev else range(CZ - HALO, CZ)

    @pl.when(most <= WORDS)
    def _():
        q[...] = project(pay, rows, shift, planes, (1, 3) if prev else (0, 2))

    @pl.when(most > WORDS)
    def _():
        q[...] = project(pay, rows, shift, planes, range(TILES))


def matrix_kernel(q0, q1, q2, q3, occ, packed, out, block, sem):
    del packed
    proj = q0[...] + q1[...] + q2[...] + q3[...]
    weighted = proj * occ[...]
    full = lax.dot_general(
        weighted, proj, (((0,), (0,)), ((), ())), precision=HIGHEST, preferred_element_type=F32
    )
    lane_atom = lax.broadcasted_iota(jnp.int32, (16, LANES), 1) // 16
    acc = jnp.zeros((16, LANES), F32)
    for a in range(ATOM_DEV):
        acc = acc + jnp.where(lane_atom == a, full[a * 16 : (a + 1) * 16, :], 0.0)
    i = lax.broadcasted_iota(jnp.int32, (8, LANES), 0)
    j = lax.broadcasted_iota(jnp.int32, (8, LANES), 1) % 16
    corner = pltpu.roll(pltpu.roll(acc[8:16], 1, 0), LANES - 8, 1)
    half = jnp.where(j < i, corner, acc[0:8])
    for b in range(16):
        block[b] = half
    copy = pltpu.make_async_copy(block, out.at[:, pl.ds(16, 8), :], sem)
    copy.start()
    copy.wait()


def charge_kernel(start, recv, coupling, shapes, offsets, core, down, up, matrices):
    total = recv[0]
    for b in range(1, 16):
        total = total + recv[b]
    matrix = total[16:24]
    matrices[...] = matrix
    per_lane = jnp.concatenate(
        [jnp.sum(coupling[l] * matrix, axis=0, keepdims=True) for l in range(NL)], axis=0
    )
    atom = lax.broadcasted_iota(jnp.int32, (ATOM_DEV, LANES), 0)
    lane_atom = lax.broadcasted_iota(jnp.int32, (ATOM_DEV, LANES), 1) // 16
    pick = (atom == lane_atom).astype(F32)
    charges = lax.dot_general(
        pick, per_lane, (((1,), (1,)), ((), ())), precision=HIGHEST, preferred_element_type=F32
    )
    comp = jnp.zeros((ATOM_DEV, SPHERE), F32)
    for l in range(NL):
        comp = comp + charges[:, l : l + 1] * shapes[l]
    c1 = comp.astype(BF16).astype(F32)
    c2 = (comp - c1).astype(BF16).astype(F32)
    c3 = comp - c1 - c2
    plane = offsets[...] >> 12
    column = (offsets[...] & (PLANE - 1)) - start[0]
    column = jnp.transpose(column.astype(F32))
    row = lax.broadcasted_iota(jnp.int32, (24, SPHERE), 0)
    target = jnp.where(row < 8, row + HALO, jnp.where(row < 16, row - 11, row - 3))
    acc = jnp.zeros((80, 256), F32)
    for a in range(ATOM_DEV):
        here = target == plane[a : a + 1, :]
        left = jnp.concatenate(
            [jnp.where(here, c[a : a + 1, :], 0.0) for c in (c1, c2, c3)]
            + [jnp.zeros((8, SPHERE), F32)],
            axis=0,
        ).astype(BF16)
        right = one_hot(column[:, a : a + 1], 256)
        acc = acc + jnp.dot(left, right, preferred_element_type=F32)
    placed = acc[0:24] + acc[24:48] + acc[48:72]
    core[...] = placed[0:8] + jnp.concatenate([total[0:8], total[8:16]], axis=1)
    down[...] = placed[8:16]
    up[...] = placed[16:24]


def shape(*dims):
    return jax.ShapeDtypeStruct(dims, F32)


def local(orbitals, occupations, projectors, shapes, coupling, sphere_offsets, sphere_sizes):
    slabs = lax.axis_size("slab")
    to_next = [(i, (i + 1) % slabs) for i in range(slabs)]
    to_prev = [((i + 1) % slabs, i) for i in range(slabs)]
    grid_values = orbitals.reshape(BANDS * CZ, PLANE)
    table = pl.pallas_call(
        table_kernel,
        out_shape=shape(PLANE, LANES),
        in_specs=[VM],
        out_specs=VM,
        compiler_params=params(),
        cost_estimate=pl.CostEstimate(flops=0, bytes_accessed=8 * 2**20, transcendentals=0),
        name="grid_table",
    )(grid_values)
    pay, lists = pl.pallas_call(
        sort_kernel,
        out_shape=(
            shape(SORTED + 2 * LIST, LANES),
            jax.ShapeDtypeStruct((LIST, LANES), jnp.int32),
        ),
        in_specs=[ANY] * 3,
        out_specs=(VM, VM),
        scratch_shapes=[
            pltpu.SMEM((ATOM_DEV,), jnp.int32),
            pltpu.VMEM((ATOM_DEV, SPHERE), jnp.int32),
            pltpu.VMEM((NI, ATOM_DEV, SPHERE), F32),
            pltpu.SemaphoreType.DMA((3,)),
        ],
        compiler_params=params(58 * 2**20),
        cost_estimate=pl.CostEstimate(flops=10**9, bytes_accessed=8 * 2**20, transcendentals=0),
        name="sort_points",
    )(sphere_sizes, sphere_offsets, projectors.transpose(1, 0, 2))
    pay_lo = lax.ppermute(pay, "slab", to_next)
    pay_hi = lax.ppermute(pay, "slab", to_prev)

    own_list = lists.reshape(-1)
    scratch = [pltpu.VMEM((ATOM_DEV * SPHERE, LANES), F32)]
    q_early = pl.pallas_call(
        early_kernel,
        out_shape=shape(BANDS, LANES),
        in_specs=[SM, VM, VM],
        out_specs=VM,
        scratch_shapes=scratch,
        compiler_params=params(),
        cost_estimate=pl.CostEstimate(flops=10**9, bytes_accessed=8 * 2**20, transcendentals=0),
        name="own_points_early",
    )(own_list, table, pay)

    def side(prev, block, after):
        return pl.pallas_call(
            functools.partial(side_kernel, prev),
            out_shape=shape(BANDS, LANES),
            in_specs=[SM, VM, VM, ANY],
            out_specs=VM,
            scratch_shapes=scratch,
            compiler_params=params(),
            cost_estimate=pl.CostEstimate(
                flops=10**9, bytes_accessed=6 * 2**20, transcendentals=0
            ),
            name="previous_points" if prev else "next_points",
        )(words_of(block), table, block, after)

    q_hi = side(False, pay_hi, q_early)
    q_lo = side(True, pay_lo, q_hi)
    back_hi = lax.ppermute(q_lo, "slab", to_prev)
    back_lo = lax.ppermute(q_hi, "slab", to_next)

    packed, q_late = pl.pallas_call(
        late_kernel,
        out_shape=(shape(16, 24, LANES), shape(BANDS, LANES)),
        in_specs=[SM, SM, VM, VM, VM, ANY],
        out_specs=(VM, VM),
        scratch_shapes=scratch,
        compiler_params=params(),
        cost_estimate=pl.CostEstimate(flops=10**9, bytes_accessed=8 * 2**20, transcendentals=0),
        name="own_points_late",
    )(own_list, occupations, grid_values, table, pay, q_lo)

    packed = pl.pallas_call(
        matrix_kernel,
        out_shape=shape(16, 24, LANES),
        in_specs=[VM] * 5 + [ANY],
        out_specs=ANY,
        scratch_shapes=[pltpu.VMEM((16, 8, LANES), F32), pltpu.SemaphoreType.DMA],
        input_output_aliases={5: 0},
        compiler_params=params(),
        name="partial_matrices",
    )(
        q_early,
        q_late,
        back_hi,
        back_lo,
        jnp.broadcast_to(occupations[:, None], (BANDS, LANES)),
        packed,
    )
    recv = lax.all_to_all(packed, "band", 0, 0)

    unpack = np.zeros((8, 16, NI, NI), np.float32)
    for i in range(NI):
        for j in range(NI):
            r, c = min(i, j), max(i, j)
            p, q = (r, c) if r < 8 else (c - 7, r - 8)
            unpack[p, q, i, j] = 1.0
    both_ways = jnp.where(np.eye(NI, dtype=bool), coupling, coupling + coupling.transpose(0, 2, 1))
    top = jnp.pad(both_ways[:, :8], ((0, 0), (0, 0), (0, 3)))
    low = jnp.pad(both_ways[:, 8:, 8:], ((0, 0), (1, 2), (0, 11)))
    coupling_packed = jnp.where(np.tri(8, 16, -1, dtype=bool), low, top)
    coupling_lanes = jnp.tile(coupling_packed, (1, 1, ATOM_DEV))
    live = jnp.arange(SPHERE, dtype=jnp.int32)[None, :] < sphere_sizes[:, None]
    shapes_live = jnp.where(live[:, None, :], shapes, 0.0).transpose(1, 0, 2)
    width = PLANE // lax.axis_size("band")
    start = (lax.axis_index("band") * width).astype(jnp.int32).reshape(1)
    core, down, up, matrices = pl.pallas_call(
        charge_kernel,
        out_shape=(shape(CZ, 256), shape(CZ, 256), shape(CZ, 256), shape(8, LANES)),
        in_specs=[SM, VM, VM, VM, VM],
        out_specs=(VM, VM, VM, VM),
        compiler_params=params(),
        name="charges",
    )(start, recv, coupling_lanes, shapes_live, sphere_offsets)
    from_above = lax.ppermute(down, "slab", to_prev)
    from_below = lax.ppermute(up, "slab", to_next)
    density = core + from_above + from_below
    density_matrices = jnp.einsum(
        "paq,pqij->aij", matrices.reshape(8, ATOM_DEV, 16), unpack, precision=HIGHEST
    )
    return (density, density_matrices)


def solution(mesh):
    placed = (
        P("band", "slab", None),
        P("band"),
        P("slab", None, None),
        P("slab", None, None),
        P(),
        P("slab", None),
        P("slab"),
    )
    return jax.shard_map(
        local,
        mesh=mesh,
        in_specs=placed,
        out_specs=(P("slab", "band"), P("slab", None, None)),
        check_vma=False,
    )
```

```python
import functools

import jax
import jax.numpy as jnp
import numpy as np
from jax import lax
from jax.experimental import pallas as pl
from jax.experimental.pallas import tpu as pltpu
from jax.sharding import PartitionSpec as P

HALO = 5
PLANE = 4096
CZ = 8
ATOM_DEV = 8
SPHERE = 512
NI = 13
NL = 9
BANDS = 16
LANES = 128
EARLY = 5
TILES = SPHERE // LANES
WORDS = SPHERE // 2
SORTED = TILES * ATOM_DEV * 16
LIST = WORDS // LANES * ATOM_DEV + ATOM_DEV
HIGHEST = lax.Precision.HIGHEST
F32 = jnp.float32
BF16 = jnp.bfloat16

VM = pl.BlockSpec(memory_space=pltpu.VMEM)
SM = pl.BlockSpec(memory_space=pltpu.SMEM)
ANY = pl.BlockSpec(memory_space=pl.ANY)


def params(limit=50 * 2**20):
    return pltpu.CompilerParams(vmem_limit_bytes=limit)


def gather_rows(points, atom, first, last, step, table, rows):
    base = atom * SPHERE

    def body(s, carry):
        i = pl.multiple_of(s * step, step)
        at = (i >> 7) * (ATOM_DEV * LANES) + atom * LANES + (i & (LANES - 1))
        for u in range(step):
            word = points[at + u]
            rows[pl.ds(base + i + u, 1), :] = table[pl.ds(word & (PLANE - 1), 1), :]
            rows[pl.ds(base + WORDS + i + u, 1), :] = table[pl.ds(word >> 12, 1), :]
        return carry

    lax.fori_loop(first, last, body, 0)


def counts(points, atom):
    at = WORDS * ATOM_DEV + atom * LANES
    return points[at], points[at + LANES - 1]


def one_hot(column, width):
    place = lax.broadcasted_iota(jnp.int32, (column.shape[0], width), 1).astype(F32)
    return jnp.where(column == place, 1.0, 0.0).astype(BF16)


def project(pay, rows, shift, planes, tiles, atoms=range(ATOM_DEV)):
    width = len(tiles) * LANES
    span = len(planes) * 16
    lane_plane = lax.broadcasted_iota(jnp.int32, (16, LANES), 1) % CZ
    sub = lax.broadcasted_iota(jnp.int32, (16, width), 0)
    parts = []
    for a in range(ATOM_DEV):
        if a not in atoms:
            parts.append(jnp.zeros((16, LANES), F32))
            continue
        block = jnp.concatenate(
            [pay[(a * TILES + t) * 16 : (a * TILES + t + 1) * 16, :] for t in tiles], axis=1
        )
        plane = jnp.broadcast_to(block[15:16, :] + float(shift), (16, width)).astype(BF16)
        proj = jnp.where(sub < NI, block, 0.0)
        high = proj.astype(BF16)
        low = (proj - high.astype(F32)).astype(BF16)
        pieces = []
        for piece in (high, low):
            for z in planes:
                pieces.append(jnp.where(plane == jnp.full_like(plane, z), piece, jnp.zeros_like(piece)))
        left = jnp.concatenate(pieces, axis=0)
        gathered = jnp.concatenate(
            [rows[a * SPHERE + t * LANES : a * SPHERE + (t + 1) * LANES, :] for t in tiles], axis=0
        )
        g_high = gathered.astype(BF16)
        g_low = (gathered - g_high.astype(F32)).astype(BF16)
        both = jnp.concatenate([g_high, g_low], axis=1)
        product = jnp.dot(left, both, preferred_element_type=F32)
        total = product[:span, :LANES] + product[span:, :LANES] + product[:span, LANES:]
        acc = jnp.zeros((16, LANES), F32)
        for k, z in enumerate(planes):
            acc = acc + jnp.where(lane_plane == z, total[k * 16 : (k + 1) * 16, :], 0.0)
        parts.append(acc)
    summed = jnp.concatenate(parts, axis=0)
    band = lax.broadcasted_iota(jnp.int32, (BANDS, LANES), 0)
    lane_band = lax.broadcasted_iota(jnp.int32, (BANDS, LANES), 1) // CZ
    pick = (band == lane_band).astype(F32)
    return lax.dot_general(
        pick, summed, (((1,), (1,)), ((), ())), precision=HIGHEST, preferred_element_type=F32
    )


def table_kernel(x, table):
    for c in range(PLANE // LANES):
        cols = slice(c * LANES, (c + 1) * LANES)
        table[cols, :] = x[:, cols].T


def sort_kernel(
    sizes_in, offsets_in, projectors_in, pay, lists, sizes, offsets, projectors, sems
):
    pairs = ((sizes_in, sizes), (offsets_in, offsets), (projectors_in, projectors))
    copies = [pltpu.make_async_copy(a, b, sems.at[k]) for k, (a, b) in enumerate(pairs)]
    for copy in copies:
        copy.start()
    before = lax.broadcasted_iota(jnp.int32, (SPHERE, SPHERE), 0)
    after = lax.broadcasted_iota(jnp.int32, (SPHERE, SPHERE), 1)
    until = jnp.where(before <= after, 1.0, 0.0).astype(BF16)
    sub = lax.broadcasted_iota(jnp.int32, (ATOM_DEV, SPHERE), 0)
    lane = lax.broadcasted_iota(jnp.int32, (ATOM_DEV, SPHERE), 1)
    copies[0].wait()
    copies[1].wait()
    size = jnp.zeros((ATOM_DEV, SPHERE), jnp.int32)
    for a in range(ATOM_DEV):
        size = jnp.where(sub == a, sizes[a], size)
    live = lane < size
    off = offsets[...]
    plane = off >> 12
    point = off & (PLANE - 1)
    below = live & (plane < HALO)
    above = live & (plane >= HALO + CZ)
    own = live & (plane >= HALO) & (plane < HALO + CZ)
    flags = jnp.concatenate(
        [jnp.where(m, 1.0, 0.0) for m in (below, own, above)] + [jnp.zeros((8, SPHERE), F32)],
        axis=0,
    ).astype(BF16)
    rank = jnp.dot(flags, until, preferred_element_type=F32).astype(jnp.int32)
    n_below = jnp.max(rank[0:8], axis=1, keepdims=True)
    n_own = jnp.max(rank[8:16], axis=1, keepdims=True)
    n_above = jnp.max(rank[16:24], axis=1, keepdims=True)
    place = jnp.where(
        below,
        rank[0:8] - 1,
        jnp.where(own, n_below + rank[8:16] - 1, SPHERE - rank[16:24]),
    )
    place = jnp.where(live, (place >> 1) + (place & 1) * WORDS, -1)
    place = jnp.transpose(place.astype(F32))
    copies[2].wait()
    table = jnp.concatenate(
        [
            projectors[...],
            (point >> 6).astype(F32)[None],
            (point & 63).astype(F32)[None],
            plane.astype(F32)[None],
        ],
        axis=0,
    )
    table = jnp.transpose(table, (1, 0, 2))
    points = []
    for a in range(ATOM_DEV):
        high = table[a].astype(BF16)
        low = (table[a] - high.astype(F32)).astype(BF16)
        move = one_hot(place[:, a : a + 1], SPHERE)
        moved = jnp.dot(
            jnp.concatenate([high, low], axis=0), move, preferred_element_type=F32
        )
        moved = moved[0:16] + moved[16:32]
        first = a * TILES * 16
        for t in range(TILES):
            pay[first + t * 16 : first + (t + 1) * 16, :] = moved[:, t * LANES : (t + 1) * LANES]
        points.append(moved[13:14] * 64.0 + moved[14:15])
    points = jnp.concatenate(points, axis=0)
    words = points[:, :WORDS] + points[:, WORDS:] * float(PLANE)
    for t in range(WORDS // LANES):
        at = t * ATOM_DEV
        lists[at : at + ATOM_DEV, :] = words[:, t * LANES : (t + 1) * LANES].astype(jnp.int32)
        for start, shift in ((SORTED, 0), (SORTED + LIST, WORDS)):
            part = points[:, shift + t * LANES : shift + (t + 1) * LANES]
            pay[start + at : start + at + ATOM_DEV, :] = part
    at = LIST - ATOM_DEV
    lead = lane[:, :LANES] < LANES // 2
    pay[SORTED + at : SORTED + LIST, :] = jnp.where(lead, n_below, n_above).astype(F32)
    pay[SORTED + LIST + at : SORTED + 2 * LIST, :] = jnp.zeros((ATOM_DEV, LANES), F32)
    lists[at:LIST, :] = jnp.where(lead, n_below, n_below + n_own)


def words_of(pay):
    words = pay[SORTED : SORTED + LIST] + pay[SORTED + LIST :] * float(PLANE)
    return words.astype(jnp.int32).reshape(-1)


def own_points(atoms, lists, table, pay, rows):
    rows[...] = jnp.zeros_like(rows)
    step = 16
    for a in atoms:
        begin, end = counts(lists, a)
        first = begin // (2 * step)
        last = (end + (2 * step - 1)) // (2 * step)
        gather_rows(lists, a, first, last, step, table, rows)
    return project(pay, rows, -HALO, range(CZ), range(TILES), atoms)


def early_kernel(lists, table, pay, q, rows):
    q[...] = own_points(range(EARLY), lists, table, pay, rows)


def late_kernel(lists, occ, x, table, pay, after, packed, q, rows):
    del after
    for c in range(PLANE // LANES):
        cols = slice(c * LANES, (c + 1) * LANES)
        acc = jnp.zeros((CZ, LANES), F32)
        for n in range(BANDS):
            v = x[n * CZ : (n + 1) * CZ, cols]
            acc = acc + occ[n] * (v * v)
        packed[c // 2, (c % 2) * CZ : (c % 2 + 1) * CZ, :] = acc
    q[...] = own_points(range(EARLY, ATOM_DEV), lists, table, pay, rows)


def side_kernel(prev, points, table, pay, after, q, rows):
    del after
    rows[...] = jnp.zeros_like(rows)
    step = 8
    most = jnp.int32(0)
    for a in range(ATOM_DEV):
        most = jnp.maximum(most, counts(points, a)[1 if prev else 0])

    for a in range(ATOM_DEV):
        first, last = 0, WORDS // step
        if prev:
            first = (SPHERE - counts(points, a)[1]) // (2 * step)
        else:
            last = (counts(points, a)[0] + (2 * step - 1)) // (2 * step)
        gather_rows(points, a, first, last, step, table, rows)

    shift = -HALO - CZ if prev else CZ - HALO
    planes = range(HALO) if prev else range(CZ - HALO, CZ)

    @pl.when(most <= WORDS)
    def _():
        q[...] = project(pay, rows, shift, planes, (1, 3) if prev else (0, 2))

    @pl.when(most > WORDS)
    def _():
        q[...] = project(pay, rows, shift, planes, range(TILES))


def matrix_kernel(q0, q1, q2, q3, occ, packed, out, block, sem):
    del packed
    proj = q0[...] + q1[...] + q2[...] + q3[...]
    weighted = proj * occ[...]
    full = lax.dot_general(
        weighted, proj, (((0,), (0,)), ((), ())), precision=HIGHEST, preferred_element_type=F32
    )
    lane_atom = lax.broadcasted_iota(jnp.int32, (16, LANES), 1) // 16
    acc = jnp.zeros((16, LANES), F32)
    for a in range(ATOM_DEV):
        acc = acc + jnp.where(lane_atom == a, full[a * 16 : (a + 1) * 16, :], 0.0)
    i = lax.broadcasted_iota(jnp.int32, (8, LANES), 0)
    j = lax.broadcasted_iota(jnp.int32, (8, LANES), 1) % 16
    corner = pltpu.roll(pltpu.roll(acc[8:16], 1, 0), LANES - 8, 1)
    half = jnp.where(j < i, corner, acc[0:8])
    for b in range(16):
        block[b] = half
    copy = pltpu.make_async_copy(block, out.at[:, pl.ds(16, 8), :], sem)
    copy.start()
    copy.wait()


def charge_kernel(start, recv, coupling, shapes, offsets, core, down, up, matrices):
    total = recv[0]
    for b in range(1, 16):
        total = total + recv[b]
    matrix = total[16:24]
    matrices[...] = matrix
    per_lane = jnp.concatenate(
        [jnp.sum(coupling[l] * matrix, axis=0, keepdims=True) for l in range(NL)], axis=0
    )
    atom = lax.broadcasted_iota(jnp.int32, (ATOM_DEV, LANES), 0)
    lane_atom = lax.broadcasted_iota(jnp.int32, (ATOM_DEV, LANES), 1) // 16
    pick = (atom == lane_atom).astype(F32)
    charges = lax.dot_general(
        pick, per_lane, (((1,), (1,)), ((), ())), precision=HIGHEST, preferred_element_type=F32
    )
    comp = jnp.zeros((ATOM_DEV, SPHERE), F32)
    for l in range(NL):
        comp = comp + charges[:, l : l + 1] * shapes[l]
    c1 = comp.astype(BF16).astype(F32)
    c2 = (comp - c1).astype(BF16).astype(F32)
    c3 = comp - c1 - c2
    plane = offsets[...] >> 12
    column = (offsets[...] & (PLANE - 1)) - start[0]
    column = jnp.transpose(column.astype(F32))
    row = lax.broadcasted_iota(jnp.int32, (24, SPHERE), 0)
    target = jnp.where(row < 8, row + HALO, jnp.where(row < 16, row - 11, row - 3))
    acc = jnp.zeros((80, 256), F32)
    for a in range(ATOM_DEV):
        here = target == plane[a : a + 1, :]
        left = jnp.concatenate(
            [jnp.where(here, c[a : a + 1, :], 0.0) for c in (c1, c2, c3)]
            + [jnp.zeros((8, SPHERE), F32)],
            axis=0,
        ).astype(BF16)
        right = one_hot(column[:, a : a + 1], 256)
        acc = acc + jnp.dot(left, right, preferred_element_type=F32)
    placed = acc[0:24] + acc[24:48] + acc[48:72]
    core[...] = placed[0:8] + jnp.concatenate([total[0:8], total[8:16]], axis=1)
    down[...] = placed[8:16]
    up[...] = placed[16:24]


def shape(*dims):
    return jax.ShapeDtypeStruct(dims, F32)


def local(orbitals, occupations, projectors, shapes, coupling, sphere_offsets, sphere_sizes):
    slabs = lax.axis_size("slab")
    to_next = [(i, (i + 1) % slabs) for i in range(slabs)]
    to_prev = [((i + 1) % slabs, i) for i in range(slabs)]
    grid_values = orbitals.reshape(BANDS * CZ, PLANE)
    table = pl.pallas_call(
        table_kernel,
        out_shape=shape(PLANE, LANES),
        in_specs=[VM],
        out_specs=VM,
        compiler_params=params(),
        cost_estimate=pl.CostEstimate(flops=0, bytes_accessed=8 * 2**20, transcendentals=0),
        name="grid_table",
    )(grid_values)
    pay, lists = pl.pallas_call(
        sort_kernel,
        out_shape=(
            shape(SORTED + 2 * LIST, LANES),
            jax.ShapeDtypeStruct((LIST, LANES), jnp.int32),
        ),
        in_specs=[ANY] * 3,
        out_specs=(VM, VM),
        scratch_shapes=[
            pltpu.SMEM((ATOM_DEV,), jnp.int32),
            pltpu.VMEM((ATOM_DEV, SPHERE), jnp.int32),
            pltpu.VMEM((NI, ATOM_DEV, SPHERE), F32),
            pltpu.SemaphoreType.DMA((3,)),
        ],
        compiler_params=params(58 * 2**20),
        cost_estimate=pl.CostEstimate(flops=10**9, bytes_accessed=8 * 2**20, transcendentals=0),
        name="sort_points",
    )(sphere_sizes, sphere_offsets, projectors.transpose(1, 0, 2))
    pay_lo = lax.ppermute(pay, "slab", to_next)
    pay_hi = lax.ppermute(pay, "slab", to_prev)

    own_list = lists.reshape(-1)
    scratch = [pltpu.VMEM((ATOM_DEV * SPHERE, LANES), F32)]
    q_early = pl.pallas_call(
        early_kernel,
        out_shape=shape(BANDS, LANES),
        in_specs=[SM, VM, VM],
        out_specs=VM,
        scratch_shapes=scratch,
        compiler_params=params(),
        cost_estimate=pl.CostEstimate(flops=10**9, bytes_accessed=8 * 2**20, transcendentals=0),
        name="own_points_early",
    )(own_list, table, pay)

    def side(prev, block, after):
        return pl.pallas_call(
            functools.partial(side_kernel, prev),
            out_shape=shape(BANDS, LANES),
            in_specs=[SM, VM, VM, ANY],
            out_specs=VM,
            scratch_shapes=scratch,
            compiler_params=params(),
            cost_estimate=pl.CostEstimate(
                flops=10**9, bytes_accessed=6 * 2**20, transcendentals=0
            ),
            name="previous_points" if prev else "next_points",
        )(words_of(block), table, block, after)

    q_hi = side(False, pay_hi, q_early)
    q_lo = side(True, pay_lo, q_hi)
    back_hi = lax.ppermute(q_lo, "slab", to_prev)
    back_lo = lax.ppermute(q_hi, "slab", to_next)

    packed, q_late = pl.pallas_call(
        late_kernel,
        out_shape=(shape(16, 24, LANES), shape(BANDS, LANES)),
        in_specs=[SM, SM, VM, VM, VM, ANY],
        out_specs=(VM, VM),
        scratch_shapes=scratch,
        compiler_params=params(),
        cost_estimate=pl.CostEstimate(flops=10**9, bytes_accessed=8 * 2**20, transcendentals=0),
        name="own_points_late",
    )(own_list, occupations, grid_values, table, pay, q_lo)

    packed = pl.pallas_call(
        matrix_kernel,
        out_shape=shape(16, 24, LANES),
        in_specs=[VM] * 5 + [ANY],
        out_specs=ANY,
        scratch_shapes=[pltpu.VMEM((16, 8, LANES), F32), pltpu.SemaphoreType.DMA],
        input_output_aliases={5: 0},
        compiler_params=params(),
        name="partial_matrices",
    )(
        q_early,
        q_late,
        back_hi,
        back_lo,
        jnp.broadcast_to(occupations[:, None], (BANDS, LANES)),
        packed,
    )
    recv = lax.all_to_all(packed, "band", 0, 0)

    unpack = np.zeros((8, 16, NI, NI), np.float32)
    for i in range(NI):
        for j in range(NI):
            r, c = min(i, j), max(i, j)
            p, q = (r, c) if r < 8 else (c - 7, r - 8)
            unpack[p, q, i, j] = 1.0
    both_ways = jnp.where(np.eye(NI, dtype=bool), coupling, coupling + coupling.transpose(0, 2, 1))
    top = jnp.pad(both_ways[:, :8], ((0, 0), (0, 0), (0, 3)))
    low = jnp.pad(both_ways[:, 8:, 8:], ((0, 0), (1, 2), (0, 11)))
    coupling_packed = jnp.where(np.tri(8, 16, -1, dtype=bool), low, top)
    coupling_lanes = jnp.tile(coupling_packed, (1, 1, ATOM_DEV))
    live = jnp.arange(SPHERE, dtype=jnp.int32)[None, :] < sphere_sizes[:, None]
    shapes_live = jnp.where(live[:, None, :], shapes, 0.0).transpose(1, 0, 2)
    width = PLANE // lax.axis_size("band")
    start = (lax.axis_index("band") * width).astype(jnp.int32).reshape(1)
    core, down, up, matrices = pl.pallas_call(
        charge_kernel,
        out_shape=(shape(CZ, 256), shape(CZ, 256), shape(CZ, 256), shape(8, LANES)),
        in_specs=[SM, VM, VM, VM, VM],
        out_specs=(VM, VM, VM, VM),
        compiler_params=params(),
        name="charges",
    )(start, recv, coupling_lanes, shapes_live, sphere_offsets)
    from_above = lax.ppermute(down, "slab", to_prev)
    from_below = lax.ppermute(up, "slab", to_next)
    density = core + from_above + from_below
    density_matrices = jnp.einsum(
        "paq,pqij->aij", matrices.reshape(8, ATOM_DEV, 16), unpack, precision=HIGHEST
    )
    return (density, density_matrices)


def solution(mesh):
    placed = (
        P("band", "slab", None),
        P("band"),
        P("slab", None, None),
        P("slab", None, None),
        P(),
        P("slab", None),
        P("slab"),
    )
    return jax.shard_map(
        local,
        mesh=mesh,
        in_specs=placed,
        out_specs=(P("slab", "band"), P("slab", None, None)),
        check_vma=False,
    )
```
